128 devices in a mesh: section: 4 (over x), ctx: 16 (over y, z), tp: 2 (over core).
Axes of the slice: x: 4, y: 4, z: 4, core: 2. Of those that a mesh axis runs over, the one named last changes fastest.
Arguments:
- prefill_hidden_states: bfloat16 [32768, 8192], P(('section', 'ctx')), may hold values from -6 to 6
- decode_hidden_states: bfloat16 [2, 16, 8192], P(None, 'section', 'ctx'), may hold values from -6 to 6
- query_matrix: bfloat16 [8192, 8192], P('ctx', 'tp'), may hold values from -0.0625 to 0.0625
- key_matrix: bfloat16 [8192, 1024], P('ctx', 'tp'), may hold values from -0.0625 to 0.0625
- value_matrix: bfloat16 [8192, 1024], P('ctx', 'tp'), may hold values from -0.0625 to 0.0625
- adapter_down_maps: bfloat16 [8192, 256], P('ctx', 'tp'), may hold values from -0.0625 to 0.0625
- key_adapter_up_maps: bfloat16 [128, 1024], P(None, 'tp'), may hold values from -1.5 to 1.5
- value_adapter_up_maps: bfloat16 [128, 1024], P(None, 'tp'), may hold values from -1.5 to 1.5
- request_key_cache: bfloat16 [16, 16384, 1024], P('section', 'ctx', 'tp'), may hold values from -1000 to 1000
- request_value_cache: bfloat16 [16, 16384, 1024], P('section', 'ctx', 'tp'), may hold values from -6 to 6
- request_adapter_index: int32 [16], replicated, may hold values from 0 to 7
- prefill_request_target: int32 [4], replicated, may hold values from 0 to 15, as said below
- request_context_length: int32 [16], P('section'), may hold values from 1024 to 16384, as said below
- page_owner_index: int32 [1024, 1], P(('section', 'ctx')), may hold values from 0 to 15; in each aligned block of 16 rows (0 to 15, 16 to 31, ...) at most 2 rows name the same one
Outputs:
- page_keys: bfloat16 [2048, 32, 1024], P(('section', 'ctx'), None, 'tp')
- page_values: bfloat16 [2048, 32, 1024], P(('section', 'ctx'), None, 'tp')
- attended: bfloat16 [2, 16, 8192], P(None, 'section', 'tp')
The draws below stay inside these ranges and needn't reach their ends.
Inputs may be any that keep to these rules, and one draw needn't show every extreme that they name: `prefill_request_target`: entry j names one of the 4 requests of decode group (j + 1) mod 4, i.e. a value of ((j + 1) mod 4) * 4 to that plus 4 - 1; one entry names request 0, another the last request. `request_context_length`: one request of every draw has all 16384 positions live, another exactly 1024. `page_owner_index`: among the 16 pages of one device, no owner is named more than 2 times.
All inputs are finite; a program needn't handle non-finite values.
Results may differ from the reference program's by a relative error of at most 0.0095.
Values may be sent and summed in bfloat16 or wider, within the bound.
A program may use at most 192 MiB of HBM per device.

```python
import math
import jax
import jax.numpy as jnp
import numpy as np
from jax import lax

MODEL_WIDTH = 8192
H = 64
KVH = 8
HD = 128
ADAPTER_RANK = 16
ADAPTER_COUNT = 8
BLK = 32
STEPS = 2
RPG = 4
CTX_DEV = 1024
B = 16
L = 16384
SPAN = 8192
CROWS = 32768
BPD = 16
NBLK = 1024
SEND_MOST = 2
SLOTS = 32
KEY_VALUE_WIDTH = 1024
N_SECTION = 4
N_CTX = 16


def context_lengths(key):
    key = jax.random.fold_in(key, 12)
    length_key, chosen_key = jax.random.split(key, 2)
    lengths = jax.random.randint(length_key, (B,), CTX_DEV, L + 1, dtype=jnp.int32)
    chosen = jax.random.randint(chosen_key, (), 0, B, dtype=jnp.int32)
    places = jnp.arange(B, dtype=jnp.int32)
    lengths = jnp.where(places == (chosen + 1) % B, CTX_DEV, lengths)
    return jnp.where(places == chosen, L, lengths).astype(jnp.int32)


def draw_request_key_cache(key, part):
    cache_key = jax.random.fold_in(key, 11)
    drawn_key = jax.random.fold_in(cache_key, 0)
    drawn_keys = jnp.clip(jax.random.normal(drawn_key, (B, L, KVH * HD), jnp.float32), -6.0, 6.0)
    return drawn_keys.astype(jnp.bfloat16)


def draw_request_context_length(key, part):
    return context_lengths(key)


def draw_prefill_request_target(key, part):
    key = jax.random.fold_in(key, 13)
    offsets = jax.random.randint(key, (N_SECTION,), 0, RPG, dtype=jnp.int32)
    sections = jnp.arange(N_SECTION, dtype=jnp.int32)
    offsets = jnp.where(sections == N_SECTION - 2, RPG - 1, offsets)
    offsets = jnp.where(sections == N_SECTION - 1, 0, offsets)
    return ((sections + 1) % N_SECTION * RPG + offsets).astype(jnp.int32)


def place_ends(drawn, stream_key, low, high):
    dims = drawn.shape
    place = [jax.random.randint(jax.random.fold_in(stream_key, axis), (), 0, dims[axis]) for axis in range(len(dims))]
    drawn = drawn.at[tuple(place)].set(low)
    longest = dims.index(max(dims))
    place[longest] = (place[longest] + 1) % dims[longest]
    return drawn.at[tuple(place)].set(high)


def level_of(rng, dims, shards, smallest, top_value):
    loudness, own = 1.0, jax.random.fold_in(rng, 6)
    for axis_at, shards_of in shards:
        heights = jnp.exp(jax.random.uniform(jax.random.fold_in(own, axis_at), (shards_of,), jnp.float32, smallest / len(shards), top_value / len(shards)))
        loudness = loudness * jnp.repeat(heights, dims[axis_at] // shards_of).reshape([-1 if axis == axis_at else 1 for axis in range(len(dims))])
    return loudness


def routed_block(key, own, number, rows, amount, top, bound, skew):
    ranking = jax.random.permutation(key, amount)
    packed, usual = shares(amount, rows * top, bound, skew, True), shares(amount, rows * top, bound, skew, False)
    places = jnp.arange(amount)

    def named(sizes, rotation):
        used = int((sizes > 0).sum())
        fixed = max(1, used // 4)
        moved = fixed + (places - fixed + rotation * (used - fixed)) % max(1, amount - fixed)
        return jnp.zeros((amount,), jnp.int32).at[ranking[jnp.where(places < fixed, places, moved)]].set(jnp.asarray(sizes, jnp.int32))

    sizes = jnp.where(number % 4 == 0, named(packed, number // 4), named(usual, number - number // 4 - 1))
    mixed = jax.random.permutation(jax.random.fold_in(own, 3), amount)
    source_of, taker = mixed[0:amount // 2 * 2:2], mixed[1:amount // 2 * 2:2]
    slack = jnp.minimum(sizes[source_of] - 1, bound - sizes[taker]) // 2
    slack = jnp.where((source_of == ranking[0]) | (taker == ranking[0]) | (sizes[taker] == 0), 0, jnp.maximum(slack, 0))
    moved = jax.random.randint(jax.random.fold_in(own, 4), (amount // 2,), 0, 1 << 20) % (slack + 1)
    sizes = sizes.at[source_of].add(-moved).at[taker].add(moved)
    labels = jnp.searchsorted(jnp.cumsum(sizes), jnp.arange(rows * top), side="right").astype(jnp.int32)
    table = labels.reshape(top, rows).T
    table = table[jax.random.permutation(jax.random.fold_in(own, 1), rows)]
    rotation = jax.random.randint(jax.random.fold_in(own, 2), (rows, 1), 0, top)
    return jnp.take_along_axis(table, (jnp.arange(top)[None, :] + rotation) % top, axis=1)


def shares(number_of, total, limit, slope, full):
    weights = [(1 << 20) // math.isqrt(standing ** slope) + 1 for standing in range(1, number_of + 1)]
    largest = limit if full else min(limit, max(-(-total // number_of), total * weights[0] // sum(weights)))
    least = 1 if total - largest >= number_of - 1 else 0
    given, rest = [largest] + [least] * (number_of - 1), total - largest - least * (number_of - 1)
    while rest > 0:
        movable = [i for i in range(1, number_of) if given[i] < largest] or [i for i in range(1, number_of) if given[i] < limit]
        mass, left = sum([weights[i] for i in movable]), rest
        for i in movable:
            more = min(limit - given[i], max(1, left * weights[i] // mass), rest)
            given[i] = given[i] + more
            rest = rest - more
    return np.array(given)


def gaussian(own_key, extent, scale, limit, cuts=(), kind=jnp.bfloat16):
    array = jax.random.normal(own_key, extent, jnp.float32) * scale
    if len(cuts) > 0:
        array = level_of(own_key, extent, cuts, -0.22, 0.18) * array
    return jnp.clip(array, min=-limit, max=limit).astype(kind)


def setup_inputs(seed: int = 0) -> dict:
    key_of = jax.random.split(jax.random.key(seed), 15)
    prefill_hidden_states = gaussian(key_of[0], (CROWS, MODEL_WIDTH), 1.0, 6.0, ((0, 64),))
    decode_hidden_states = gaussian(key_of[1], (STEPS, B, MODEL_WIDTH), 1.0, 6.0, ((1, 4), (2, 16)))
    query_matrix = gaussian(key_of[2], (MODEL_WIDTH, H * HD), MODEL_WIDTH ** -0.5, 0.0625, ((0, 16), (1, 2)))
    key_matrix = gaussian(key_of[3], (MODEL_WIDTH, KEY_VALUE_WIDTH), MODEL_WIDTH ** -0.5, 0.0625, ((0, 16), (1, 2)))
    value_matrix = gaussian(key_of[4], (MODEL_WIDTH, KEY_VALUE_WIDTH), MODEL_WIDTH ** -0.5, 0.0625, ((0, 16), (1, 2)))
    adapter_down_maps = gaussian(key_of[5], (MODEL_WIDTH, 2 * ADAPTER_COUNT * ADAPTER_RANK), MODEL_WIDTH ** -0.5, 0.0625, ((0, 16), (1, 2)))
    key_adapter_up_maps = gaussian(key_of[6], (ADAPTER_COUNT * ADAPTER_RANK, KEY_VALUE_WIDTH), ADAPTER_RANK ** -0.5, 1.5, ((1, 2),))
    value_adapter_up_maps = gaussian(key_of[7], (ADAPTER_COUNT * ADAPTER_RANK, KEY_VALUE_WIDTH), ADAPTER_RANK ** -0.5, 1.5, ((1, 2),))
    request_key_cache = draw_request_key_cache(jax.random.fold_in(key_of[14], 71), 0)
    request_value_cache = gaussian(key_of[9], (B, L, KEY_VALUE_WIDTH), 1.0, 6.0, ((0, 4), (1, 16), (2, 2)))
    request_adapter_index = place_ends(jax.random.randint(key_of[10], (B,), 0, ADAPTER_COUNT), jax.random.fold_in(key_of[10], 1), 0, ADAPTER_COUNT - 1).astype(jnp.int32)
    prefill_request_target = draw_prefill_request_target(jax.random.fold_in(key_of[14], 71), 0)
    request_context_length = draw_request_context_length(jax.random.fold_in(key_of[14], 71), 0)
    page_owner_index_keys = jax.random.split(jax.random.fold_in(key_of[13], 1), NBLK // BPD)
    page_owner_index_turns = jax.random.permutation(jax.random.fold_in(key_of[13], 3), NBLK // BPD)
    page_owner_index = jax.vmap(lambda own, number: routed_block(jax.random.fold_in(key_of[13], 2), own, number, BPD, N_CTX, 1, SEND_MOST, 2))(page_owner_index_keys, page_owner_index_turns).reshape((NBLK, 1))
    return dict(prefill_hidden_states=prefill_hidden_states, decode_hidden_states=decode_hidden_states, query_matrix=query_matrix, key_matrix=key_matrix, value_matrix=value_matrix, adapter_down_maps=adapter_down_maps, key_adapter_up_maps=key_adapter_up_maps, value_adapter_up_maps=value_adapter_up_maps, request_key_cache=request_key_cache, request_value_cache=request_value_cache, request_adapter_index=request_adapter_index, prefill_request_target=prefill_request_target, request_context_length=request_context_length, page_owner_index=page_owner_index)


ADAPTER_SCALE = 0.5
NEG_FLOOR = -1e30


def add_adapter_delta(base_projection, down_columns_half, token_adapter_indices, adapter_up_maps):
    column_adapter = jnp.arange(ADAPTER_COUNT * ADAPTER_RANK, dtype=jnp.int32) // ADAPTER_RANK
    select = column_adapter[None, :] == token_adapter_indices[:, None]
    selected_maps = jnp.where(select, down_columns_half, jnp.zeros_like(down_columns_half))
    adapter_delta = jnp.dot(selected_maps, adapter_up_maps, preferred_element_type=jnp.float32)
    return (base_projection + ADAPTER_SCALE * adapter_delta).astype(jnp.bfloat16)


def owner_pages(span_rows, placing):
    blocks = span_rows.reshape(N_SECTION, N_CTX, BPD, BLK * KEY_VALUE_WIDTH).astype(jnp.float32)
    sent = jnp.einsum("scob,scbe->scoe", placing, blocks).astype(jnp.bfloat16)
    sent = sent.reshape(N_SECTION, N_CTX, N_CTX, SEND_MOST, BLK * KEY_VALUE_WIDTH)
    arrived = jnp.transpose(jnp.roll(sent, 1, axis=0), (0, 2, 1, 3, 4))
    return arrived.reshape(N_SECTION * N_CTX * SLOTS, BLK, KEY_VALUE_WIDTH)


def reference(prefill_hidden_states, decode_hidden_states, query_matrix, key_matrix, value_matrix, adapter_down_maps, key_adapter_up_maps, value_adapter_up_maps, request_key_cache, request_value_cache, request_adapter_index, prefill_request_target, request_context_length, page_owner_index):
    rank_half_width = ADAPTER_COUNT * ADAPTER_RANK
    prefill_down_product = jnp.dot(prefill_hidden_states, adapter_down_maps, preferred_element_type=jnp.float32).astype(jnp.bfloat16)
    row_request = prefill_request_target[jnp.arange(CROWS, dtype=jnp.int32) // SPAN]
    token_adapter_index = request_adapter_index[row_request]
    prefill_key_rows = add_adapter_delta(jnp.dot(prefill_hidden_states, key_matrix, preferred_element_type=jnp.float32), prefill_down_product[:, :rank_half_width], token_adapter_index, key_adapter_up_maps)
    prefill_value_rows = add_adapter_delta(jnp.dot(prefill_hidden_states, value_matrix, preferred_element_type=jnp.float32), prefill_down_product[:, rank_half_width:], token_adapter_index, value_adapter_up_maps)

    owners = page_owner_index[:, 0].reshape(N_SECTION, N_CTX, BPD)
    order = jnp.arange(BPD, dtype=jnp.int32)
    same_owner = owners[..., :, None] == owners[..., None, :]
    earlier = order[None, :] < order[:, None]
    rank = jnp.sum(jnp.logical_and(same_owner, earlier), axis=-1).astype(jnp.int32)
    slot_of = owners * SEND_MOST + rank
    placing = (slot_of[..., None, :] == jnp.arange(SLOTS, dtype=jnp.int32)[:, None]).astype(jnp.float32)
    page_keys = owner_pages(prefill_key_rows, placing)
    page_values = owner_pages(prefill_value_rows, placing)
    taken = jnp.sum(placing, axis=-1).reshape(N_SECTION, N_CTX, N_CTX, SEND_MOST)
    taken = jnp.transpose(jnp.roll(taken, 1, axis=0), (0, 2, 1, 3)).reshape(N_SECTION, N_CTX, SLOTS)
    page_live = jnp.repeat(taken, BLK, axis=-1) > 0.5
    page_request = jnp.roll(prefill_request_target, 1)

    cache_k = request_key_cache.reshape(B, N_CTX, CTX_DEV, KVH, HD)
    cache_v = request_value_cache.reshape(B, N_CTX, CTX_DEV, KVH, HD)
    pages_k = page_keys.reshape(N_SECTION, N_CTX, SLOTS * BLK, KVH, HD)
    pages_v = page_values.reshape(N_SECTION, N_CTX, SLOTS * BLK, KVH, HD)
    positions = jnp.arange(L, dtype=jnp.int32).reshape(N_CTX, CTX_DEV)
    inv_root = HD ** -0.5
    group_heads = H // KVH

    decode_key_rows = []
    decode_value_rows = []
    attended = []
    for step in range(STEPS):
        step_hidden_states = decode_hidden_states[step]
        queries = jnp.dot(step_hidden_states, query_matrix, preferred_element_type=jnp.float32).astype(jnp.bfloat16)
        decode_down_product = jnp.dot(step_hidden_states, adapter_down_maps, preferred_element_type=jnp.float32).astype(jnp.bfloat16)
        decode_key_rows.append(add_adapter_delta(jnp.dot(step_hidden_states, key_matrix, preferred_element_type=jnp.float32), decode_down_product[:, :rank_half_width], request_adapter_index, key_adapter_up_maps))
        decode_value_rows.append(add_adapter_delta(jnp.dot(step_hidden_states, value_matrix, preferred_element_type=jnp.float32), decode_down_product[:, rank_half_width:], request_adapter_index, value_adapter_up_maps))
        stacked_k = jnp.stack(decode_key_rows, axis=1)
        stacked_v = jnp.stack(decode_value_rows, axis=1)

        def attend_one(index):
            group = index // RPG
            query = queries[index].reshape(KVH, group_heads, HD).astype(jnp.float32)
            keys = jnp.concatenate([cache_k[index], pages_k[group]], axis=1).astype(jnp.float32)
            values = jnp.concatenate([cache_v[index], pages_v[group]], axis=1).astype(jnp.float32)
            live = jnp.concatenate([positions < request_context_length[index], jnp.logical_and(page_live[group], page_request[group] == index)], axis=1)
            scores = jnp.einsum("kgd,cpkd->ckgp", query, keys) * inv_root
            live_wide = live[:, None, None, :]
            block_max = jnp.max(jnp.where(live_wide, scores, NEG_FLOOR), axis=-1)
            weights = jnp.where(live_wide, jnp.exp(scores - block_max[..., None]), 0.0).astype(jnp.bfloat16)
            weights = lax.optimization_barrier(weights).astype(jnp.float32)
            block_total = jnp.sum(weights, axis=-1)
            block_out = jnp.einsum("ckgp,cpkd->ckgd", weights, values)
            own_keys = stacked_k[index].reshape(step + 1, KVH, HD).astype(jnp.float32)
            own_values = stacked_v[index].reshape(step + 1, KVH, HD).astype(jnp.float32)
            token_scores = jnp.einsum("kgd,ukd->kgu", query, own_keys) * inv_root
            top = jnp.maximum(jnp.max(block_max, axis=0), jnp.max(token_scores, axis=-1))
            block_scale = jnp.exp(block_max - top[None])
            token_weights = jnp.exp(token_scores - top[..., None])
            numer = jnp.sum(block_out * block_scale[..., None], axis=0) + jnp.einsum("kgu,ukd->kgd", token_weights, own_values)
            denom = jnp.sum(block_total * block_scale, axis=0) + jnp.sum(token_weights, axis=-1)
            return (numer / denom[..., None]).reshape(H * HD).astype(jnp.bfloat16)

        attended.append(lax.map(attend_one, jnp.arange(B, dtype=jnp.int32)))
    return page_keys, page_values, jnp.stack(attended, axis=0)
```

```python
import functools

import jax
import jax.numpy as jnp
from jax import lax
from jax.experimental import pallas as pl
from jax.experimental.pallas import tpu as pltpu
from jax.sharding import PartitionSpec as P

H = 64
KVH = 8
HD = 128
ADAPTER_RANK = 16
BLK = 32
STEPS = 2

ADAPTER_SCALE = 0.5
NEG_FLOOR = -1e30
INV_ROOT = HD ** (-0.5)

SIDE = 4
N_CTX = 16
SHARD = 512
UNITS = 9
HEADS = 4
ROWS = 512
SLOT_ROWS = 1024
PAIR = 64
RPG = 4
CTX_DEV = 1024
QROWS = 64
DBLOCKS = 48
PER = 3

MESH = pl.DeviceIdType.MESH
F32 = jnp.float32
BF16 = jnp.bfloat16


def pick_entry(table, wanted):
    places = jnp.arange(table.shape[0], dtype=jnp.int32)
    return jnp.sum(jnp.where(places == wanted, table, 0))


def wait_bytes(ref, sem):
    pltpu.make_async_copy(ref, ref, sem).wait()


def nt_dot(a, b):
    return lax.dot_general(a, b, (((1,), (1,)), ((), ())), preferred_element_type=F32)


def layer_kernel(
    info,
    xd,
    drow,
    x_hbm,
    wq_hbm,
    wk_hbm,
    wv_hbm,
    wd_hbm,
    uk_hbm,
    uv_hbm,
    kc_hbm,
    vc_hbm,
    pk_out,
    pv_out,
    att_out,
    x_v,
    w_v,
    wq_v,
    up_v,
    kc_v,
    vc_v,
    acc,
    dn,
    row,
    raw,
    place_m,
    drow_r,
    sendb,
    pages,
    part,
    rsr,
    ag,
    qp,
    tkv,
    pst,
    mgs,
    mgr,
    att,
    w_load,
    q_load,
    x_load,
    c_load,
    u_load,
    g_recv,
    g_send,
    row_send,
    row_recv,
    a_send,
    a_recv,
    small_send,
    small_recv,
    out_sem,
):
    s = lax.axis_index("section")
    c = lax.axis_index("ctx")
    t = lax.axis_index("tp")
    n_sec = lax.axis_size("section")
    y = c // SIDE
    z = lax.rem(c, SIDE)

    def chip(dy, dz):
        return lax.rem(y + dy + SIDE, SIDE) * SIDE + lax.rem(z + dz + SIDE, SIDE)

    def here(ctx):
        return (s, ctx, t)

    right = (lax.rem(s + 1, n_sec), c, t)
    left = (lax.rem(s + n_sec - 1, n_sec), c, t)
    partner = (s, c, 1 - t)

    barrier = pltpu.get_barrier_semaphore()

    @pl.loop(1, N_CTX)
    def _(j):
        pl.semaphore_signal(
            barrier, inc=1, device_id=here(lax.rem(c + j, N_CTX)), device_id_type=MESH
        )

    for peer in (left, right, partner):
        pl.semaphore_signal(barrier, inc=1, device_id=peer, device_id_type=MESH)

    mine = pl.ds(pl.multiple_of(c * SHARD, SHARD), SHARD)
    loads = [pltpu.make_async_copy(wd_hbm, w_v.at[0, mine], w_load.at[0])]
    for h in range(HEADS):
        cols = pl.ds(h * HD, HD)
        loads.append(
            pltpu.make_async_copy(wk_hbm.at[:, cols], w_v.at[1 + h, mine], w_load.at[1 + h])
        )
    for h in range(HEADS):
        cols = pl.ds(h * HD, HD)
        loads.append(
            pltpu.make_async_copy(wv_hbm.at[:, cols], w_v.at[5 + h, mine], w_load.at[5 + h])
        )
    for load in loads:
        load.start()
    q_copy = pltpu.make_async_copy(wq_hbm, wq_v, q_load)
    q_copy.start()
    ups = []
    for h in range(HEADS):
        cols = pl.ds(h * HD, HD)
        ups.append(pltpu.make_async_copy(uk_hbm.at[:, cols], up_v.at[h], u_load.at[h]))
        ups.append(pltpu.make_async_copy(uv_hbm.at[:, cols], up_v.at[4 + h], u_load.at[4 + h]))
    for load in ups:
        load.start()
    x_copy = pltpu.make_async_copy(x_hbm, x_v, x_load)
    x_copy.start()
    k_copy = pltpu.make_async_copy(kc_hbm, kc_v, c_load.at[0])
    v_copy = pltpu.make_async_copy(vc_hbm, vc_v, c_load.at[1])
    k_copy.start()
    v_copy.start()

    pl.semaphore_wait(barrier, N_CTX + 2)

    def send(src, dst, send_sem, recv_sem, device):
        pltpu.make_async_remote_copy(
            src_ref=src,
            dst_ref=dst,
            send_sem=send_sem,
            recv_sem=recv_sem,
            device_id=device,
            device_id_type=MESH,
        ).start()

    send(drow, drow_r, small_send.at[0], small_recv.at[0], right)

    for load in loads:
        load.wait()
    for load in ups:
        load.wait()

    def pass_on(u, stage, shard, first, count, ctx):
        rows = pl.ds(pl.multiple_of(shard * SHARD + first, 128), count)
        piece = w_v.at[u, rows]
        send(piece, piece, g_send.at[u], g_recv.at[u, stage], here(ctx))

    yp, ym, zp, zm = chip(1, 0), chip(-1, 0), chip(0, 1), chip(0, -1)
    A, B, A0, A1, B0, B1, ZERO = (
        (0, 256),
        (256, 256),
        (128, 128),
        (0, 128),
        (256, 128),
        (384, 128),
        (128, 256),
    )

    def stage1(u):
        for ctx in (yp, zp, ym, zm):
            pass_on(u, 0, c, 0, SHARD, ctx)

    def stage2(u):
        wait_bytes(w_v.at[u, pl.ds(0, 4 * SHARD)], g_recv.at[u, 0])
        pass_on(u, 1, ym, *ZERO, yp)
        pass_on(u, 1, yp, *A1, ym)
        pass_on(u, 1, yp, *B1, ym)
        pass_on(u, 1, zm, *ZERO, zp)
        pass_on(u, 1, zp, *A1, zm)
        pass_on(u, 1, zp, *B1, zm)
        for shard in (ym, yp):
            for ctx in (zp, zm):
                pass_on(u, 1, shard, *A, ctx)
        for shard in (zm, zp):
            for ctx in (yp, ym):
                pass_on(u, 1, shard, *B, ctx)

    def stage3(u):
        wait_bytes(w_v.at[u, pl.ds(0, 6 * SHARD)], g_recv.at[u, 1])
        yy, zz = chip(2, 0), chip(0, 2)
        for ctx in (zp, zm):
            pass_on(u, 2, yy, *A, ctx)
        for ctx in (yp, ym):
            pass_on(u, 2, zz, *B, ctx)
        for d in (-1, 1):
            pass_on(u, 2, chip(d, -1), *A0, zp)
            pass_on(u, 2, chip(d, 1), *A1, zm)
            pass_on(u, 2, chip(-1, d), *B0, yp)
            pass_on(u, 2, chip(1, d), *B1, ym)

    def stage4(u):
        wait_bytes(w_v.at[u, pl.ds(0, 4 * SHARD)], g_recv.at[u, 2])
        pass_on(u, 3, chip(2, -1), *A0, zp)
        pass_on(u, 3, chip(2, 1), *A1, zm)
        pass_on(u, 3, chip(-1, 2), *B0, yp)
        pass_on(u, 3, chip(1, 2), *B1, ym)

    def project(u):
        wait_bytes(w_v.at[u, pl.ds(0, SHARD)], g_recv.at[u, 3])

        @pl.when(u == 0)
        def _():
            x_copy.wait()

        acc[...] = jnp.zeros_like(acc)

        @pl.loop(0, 8)
        def _(i):
            part_k = pl.ds(pl.multiple_of(i * 1024, 1024), 1024)
            acc[...] += jnp.dot(x_v[:, part_k], w_v[u, part_k], preferred_element_type=F32)

        @pl.when(u == 0)
        def _():
            dn[t] = acc[...].astype(BF16)
            send(dn.at[t], dn.at[t], small_send.at[1], small_recv.at[1], partner)

        @pl.when(u == 1)
        def _():
            wait_bytes(dn.at[0], small_recv.at[1])

        @pl.when(u > 0)
        def _():
            n = u - 1
            column = lax.broadcasted_iota(jnp.int32, (ROWS, HD), 1) // ADAPTER_RANK
            picked = jnp.where(column == info[8], dn[n // HEADS].astype(F32), 0.0).astype(BF16)
            delta = jnp.dot(picked, up_v[n], preferred_element_type=F32)
            row[n] = (acc[...] + ADAPTER_SCALE * delta).astype(BF16)
            send(row.at[n], raw.at[n], row_send.at[n], row_recv.at[n], right)

    def exchange(n):
        @pl.loop(1, N_CTX)
        def _(j):
            ctx = lax.rem(c + j, N_CTX)
            theirs = pl.ds(pl.multiple_of(ctx * PAIR, PAIR), PAIR)
            ours = pl.ds(pl.multiple_of(c * PAIR, PAIR), PAIR)
            send(
                sendb.at[n, theirs], pages.at[n, ours], a_send.at[n], a_recv.at[n], here(ctx)
            )

        ours = pl.ds(pl.multiple_of(c * PAIR, PAIR), PAIR)
        pages[n, ours] = sendb[n, ours]

    def place(n):
        wait_bytes(raw.at[n], row_recv.at[n])

        @pl.loop(0, 4)
        def _(i):
            some = pl.ds(pl.multiple_of(i * 256, 256), 256)
            sendb[n, some] = jnp.dot(
                place_m[some], raw[n], preferred_element_type=F32
            ).astype(BF16)

        exchange(n)

    def page_flags():
        wait_bytes(drow_r, small_recv.at[0])

        @pl.loop(0, 4)
        def _(i):
            some = pl.ds(pl.multiple_of(i * 256, 256), 256)
            slot_row = lax.broadcasted_iota(jnp.int32, (256, ROWS), 0) + i * 256
            hit = slot_row == drow_r[0:1]
            place_m[some] = jnp.where(hit, 1.0, 0.0).astype(BF16)
            flag = jnp.max(jnp.where(hit, 1.0, 0.0), axis=1, keepdims=True)
            sendb[8, some] = jnp.broadcast_to(flag, (256, HD)).astype(BF16)

        exchange(8)

    def landed(n):
        wait_bytes(pages.at[n, pl.ds(0, SLOT_ROWS - PAIR)], a_recv.at[n])

    def write_out(n):
        cols = pl.ds(pl.multiple_of(lax.rem(n, HEADS) * HD, HD), HD)

        @pl.when(n < HEADS)
        def _():
            pltpu.make_async_copy(pages.at[n], pk_out.at[:, cols], out_sem.at[n]).start()

        @pl.when(n >= HEADS)
        def _():
            pltpu.make_async_copy(pages.at[n], pv_out.at[:, cols], out_sem.at[n]).start()

    def decode_project():
        q_copy.wait()

        def blocks(product, first):
            for i in range(product.shape[1] // HD):
                part[first + i] = product[:, i * HD : (i + 1) * HD]

        hidden = xd[...]
        part[DBLOCKS - 6 :] = jnp.zeros((6, 8, HD), F32)
        for i in range(8):
            piece = wq_v[:, i * 512 : (i + 1) * 512]
            blocks(jnp.dot(hidden, piece, preferred_element_type=F32), 4 * i)
        for u in range(1, UNITS):
            blocks(jnp.dot(hidden, w_v[u, mine], preferred_element_type=F32), 31 + u)
        part[40 + t] = jnp.dot(hidden, w_v[0, mine], preferred_element_type=F32)
        send(part.at[40 + t], part.at[40 + t], small_send.at[2], small_recv.at[2], partner)
        wait_bytes(part.at[0], small_recv.at[2])

        @pl.loop(1, N_CTX)
        def _(j):
            ctx = lax.rem(c + j, N_CTX)
            send(
                part.at[pl.ds(ctx * PER, PER)],
                rsr.at[c],
                small_send.at[3],
                small_recv.at[3],
                here(ctx),
            )

        rsr[c] = part[pl.ds(c * PER, PER)]

    def decode_sum():
        wait_bytes(rsr.at[pl.ds(0, N_CTX - 1)], small_recv.at[3])
        ag[pl.ds(c * PER, PER)] = jnp.sum(rsr[...], axis=0)

        @pl.loop(1, N_CTX)
        def _(j):
            ctx = lax.rem(c + j, N_CTX)
            piece = ag.at[pl.ds(c * PER, PER)]
            send(piece, piece, small_send.at[4], small_recv.at[4], here(ctx))

    def decode_rows():
        wait_bytes(ag.at[pl.ds(0, (N_CTX - 1) * PER)], small_recv.at[4])
        to = lax.broadcasted_iota(jnp.int32, (QROWS, QROWS), 0)
        at = lax.broadcasted_iota(jnp.int32, (QROWS, QROWS), 1)
        source = lax.rem(to, 8) * 8 + lax.rem(to // 8, STEPS) * RPG + to // 16
        perm = jnp.where(at == source, 1.0, 0.0).astype(BF16)
        for k in range(HEADS):
            queries = ag[8 * k : 8 * k + 8].reshape(QROWS, HD).astype(BF16)
            qp[k] = jnp.dot(perm, queries, preferred_element_type=F32).astype(BF16)
        lane = lax.broadcasted_iota(jnp.int32, (8, HD), 1) // ADAPTER_RANK
        who = lax.rem(lax.broadcasted_iota(jnp.int32, (8, HD), 0), RPG)
        adapter = jnp.zeros((8, HD), jnp.int32)
        for b in range(RPG):
            adapter = jnp.where(who == b, info[9 + b], adapter)
        for kind in range(2):
            down = ag[40 + kind].astype(BF16).astype(F32)
            picked = jnp.where(lane == adapter, down, 0.0).astype(BF16)
            for k in range(HEADS):
                n = 4 * kind + k
                delta = jnp.dot(picked, up_v[n], preferred_element_type=F32)
                tkv[n] = (ag[32 + n] + ADAPTER_SCALE * delta).astype(BF16).astype(F32)

    def cache_block(b):
        @pl.when(b == 0)
        def _():
            k_copy.wait()
            v_copy.wait()

        left_len = info[b]
        live = lax.broadcasted_iota(jnp.int32, (16, CTX_DEV), 1) < left_len
        rows = pl.ds(pl.multiple_of(b * 16, 16), 16)
        for k in range(HEADS):
            cols = slice(k * HD, (k + 1) * HD)
            scores = nt_dot(qp[k, rows], kc_v[b, :, cols]) * INV_ROOT
            block_max = jnp.max(jnp.where(live, scores, NEG_FLOOR), axis=1, keepdims=True)
            weights = jnp.where(live, jnp.exp(scores - block_max), 0.0).astype(BF16)
            total = jnp.sum(weights.astype(F32), axis=1, keepdims=True)
            pst[0, k, rows] = jnp.broadcast_to(block_max, (16, HD))
            pst[1, k, rows] = jnp.broadcast_to(total, (16, HD))
            pst[2, k, rows] = jnp.dot(weights, vc_v[b, :, cols], preferred_element_type=F32)

    @pl.loop(0, UNITS + 6)
    def _(i):
        @pl.when(i < UNITS)
        def _():
            stage1(i)

        @pl.when(i == 0)
        def _():
            decode_project()

        @pl.when((i >= 3) & (i < UNITS + 3))
        def _():
            stage4(i - 3)

        @pl.when((i >= 2) & (i < UNITS + 2))
        def _():
            stage3(i - 2)

        @pl.when((i >= 1) & (i < UNITS + 1))
        def _():
            stage2(i - 1)

        @pl.when(i == 1)
        def _():
            decode_sum()
            page_flags()

        @pl.when(i == 2)
        def _():
            decode_rows()

        @pl.when((i >= 3) & (i < 3 + RPG))
        def _():
            cache_block(i - 3)

        @pl.when((i >= 4) & (i < UNITS + 4))
        def _():
            project(i - 4)

        @pl.when((i >= 6) & (i < UNITS + 5))
        def _():
            place(i - 6)

        @pl.when(i >= 7)
        def _():
            landed(i - 7)
            write_out(i - 7)

    landed(8)

    live = nt_dot(jnp.ones((16, HD), BF16), pages[8]) > 0.5
    which = lax.broadcasted_iota(jnp.int32, (QROWS, 8), 0)
    other = lax.broadcasted_iota(jnp.int32, (QROWS, 8), 1)
    tok_live = (
        (lax.rem(other, RPG) == which // 16)
        & (other // RPG <= lax.rem(which // 8, STEPS))
        & (c == 0)
    )
    lane = lax.broadcasted_iota(jnp.int32, (16, HD), 1)
    for k in range(HEADS):
        query = jnp.zeros((16, HD), F32)
        for b in range(RPG):
            query = jnp.where(info[4 + b] == 1, qp[k, b * 16 : b * 16 + 16].astype(F32), query)
        scores = nt_dot(query.astype(BF16), pages[k]) * INV_ROOT
        p_max = jnp.max(jnp.where(live, scores, NEG_FLOOR), axis=1, keepdims=True)
        weights = jnp.where(live, jnp.exp(scores - p_max), 0.0).astype(BF16)
        p_total = jnp.sum(weights.astype(F32), axis=1, keepdims=True)
        p_out = jnp.dot(weights, pages[4 + k], preferred_element_type=F32)
        tok = nt_dot(qp[k], tkv[k].astype(BF16)) * INV_ROOT
        tok_max = jnp.max(jnp.where(tok_live, tok, NEG_FLOOR), axis=1, keepdims=True)
        tok_w = jnp.where(tok_live, jnp.exp(tok - tok_max), 0.0)
        tok_total = jnp.sum(tok_w, axis=1, keepdims=True)
        tok_out = jnp.zeros((QROWS, HD), F32)
        for i in range(8):
            tok_out = tok_out + tok_w[:, i : i + 1] * tkv[4 + k, i : i + 1]
        for b in range(RPG):
            rows = slice(b * 16, b * 16 + 16)
            wanted = info[4 + b] == 1
            pm = jnp.where(wanted, p_max, NEG_FLOOR)
            pt = jnp.where(wanted, p_total, 0.0)
            po = jnp.where(wanted, p_out, 0.0)
            cm = pst[0, k, rows]
            tm = tok_max[rows]
            top = jnp.maximum(jnp.maximum(cm, pm), tm)
            c_scale, p_scale, t_scale = jnp.exp(cm - top), jnp.exp(pm - top), jnp.exp(tm - top)
            total = c_scale * pst[1, k, rows] + p_scale * pt + t_scale * tok_total[rows]
            mgs[k * 4 + b, 0] = (
                c_scale * pst[2, k, rows] + p_scale * po + t_scale * tok_out[rows]
            )
            mgs[k * 4 + b, 1] = jnp.where(lane < 64, top, total)

    @pl.loop(1, N_CTX)
    def _(j):
        ctx = lax.rem(c + j, N_CTX)
        send(mgs.at[ctx], mgr.at[c], small_send.at[5], small_recv.at[5], here(ctx))

    mgr[c] = mgs[c]
    wait_bytes(mgr.at[pl.ds(0, N_CTX - 1)], small_recv.at[5])
    stats = mgr[:, 1]
    tops, totals = stats[:, :, 0:1], stats[:, :, 64:65]
    scale = jnp.exp(tops - jnp.max(tops, axis=0, keepdims=True))
    numer = jnp.sum(scale * mgr[:, 0], axis=0)
    denom = jnp.sum(scale * totals, axis=0)
    att[c] = (numer / denom).astype(BF16)

    @pl.loop(1, N_CTX)
    def _(j):
        ctx = lax.rem(c + j, N_CTX)
        send(att.at[c], att.at[c], small_send.at[6], small_recv.at[6], here(ctx))

    wait_bytes(att.at[pl.ds(0, N_CTX - 1)], small_recv.at[6])
    att_out[...] = att[...]

    @pl.loop(0, UNITS)
    def _(u):
        wait_bytes(w_v.at[u, pl.ds(0, 15 * SHARD)], g_send.at[u])
        wait_bytes(sendb.at[u, pl.ds(0, SLOT_ROWS - PAIR)], a_send.at[u])

    @pl.loop(0, 2 * HEADS)
    def _(n):
        wait_bytes(row.at[n], row_send.at[n])
        wait_bytes(pages.at[n], out_sem.at[n])

    wait_bytes(drow, small_send.at[0])
    wait_bytes(dn.at[0], small_send.at[1])
    wait_bytes(part.at[0], small_send.at[2])
    wait_bytes(rsr.at[pl.ds(0, N_CTX - 1)], small_send.at[3])
    wait_bytes(ag.at[pl.ds(0, (N_CTX - 1) * PER)], small_send.at[4])
    wait_bytes(mgr.at[pl.ds(0, N_CTX - 1)], small_send.at[5])
    wait_bytes(att.at[pl.ds(0, N_CTX - 1)], small_send.at[6])


def on_device(
    prefill_hidden_states,
    decode_hidden_states,
    query_matrix,
    key_matrix,
    value_matrix,
    adapter_down_maps,
    key_adapter_up_maps,
    value_adapter_up_maps,
    request_key_cache,
    request_value_cache,
    request_adapter_index,
    prefill_request_target,
    request_context_length,
    page_owner_index,
):
    n_section = lax.axis_size("section")
    section_at = lax.axis_index("section")
    ctx_at = lax.axis_index("ctx")
    span_request = pick_entry(prefill_request_target, section_at)
    span_adapter = pick_entry(request_adapter_index, span_request)
    page_request = pick_entry(prefill_request_target, (section_at + n_section - 1) % n_section)
    local_ids = section_at * RPG + jnp.arange(RPG, dtype=jnp.int32)
    batch_ids = jnp.arange(request_adapter_index.shape[0], dtype=jnp.int32)
    adapters = jnp.sum(
        jnp.where(local_ids[:, None] == batch_ids[None, :], request_adapter_index[None, :], 0),
        axis=1,
    )
    info = jnp.concatenate(
        [
            request_context_length - ctx_at * CTX_DEV,
            (local_ids == page_request).astype(jnp.int32),
            span_adapter[None],
            adapters,
            jnp.zeros((3,), jnp.int32),
        ]
    ).astype(jnp.int32)
    owners = page_owner_index[:, 0]
    order = jnp.arange(owners.shape[0], dtype=jnp.int32)
    earlier = (owners[None, :] == owners[:, None]) & (order[None, :] < order[:, None])
    slot_of = owners * 2 + jnp.sum(earlier, axis=1).astype(jnp.int32)
    drow = (slot_of[:, None] * BLK + jnp.arange(BLK, dtype=jnp.int32)[None, :]).reshape(1, ROWS)
    drow = jnp.broadcast_to(drow, (8, ROWS))
    decode_rows = decode_hidden_states.reshape(STEPS * RPG, SHARD)

    hbm = pl.BlockSpec(memory_space=pl.ANY)
    vmem = pl.BlockSpec(memory_space=pltpu.VMEM)
    smem = pl.BlockSpec(memory_space=pltpu.SMEM)
    dma = pltpu.SemaphoreType.DMA
    page_keys, page_values, attended = pl.pallas_call(
        layer_kernel,
        out_shape=(
            jax.ShapeDtypeStruct((SLOT_ROWS, HEADS * HD), BF16),
            jax.ShapeDtypeStruct((SLOT_ROWS, HEADS * HD), BF16),
            jax.ShapeDtypeStruct((N_CTX, 16, HD), BF16),
        ),
        in_specs=[smem, vmem, vmem] + [hbm] * 9,
        out_specs=(hbm, hbm, vmem),
        scratch_shapes=[
            pltpu.VMEM((ROWS, 8192), BF16),
            pltpu.VMEM((UNITS, 8192, HD), BF16),
            pltpu.VMEM((SHARD, 4096), BF16),
            pltpu.VMEM((8, HD, HD), BF16),
            pltpu.VMEM((RPG, CTX_DEV, HEADS * HD), BF16),
            pltpu.VMEM((RPG, CTX_DEV, HEADS * HD), BF16),
            pltpu.VMEM((ROWS, HD), F32),
            pltpu.VMEM((2, ROWS, HD), BF16),
            pltpu.VMEM((8, ROWS, HD), BF16),
            pltpu.VMEM((8, ROWS, HD), BF16),
            pltpu.VMEM((SLOT_ROWS, ROWS), BF16),
            pltpu.VMEM((8, ROWS), jnp.int32),
            pltpu.VMEM((9, SLOT_ROWS, HD), BF16),
            pltpu.VMEM((9, SLOT_ROWS, HD), BF16),
            pltpu.VMEM((DBLOCKS, 8, HD), F32),
            pltpu.VMEM((N_CTX, PER, 8, HD), F32),
            pltpu.VMEM((DBLOCKS, 8, HD), F32),
            pltpu.VMEM((HEADS, QROWS, HD), BF16),
            pltpu.VMEM((8, 8, HD), F32),
            pltpu.VMEM((3, HEADS, QROWS, HD), F32),
            pltpu.VMEM((N_CTX, 2, 16, HD), F32),
            pltpu.VMEM((N_CTX, 2, 16, HD), F32),
            pltpu.VMEM((N_CTX, 16, HD), BF16),
            dma((UNITS,)),
            dma,
            dma,
            dma((2,)),
            dma((8,)),
            dma((UNITS, 4)),
            dma((UNITS,)),
            dma((8,)),
            dma((8,)),
            dma((9,)),
            dma((9,)),
            dma((7,)),
            dma((7,)),
            dma((8,)),
        ],
        compiler_params=pltpu.CompilerParams(
            collective_id=0, has_side_effects=True, vmem_limit_bytes=58 * 1024 * 1024
        ),
        cost_estimate=pl.CostEstimate(
            flops=12_000_000_000, bytes_accessed=30_000_000, transcendentals=600_000
        ),
    )(
        info,
        decode_rows,
        drow,
        prefill_hidden_states,
        query_matrix,
        key_matrix,
        value_matrix,
        adapter_down_maps,
        key_adapter_up_maps,
        value_adapter_up_maps,
        request_key_cache,
        request_value_cache,
    )
    page_shape = (SLOT_ROWS // BLK, BLK, HEADS * HD)
    attended = attended.reshape(HEADS, RPG, STEPS, H // KVH, HD)
    attended = jnp.transpose(attended, (2, 1, 0, 3, 4)).reshape(STEPS, RPG, HEADS * 8 * HD)
    return (page_keys.reshape(page_shape), page_values.reshape(page_shape), attended)


def solution(mesh):
    return jax.shard_map(
        on_device,
        mesh=mesh,
        in_specs=(
            P(("section", "ctx"), None),
            P(None, "section", "ctx"),
            P("ctx", "tp"),
            P("ctx", "tp"),
            P("ctx", "tp"),
            P("ctx", "tp"),
            P(None, "tp"),
            P(None, "tp"),
            P("section", "ctx", "tp"),
            P("section", "ctx", "tp"),
            P(),
            P(),
            P("section"),
            P(("section", "ctx"), None),
        ),
        out_specs=(
            P(("section", "ctx"), None, "tp"),
            P(("section", "ctx"), None, "tp"),
            P(None, "section", "tp"),
        ),
        check_vma=False,
    )
```

```python
import functools

import jax
import jax.numpy as jnp
from jax import lax
from jax.experimental import pallas as pl
from jax.experimental.pallas import tpu as pltpu
from jax.sharding import PartitionSpec as P

H = 64
KVH = 8
HD = 128
ADAPTER_RANK = 16
BLK = 32
STEPS = 2

ADAPTER_SCALE = 0.5
CUT = 128
NEG_FLOOR = -1e30
INV_ROOT = HD ** (-0.5)

SIDE = 4
N_CTX = 16
SHARD = 512
UNITS = 5
BLOCKS = 8
HEADS = 4
ROWS = 512
SLOT_ROWS = 1024
PAIR = 64
RPG = 4
CTX_DEV = 1024
QROWS = 64
DBLOCKS = 48
PER = 3

MESH = pl.DeviceIdType.MESH
F32 = jnp.float32
BF16 = jnp.bfloat16


def wait_bytes(ref, sem):
    pltpu.make_async_copy(ref, ref, sem).wait()


def nt_dot(a, b):
    return lax.dot_general(a, b, (((1,), (1,)), ((), ())), preferred_element_type=F32)


def layer_kernel(
    adapter_of,
    target_of,
    length_of,
    owner_of,
    xd,
    x_hbm,
    wq_hbm,
    wk_hbm,
    wv_hbm,
    wd_hbm,
    uk_hbm,
    uv_hbm,
    kc_hbm,
    vc_hbm,
    pk_out,
    pv_out,
    att_out,
    x_v,
    w_v,
    wq_v,
    wd_v,
    dt_v,
    hid,
    up_v,
    kc_v,
    vc_v,
    acc,
    dn,
    row,
    raw,
    place_m,
    drow,
    drow_r,
    sendb,
    pages,
    part,
    rsr,
    ag,
    qp,
    tkv,
    pst,
    mgs,
    mgr,
    att,
    w_load,
    q_load,
    x_load,
    c_load,
    u_load,
    g_recv,
    g_send,
    x_recv,
    x_send,
    f_recv,
    f_send,
    row_send,
    row_recv,
    a_send,
    a_recv,
    small_send,
    small_recv,
    out_sem,
):
    s = lax.axis_index("section")
    c = lax.axis_index("ctx")
    t = lax.axis_index("tp")
    n_sec = lax.axis_size("section")
    y = c // SIDE
    z = lax.rem(c, SIDE)

    def chip(dy, dz):
        return lax.rem(y + dy + SIDE, SIDE) * SIDE + lax.rem(z + dz + SIDE, SIDE)

    def here(ctx):
        return (s, ctx, t)

    right = (lax.rem(s + 1, n_sec), c, t)
    left = (lax.rem(s + n_sec - 1, n_sec), c, t)
    partner = (s, c, 1 - t)
    s_left = lax.rem(s + n_sec - 1, n_sec)
    s_right = lax.rem(s + 1, n_sec)
    s_far = lax.rem(s + 2, n_sec)

    barrier = pltpu.get_barrier_semaphore()

    @pl.loop(1, N_CTX)
    def _(j):
        pl.semaphore_signal(
            barrier, inc=1, device_id=here(lax.rem(c + j, N_CTX)), device_id_type=MESH
        )

    for peer in (left, right, partner):
        pl.semaphore_signal(barrier, inc=1, device_id=peer, device_id_type=MESH)

    mine = pl.ds(pl.multiple_of(c * SHARD, SHARD), SHARD)
    shard_loads = []
    for n, hbm in enumerate([wk_hbm] * HEADS + [wv_hbm] * HEADS):
        cols = pl.ds(n % HEADS * HD, HD)
        shard_loads.append(
            pltpu.make_async_copy(hbm.at[:, cols], w_v.at[n, mine], w_load.at[n])
        )
    down_load = pltpu.make_async_copy(wd_hbm, wd_v, w_load.at[8])
    down_load.start()
    for load in shard_loads:
        load.start()
    q_copy = pltpu.make_async_copy(wq_hbm, wq_v, q_load)
    q_copy.start()
    ups = []
    for h in range(HEADS):
        cols = pl.ds(h * HD, HD)
        ups.append(pltpu.make_async_copy(uk_hbm.at[:, cols], up_v.at[h], u_load.at[h]))
        ups.append(pltpu.make_async_copy(uv_hbm.at[:, cols], up_v.at[4 + h], u_load.at[4 + h]))
    for load in ups:
        load.start()
    x_copy = pltpu.make_async_copy(x_hbm, x_v, x_load)
    x_copy.start()
    k_copy = pltpu.make_async_copy(kc_hbm, kc_v, c_load.at[0])
    v_copy = pltpu.make_async_copy(vc_hbm, vc_v, c_load.at[1])
    k_copy.start()
    v_copy.start()

    pl.semaphore_wait(barrier, N_CTX + 2)

    def send(src, dst, send_sem, recv_sem, device):
        pltpu.make_async_remote_copy(
            src_ref=src,
            dst_ref=dst,
            send_sem=send_sem,
            recv_sem=recv_sem,
            device_id=device,
            device_id_type=MESH,
        ).start()

    for load in shard_loads:
        load.wait()

    def pass_on(u, stage, shard, first, count, ctx):
        rows = pl.ds(pl.multiple_of(shard * SHARD + first, 128), count)
        piece = w_v.at[block_of(u), rows]
        send(piece, piece, g_send.at[u], g_recv.at[u, stage], here(ctx))

    def block_of(u):
        return jnp.where(u == 0, HEADS + s, u - 1)

    def arrived(u, stage, shards):
        wait_bytes(w_v.at[block_of(u), pl.ds(0, shards * SHARD)], g_recv.at[u, stage])

    yp, ym, zp, zm = chip(1, 0), chip(-1, 0), chip(0, 1), chip(0, -1)
    A, B, A0, A1, B0, B1, ZERO = (
        (0, 256),
        (256, 256),
        (128, 128),
        (0, 128),
        (256, 128),
        (384, 128),
        (128, 256),
    )

    def stage1(u):
        for ctx in (yp, zp, ym, zm):
            pass_on(u, 0, c, 0, SHARD, ctx)

    def stage2(u):
        arrived(u, 0, 4)
        pass_on(u, 1, ym, *ZERO, yp)
        pass_on(u, 1, yp, *A1, ym)
        pass_on(u, 1, yp, *B1, ym)
        pass_on(u, 1, zm, *ZERO, zp)
        pass_on(u, 1, zp, *A1, zm)
        pass_on(u, 1, zp, *B1, zm)
        for shard in (ym, yp):
            for ctx in (zp, zm):
                pass_on(u, 1, shard, *A, ctx)
        for shard in (zm, zp):
            for ctx in (yp, ym):
                pass_on(u, 1, shard, *B, ctx)

    def stage3(u):
        arrived(u, 1, 6)
        yy, zz = chip(2, 0), chip(0, 2)
        for ctx in (zp, zm):
            pass_on(u, 2, yy, *A, ctx)
        for ctx in (yp, ym):
            pass_on(u, 2, zz, *B, ctx)
        for d in (-1, 1):
            pass_on(u, 2, chip(d, -1), *A0, zp)
            pass_on(u, 2, chip(d, 1), *A1, zm)
            pass_on(u, 2, chip(-1, d), *B0, yp)
            pass_on(u, 2, chip(1, d), *B1, ym)

    def stage4(u):
        arrived(u, 2, 4)
        pass_on(u, 3, chip(2, -1), *A0, zp)
        pass_on(u, 3, chip(2, 1), *A1, zm)
        pass_on(u, 3, chip(-1, 2), *B0, yp)
        pass_on(u, 3, chip(1, 2), *B1, ym)

    GROUPS = (
        (ym, yp, zm, zp),
        (chip(-1, -1), chip(-1, 1), chip(1, -1), chip(1, 1), chip(2, 0), chip(0, 2)),
        (chip(-1, 2), chip(1, 2), chip(2, -1), chip(2, 1)),
        (chip(2, 2),),
    )

    def across(group):
        for shard in GROUPS[group]:
            rows = pl.ds(pl.multiple_of(shard * SHARD, SHARD), SHARD)
            piece = w_v.at[HEADS + s, rows]
            send(piece, piece, x_send.at[0], x_recv.at[0, group], right)
            send(piece, piece, x_send.at[1], x_recv.at[1, group], left)

    def across_again(group):
        count = len(GROUPS[group])
        wait_bytes(w_v.at[HEADS + s_left, pl.ds(0, count * SHARD)], x_recv.at[0, group])
        wait_bytes(w_v.at[HEADS + s_right, pl.ds(0, count * SHARD)], x_recv.at[1, group])
        for shard in GROUPS[group]:
            rows = pl.ds(pl.multiple_of(shard * SHARD, SHARD), CUT)
            piece = w_v.at[HEADS + s_left, rows]
            send(piece, piece, f_send.at[0], f_recv.at[0], right)
            rows = pl.ds(pl.multiple_of(shard * SHARD + CUT, 128), SHARD - CUT)
            piece = w_v.at[HEADS + s_right, rows]
            send(piece, piece, f_send.at[1], f_recv.at[1], left)

    span_request = target_of[s]
    span_adapter = jnp.int32(0)
    for b in range(N_CTX):
        span_adapter = jnp.where(span_request == b, adapter_of[b], span_adapter)
    pick_row = lax.broadcasted_iota(jnp.int32, (ADAPTER_RANK, HD), 0)
    pick_col = lax.broadcasted_iota(jnp.int32, (ADAPTER_RANK, HD), 1)
    pick = jnp.where(pick_col == span_adapter * ADAPTER_RANK + pick_row, 1.0, 0.0).astype(BF16)

    def down_rows():
        down_load.wait()
        own = pl.ds(pl.multiple_of(c * SHARD, SHARD), SHARD)
        dt_v[:, own] = nt_dot(pick, wd_v[...]).astype(BF16)

        @pl.loop(1, N_CTX)
        def _(j):
            piece = dt_v.at[:, own]
            ctx = lax.rem(c + j, N_CTX)
            send(piece, piece, small_send.at[7], small_recv.at[7], here(ctx))

    def project_down():
        x_copy.wait()
        wait_bytes(dt_v.at[:, pl.ds(0, (N_CTX - 1) * SHARD)], small_recv.at[7])
        acc[...] = jnp.zeros_like(acc)

        @pl.loop(0, 8)
        def _(i):
            part_k = pl.ds(pl.multiple_of(i * 1024, 1024), 1024)
            acc[:, 0:ADAPTER_RANK] += nt_dot(x_v[:, part_k], dt_v[:, part_k])

        down = acc[:, 0:ADAPTER_RANK].astype(BF16)
        dn[t] = jnp.dot(down, pick, preferred_element_type=F32).astype(BF16)
        send(dn.at[t], dn.at[t], small_send.at[1], small_recv.at[1], partner)

    def nth(p, sec):
        far = jnp.where(p == 5, sec + n_sec - 1, jnp.where(p == 6, sec + 1, sec + 2))
        value = HEADS + jnp.where(p == 0, sec, lax.rem(far, n_sec))
        return jnp.where((p >= 1) & (p <= HEADS), p - 1, value)

    def project(p):
        n = nth(p, s)

        @pl.when((p >= 1) & (p < UNITS))
        def _():
            arrived(p, 3, 1)

        @pl.when(p == 0)
        def _():
            wait_bytes(dn.at[0], small_recv.at[1])

        @pl.when(p == BLOCKS - 1)
        def _():
            wait_bytes(w_v.at[n, pl.ds(0, 15 * CUT)], f_recv.at[0])
            wait_bytes(w_v.at[n, pl.ds(0, 15 * (SHARD - CUT))], f_recv.at[1])

        acc[...] = jnp.dot(dn[n // HEADS], up_v[n], preferred_element_type=F32) * ADAPTER_SCALE

        @pl.loop(0, 8)
        def _(i):
            part_k = pl.ds(pl.multiple_of(i * 1024, 1024), 1024)
            acc[...] += jnp.dot(x_v[:, part_k], w_v[n, part_k], preferred_element_type=F32)

        row[n] = acc[...].astype(BF16)
        send(row.at[n], raw.at[n], row_send.at[n], row_recv.at[n], right)

    def exchange(n):
        @pl.loop(1, N_CTX)
        def _(j):
            ctx = lax.rem(c + j, N_CTX)
            theirs = pl.ds(pl.multiple_of(ctx * PAIR, PAIR), PAIR)
            ours = pl.ds(pl.multiple_of(c * PAIR, PAIR), PAIR)
            send(
                sendb.at[n, theirs], pages.at[n, ours], a_send.at[n], a_recv.at[n], here(ctx)
            )

        ours = pl.ds(pl.multiple_of(c * PAIR, PAIR), PAIR)
        pages[n, ours] = sendb[n, ours]

    def place(n):
        wait_bytes(raw.at[n], row_recv.at[n])

        @pl.loop(0, 4)
        def _(i):
            some = pl.ds(pl.multiple_of(i * 256, 256), 256)
            sendb[n, some] = jnp.dot(
                place_m[some], raw[n], preferred_element_type=F32
            ).astype(BF16)

        exchange(n)

    def page_rows():
        owners = [owner_of[i, 0] for i in range(16)]
        lane = lax.broadcasted_iota(jnp.int32, (8, ROWS), 1)
        rows = jnp.zeros((8, ROWS), jnp.int32)
        for i in range(16):
            slot = owners[i] * 2
            for j in range(i):
                slot = slot + jnp.where(owners[j] == owners[i], 1, 0)
            rows = jnp.where(lane // BLK == i, slot * BLK + lax.rem(lane, BLK), rows)
        drow[...] = rows
        send(drow, drow_r, small_send.at[0], small_recv.at[0], right)

    def page_flags():
        wait_bytes(drow_r, small_recv.at[0])

        @pl.loop(0, 4)
        def _(i):
            some = pl.ds(pl.multiple_of(i * 256, 256), 256)
            slot_row = lax.broadcasted_iota(jnp.int32, (256, ROWS), 0) + i * 256
            hit = slot_row == drow_r[0:1]
            place_m[some] = jnp.where(hit, 1.0, 0.0).astype(BF16)
            flag = jnp.max(jnp.where(hit, 1.0, 0.0), axis=1, keepdims=True)
            sendb[8, some] = jnp.broadcast_to(flag, (256, HD)).astype(BF16)

        exchange(8)

    def landed(n):
        wait_bytes(pages.at[n, pl.ds(0, SLOT_ROWS - PAIR)], a_recv.at[n])

    def write_out(n):
        cols = pl.ds(pl.multiple_of(lax.rem(n, HEADS) * HD, HD), HD)

        @pl.when(n < HEADS)
        def _():
            pltpu.make_async_copy(pages.at[n], pk_out.at[:, cols], out_sem.at[n]).start()

        @pl.when(n >= HEADS)
        def _():
            pltpu.make_async_copy(pages.at[n], pv_out.at[:, cols], out_sem.at[n]).start()

    def decode_project():
        q_copy.wait()

        def blocks(product, first):
            for i in range(product.shape[1] // HD):
                part[first + i] = product[:, i * HD : (i + 1) * HD]

        hid[0:4] = xd[0].astype(F32)
        hid[4:8] = xd[1].astype(F32)
        hidden = hid[...].astype(BF16)
        part[DBLOCKS - 6 :] = jnp.zeros((6, 8, HD), F32)
        for i in range(8):
            piece = wq_v[:, i * 512 : (i + 1) * 512]
            blocks(jnp.dot(hidden, piece, preferred_element_type=F32), 4 * i)
        for n in range(BLOCKS):
            blocks(jnp.dot(hidden, w_v[n, mine], preferred_element_type=F32), 32 + n)
        part[40 + t] = jnp.dot(hidden, wd_v[...], preferred_element_type=F32)
        send(part.at[40 + t], part.at[40 + t], small_send.at[2], small_recv.at[2], partner)
        wait_bytes(part.at[0], small_recv.at[2])

        @pl.loop(1, N_CTX)
        def _(j):
            ctx = lax.rem(c + j, N_CTX)
            send(
                part.at[pl.ds(ctx * PER, PER)],
                rsr.at[c],
                small_send.at[3],
                small_recv.at[3],
                here(ctx),
            )

        rsr[c] = part[pl.ds(c * PER, PER)]

    def decode_sum():
        wait_bytes(rsr.at[pl.ds(0, N_CTX - 1)], small_recv.at[3])
        ag[pl.ds(c * PER, PER)] = jnp.sum(rsr[...], axis=0)

        @pl.loop(1, N_CTX)
        def _(j):
            ctx = lax.rem(c + j, N_CTX)
            piece = ag.at[pl.ds(c * PER, PER)]
            send(piece, piece, small_send.at[4], small_recv.at[4], here(ctx))

    def decode_rows():
        wait_bytes(ag.at[pl.ds(0, (N_CTX - 1) * PER)], small_recv.at[4])
        for load in ups:
            load.wait()
        to = lax.broadcasted_iota(jnp.int32, (QROWS, QROWS), 0)
        at = lax.broadcasted_iota(jnp.int32, (QROWS, QROWS), 1)
        source = lax.rem(to, 8) * 8 + lax.rem(to // 8, STEPS) * RPG + to // 16
        perm = jnp.where(at == source, 1.0, 0.0).astype(BF16)
        for k in range(HEADS):
            queries = ag[8 * k : 8 * k + 8].reshape(QROWS, HD).astype(BF16)
            qp[k] = jnp.dot(perm, queries, preferred_element_type=F32).astype(BF16)
        lane = lax.broadcasted_iota(jnp.int32, (8, HD), 1) // ADAPTER_RANK
        who = lax.rem(lax.broadcasted_iota(jnp.int32, (8, HD), 0), RPG)
        adapter = jnp.zeros((8, HD), jnp.int32)
        for b in range(RPG):
            adapter = jnp.where(who == b, adapter_of[s * RPG + b], adapter)
        for kind in range(2):
            down = ag[40 + kind].astype(BF16).astype(F32)
            picked = jnp.where(lane == adapter, down, 0.0).astype(BF16)
            for k in range(HEADS):
                n = 4 * kind + k
                delta = jnp.dot(picked, up_v[n], preferred_element_type=F32)
                tkv[n] = (ag[32 + n] + ADAPTER_SCALE * delta).astype(BF16).astype(F32)
        which = lax.broadcasted_iota(jnp.int32, (QROWS, 8), 0)
        other = lax.broadcasted_iota(jnp.int32, (QROWS, 8), 1)
        tok_live = (
            (lax.rem(other, RPG) == which // 16)
            & (other // RPG <= lax.rem(which // 8, STEPS))
            & (c == 0)
        )
        for k in range(HEADS):
            tok = nt_dot(qp[k], tkv[k].astype(BF16)) * INV_ROOT
            tok_max = jnp.max(jnp.where(tok_live, tok, NEG_FLOOR), axis=1, keepdims=True)
            tok_w = jnp.where(tok_live, jnp.exp(tok - tok_max), 0.0)
            tok_out = jnp.zeros((QROWS, HD), F32)
            for i in range(8):
                tok_out = tok_out + tok_w[:, i : i + 1] * tkv[4 + k, i : i + 1]
            pst[0, k] = jnp.broadcast_to(tok_max, (QROWS, HD))
            pst[1, k] = jnp.broadcast_to(jnp.sum(tok_w, axis=1, keepdims=True), (QROWS, HD))
            pst[2, k] = tok_out

    def merge(k, rows, block_max, total, out):
        old = pst[0, k, rows]
        top = jnp.maximum(old, block_max)
        old_scale, scale = jnp.exp(old - top), jnp.exp(block_max - top)
        pst[0, k, rows] = top
        pst[1, k, rows] = old_scale * pst[1, k, rows] + scale * total
        pst[2, k, rows] = old_scale * pst[2, k, rows] + scale * out

    def cache_block(b):
        @pl.when(b == 0)
        def _():
            k_copy.wait()
            v_copy.wait()

        left_len = length_of[b] - c * CTX_DEV
        live = lax.broadcasted_iota(jnp.int32, (16, CTX_DEV), 1) < left_len
        rows = pl.ds(pl.multiple_of(b * 16, 16), 16)
        for k in range(HEADS):
            cols = slice(k * HD, (k + 1) * HD)
            scores = nt_dot(qp[k, rows], kc_v[b, :, cols]) * INV_ROOT
            block_max = jnp.max(jnp.where(live, scores, NEG_FLOOR), axis=1, keepdims=True)
            weights = jnp.where(live, jnp.exp(scores - block_max), 0.0).astype(BF16)
            total = jnp.sum(weights.astype(F32), axis=1, keepdims=True)
            out = jnp.dot(weights, vc_v[b, :, cols], preferred_element_type=F32)
            merge(k, rows, block_max, total, out)

    stage1(0)
    stage1(1)
    down_rows()
    page_rows()

    @pl.loop(0, BLOCKS + 7)
    def _(i):
        @pl.when((i >= 1) & (i < UNITS - 1))
        def _():
            stage1(i + 1)

        @pl.when((i >= 3) & (i < UNITS + 3))
        def _():
            stage4(i - 3)

        @pl.when((i >= 2) & (i < UNITS + 2))
        def _():
            stage3(i - 2)

        @pl.when((i >= 1) & (i < UNITS + 1))
        def _():
            stage2(i - 1)

        @pl.when(i == 1)
        def _():
            across(0)
            decode_project()

        @pl.when(i == 2)
        def _():
            across(1)
            decode_sum()
            page_flags()

        @pl.when(i == 3)
        def _():
            across(2)
            across_again(0)
            project_down()
            decode_rows()

        @pl.when(i == 4)
        def _():
            arrived(0, 3, 1)
            across(3)

        @pl.when(i == 5)
        def _():
            across_again(1)

        @pl.when(i == 6)
        def _():
            across_again(2)

        @pl.when(i == 7)
        def _():
            across_again(3)

        @pl.when((i >= 4) & (i < 4 + RPG))
        def _():
            cache_block(i - 4)

        @pl.when((i >= 4) & (i < BLOCKS + 4))
        def _():
            project(i - 4)

        @pl.when((i >= 6) & (i < BLOCKS + 6))
        def _():
            place(nth(i - 6, s_left))

        @pl.when(i >= 7)
        def _():
            landed(nth(i - 7, s_left))
            write_out(nth(i - 7, s_left))

    landed(8)

    page_request = target_of[s_left] - s * RPG
    live = nt_dot(jnp.ones((16, HD), BF16), pages[8]) > 0.5
    for k in range(HEADS):
        query = jnp.zeros((16, HD), F32)
        for b in range(RPG):
            query = jnp.where(page_request == b, qp[k, b * 16 : b * 16 + 16].astype(F32), query)
        scores = nt_dot(query.astype(BF16), pages[k]) * INV_ROOT
        p_max = jnp.max(jnp.where(live, scores, NEG_FLOOR), axis=1, keepdims=True)
        weights = jnp.where(live, jnp.exp(scores - p_max), 0.0).astype(BF16)
        p_total = jnp.sum(weights.astype(F32), axis=1, keepdims=True)
        p_out = jnp.dot(weights, pages[4 + k], preferred_element_type=F32)
        for b in range(RPG):
            rows = slice(b * 16, b * 16 + 16)
            wanted = page_request == b
            merge(
                k,
                rows,
                jnp.where(wanted, p_max, NEG_FLOOR),
                jnp.where(wanted, p_total, 0.0),
                jnp.where(wanted, p_out, 0.0),
            )
            lane = lax.broadcasted_iota(jnp.int32, (16, HD), 1)
            mgs[k * 4 + b, 0] = pst[2, k, rows]
            mgs[k * 4 + b, 1] = jnp.where(lane < 64, pst[0, k, rows], pst[1, k, rows])

    @pl.loop(1, N_CTX)
    def _(j):
        ctx = lax.rem(c + j, N_CTX)
        send(mgs.at[ctx], mgr.at[c], small_send.at[5], small_recv.at[5], here(ctx))

    mgr[c] = mgs[c]
    wait_bytes(mgr.at[pl.ds(0, N_CTX - 1)], small_recv.at[5])
    stats = mgr[:, 1]
    tops, totals = stats[:, :, 0:1], stats[:, :, 64:65]
    scale = jnp.exp(tops - jnp.max(tops, axis=0, keepdims=True))
    numer = jnp.sum(scale * mgr[:, 0], axis=0)
    denom = jnp.sum(scale * totals, axis=0)
    att[c] = (numer / denom).astype(BF16)

    @pl.loop(1, N_CTX)
    def _(j):
        ctx = lax.rem(c + j, N_CTX)
        send(att.at[c], att.at[c], small_send.at[6], small_recv.at[6], here(ctx))

    wait_bytes(att.at[pl.ds(0, N_CTX - 1)], small_recv.at[6])
    att_out[...] = att[...]

    @pl.loop(0, UNITS)
    def _(u):
        wait_bytes(w_v.at[u, pl.ds(0, 15 * SHARD)], g_send.at[u])

    @pl.loop(0, BLOCKS + 1)
    def _(u):
        wait_bytes(sendb.at[u, pl.ds(0, SLOT_ROWS - PAIR)], a_send.at[u])

    for d, count in ((0, CUT), (1, SHARD - CUT)):
        wait_bytes(w_v.at[0, pl.ds(0, 15 * SHARD)], x_send.at[d])
        wait_bytes(w_v.at[0, pl.ds(0, 15 * count)], f_send.at[d])

    @pl.loop(0, 2 * HEADS)
    def _(n):
        wait_bytes(row.at[n], row_send.at[n])
        wait_bytes(pages.at[n], out_sem.at[n])

    wait_bytes(drow, small_send.at[0])
    wait_bytes(dn.at[0], small_send.at[1])
    wait_bytes(part.at[0], small_send.at[2])
    wait_bytes(rsr.at[pl.ds(0, N_CTX - 1)], small_send.at[3])
    wait_bytes(ag.at[pl.ds(0, (N_CTX - 1) * PER)], small_send.at[4])
    wait_bytes(mgr.at[pl.ds(0, N_CTX - 1)], small_send.at[5])
    wait_bytes(att.at[pl.ds(0, N_CTX - 1)], small_send.at[6])
    wait_bytes(dt_v.at[:, pl.ds(0, (N_CTX - 1) * SHARD)], small_send.at[7])


def finish_kernel(pk, pv, att, pk_out, pv_out, att_out, rows, sem):
    copies = [
        pltpu.make_async_copy(pk, pk_out, sem.at[0]),
        pltpu.make_async_copy(pv, pv_out, sem.at[1]),
    ]
    for copy in copies:
        copy.start()
    for k in range(HEADS):
        for b in range(RPG):
            block = att[k * RPG + b].astype(F32)
            for step in range(STEPS):
                for g in range(8):
                    cols = slice((k * 8 + g) * HD, (k * 8 + g + 1) * HD)
                    at = step * 8 + g
                    rows[step, b : b + 1, cols] = block[at : at + 1]
    att_out[...] = rows[...].astype(BF16)
    for copy in copies:
        copy.wait()


def on_device(
    prefill_hidden_states,
    decode_hidden_states,
    query_matrix,
    key_matrix,
    value_matrix,
    adapter_down_maps,
    key_adapter_up_maps,
    value_adapter_up_maps,
    request_key_cache,
    request_value_cache,
    request_adapter_index,
    prefill_request_target,
    request_context_length,
    page_owner_index,
):
    hbm = pl.BlockSpec(memory_space=pl.ANY)
    vmem = pl.BlockSpec(memory_space=pltpu.VMEM)
    smem = pl.BlockSpec(memory_space=pltpu.SMEM)
    dma = pltpu.SemaphoreType.DMA
    page_keys, page_values, attended = pl.pallas_call(
        layer_kernel,
        out_shape=(
            jax.ShapeDtypeStruct((SLOT_ROWS, HEADS * HD), BF16),
            jax.ShapeDtypeStruct((SLOT_ROWS, HEADS * HD), BF16),
            jax.ShapeDtypeStruct((N_CTX, 16, HD), BF16),
        ),
        in_specs=[smem] * 4 + [vmem] + [hbm] * 9,
        out_specs=(hbm, hbm, vmem),
        scratch_shapes=[
            pltpu.VMEM((ROWS, 8192), BF16),
            pltpu.VMEM((BLOCKS, 8192, HD), BF16),
            pltpu.VMEM((SHARD, 4096), BF16),
            pltpu.VMEM((SHARD, HD), BF16),
            pltpu.VMEM((ADAPTER_RANK, 8192), BF16),
            pltpu.VMEM((8, SHARD), F32),
            pltpu.VMEM((8, HD, HD), BF16),
            pltpu.VMEM((RPG, CTX_DEV, HEADS * HD), BF16),
            pltpu.VMEM((RPG, CTX_DEV, HEADS * HD), BF16),
            pltpu.VMEM((ROWS, HD), F32),
            pltpu.VMEM((2, ROWS, HD), BF16),
            pltpu.VMEM((8, ROWS, HD), BF16),
            pltpu.VMEM((8, ROWS, HD), BF16),
            pltpu.VMEM((SLOT_ROWS, ROWS), BF16),
            pltpu.VMEM((8, ROWS), jnp.int32),
            pltpu.VMEM((8, ROWS), jnp.int32),
            pltpu.VMEM((9, SLOT_ROWS, HD), BF16),
            pltpu.VMEM((9, SLOT_ROWS, HD), BF16),
            pltpu.VMEM((DBLOCKS, 8, HD), F32),
            pltpu.VMEM((N_CTX, PER, 8, HD), F32),
            pltpu.VMEM((DBLOCKS, 8, HD), F32),
            pltpu.VMEM((HEADS, QROWS, HD), BF16),
            pltpu.VMEM((8, 8, HD), F32),
            pltpu.VMEM((3, HEADS, QROWS, HD), F32),
            pltpu.VMEM((N_CTX, 2, 16, HD), F32),
            pltpu.VMEM((N_CTX, 2, 16, HD), F32),
            pltpu.VMEM((N_CTX, 16, HD), BF16),
            dma((9,)),
            dma,
            dma,
            dma((2,)),
            dma((8,)),
            dma((UNITS, 4)),
            dma((UNITS,)),
            dma((2, 4)),
            dma((2,)),
            dma((2,)),
            dma((2,)),
            dma((8,)),
            dma((8,)),
            dma((9,)),
            dma((9,)),
            dma((8,)),
            dma((8,)),
            dma((8,)),
        ],
        compiler_params=pltpu.CompilerParams(
            collective_id=0, has_side_effects=True, vmem_limit_bytes=58 * 1024 * 1024
        ),
        cost_estimate=pl.CostEstimate(
            flops=12_000_000_000, bytes_accessed=30_000_000, transcendentals=600_000
        ),
    )(
        request_adapter_index,
        prefill_request_target,
        request_context_length,
        page_owner_index,
        decode_hidden_states,
        prefill_hidden_states,
        query_matrix,
        key_matrix,
        value_matrix,
        adapter_down_maps,
        key_adapter_up_maps,
        value_adapter_up_maps,
        request_key_cache,
        request_value_cache,
    )
    page_shape = (SLOT_ROWS // BLK, BLK, HEADS * HD)
    page_keys, page_values, attended = pl.pallas_call(
        finish_kernel,
        out_shape=(
            jax.ShapeDtypeStruct((SLOT_ROWS, HEADS * HD), BF16),
            jax.ShapeDtypeStruct((SLOT_ROWS, HEADS * HD), BF16),
            jax.ShapeDtypeStruct((STEPS, RPG, HEADS * 8 * HD), BF16),
        ),
        in_specs=[hbm, hbm, vmem],
        out_specs=(hbm, hbm, vmem),
        scratch_shapes=[pltpu.VMEM((STEPS, RPG, HEADS * 8 * HD), F32), dma((2,))],
        compiler_params=pltpu.CompilerParams(vmem_limit_bytes=4 * 1024 * 1024),
    )(page_keys, page_values, attended)
    return (page_keys.reshape(page_shape), page_values.reshape(page_shape), attended)


def solution(mesh):
    return jax.shard_map(
        on_device,
        mesh=mesh,
        in_specs=(
            P(("section", "ctx"), None),
            P(None, "section", "ctx"),
            P("ctx", "tp"),
            P("ctx", "tp"),
            P("ctx", "tp"),
            P("ctx", "tp"),
            P(None, "tp"),
            P(None, "tp"),
            P("section", "ctx", "tp"),
            P("section", "ctx", "tp"),
            P(),
            P(),
            P("section"),
            P(("section", "ctx"), None),
        ),
        out_specs=(
            P(("section", "ctx"), None, "tp"),
            P(("section", "ctx"), None, "tp"),
            P(None, "section", "tp"),
        ),
        check_vma=False,
    )
```

```python
import functools

import jax
import jax.numpy as jnp
from jax import lax
from jax.experimental import pallas as pl
from jax.experimental.pallas import tpu as pltpu
from jax.sharding import PartitionSpec as P

H = 64
KVH = 8
HD = 128
ADAPTER_RANK = 16
BLK = 32
STEPS = 2

ADAPTER_SCALE = 0.5
CUT = 128
NEG_FLOOR = -1e30
INV_ROOT = HD ** (-0.5)

SIDE = 4
N_CTX = 16
SHARD = 512
UNITS = 5
HALVES = 2 * UNITS
HALF = 256
BLOCKS = 8
HEADS = 4
ROWS = 512
SLOT_ROWS = 1024
PAIR = 64
RPG = 4
CTX_DEV = 1024
QROWS = 64
DBLOCKS = 48
PER = 3

PROJECT_AT = (9, 11, 12, 13, 14, 15, 17, 18)
PLACE_AT = tuple(at + 2 for at in PROJECT_AT)
LAND_AT = tuple(at + 4 for at in PROJECT_AT)
CACHE_AT = (10, 14, 16, 18)
ADD_LAG = (3, 5, 7, 8)
ACROSS_AT = (9, 11, 12, 12)
FAR_AT = (15, 17, 18, 18)
LAST = LAND_AT[-1]

MESH = pl.DeviceIdType.MESH
F32 = jnp.float32
BF16 = jnp.bfloat16


def wait_bytes(ref, sem):
    pltpu.make_async_copy(ref, ref, sem).wait()


def turn(i, slots):
    here, which = False, -1
    for at in slots:
        here = here | (i == at)
        which = which + jnp.where(i >= at, 1, 0)
    return here, which


def nt_dot(a, b):
    return lax.dot_general(a, b, (((1,), (1,)), ((), ())), preferred_element_type=F32)


def layer_kernel(
    adapter_of,
    target_of,
    length_of,
    owner_of,
    xd,
    x_hbm,
    wq_hbm,
    wk_hbm,
    wv_hbm,
    wd_hbm,
    uk_hbm,
    uv_hbm,
    kc_hbm,
    vc_hbm,
    pk_out,
    pv_out,
    att_out,
    x_v,
    w_v,
    wq_v,
    wd_v,
    dt_v,
    hid,
    up_v,
    kc_v,
    vc_v,
    acc,
    accs,
    dn,
    row,
    raw,
    place_m,
    drow,
    drow_r,
    sendb,
    pages,
    part,
    rsr,
    ag,
    qp,
    tkv,
    pst,
    pgw,
    pgs,
    mgs,
    mgr,
    att,
    w_load,
    q_load,
    x_load,
    c_load,
    u_load,
    g_recv,
    g_send,
    x_recv,
    x_send,
    f_recv,
    f_send,
    row_send,
    row_recv,
    a_send,
    a_recv,
    small_send,
    small_recv,
    out_sem,
):
    s = lax.axis_index("section")
    c = lax.axis_index("ctx")
    t = lax.axis_index("tp")
    n_sec = lax.axis_size("section")
    y = c // SIDE
    z = lax.rem(c, SIDE)

    def chip(dy, dz):
        return lax.rem(y + dy + SIDE, SIDE) * SIDE + lax.rem(z + dz + SIDE, SIDE)

    def here(ctx):
        return (s, ctx, t)

    right = (lax.rem(s + 1, n_sec), c, t)
    left = (lax.rem(s + n_sec - 1, n_sec), c, t)
    partner = (s, c, 1 - t)
    s_left = lax.rem(s + n_sec - 1, n_sec)
    s_right = lax.rem(s + 1, n_sec)
    s_far = lax.rem(s + 2, n_sec)

    barrier = pltpu.get_barrier_semaphore()

    @pl.loop(1, N_CTX)
    def _(j):
        pl.semaphore_signal(
            barrier, inc=1, device_id=here(lax.rem(c + j, N_CTX)), device_id_type=MESH
        )

    for peer in (left, right, partner):
        pl.semaphore_signal(barrier, inc=1, device_id=peer, device_id_type=MESH)

    mine = pl.ds(pl.multiple_of(c * SHARD, SHARD), SHARD)
    shard_loads = []
    for n, hbm in enumerate([wk_hbm] * HEADS + [wv_hbm] * HEADS):
        cols = pl.ds(n % HEADS * HD, HD)
        shard_loads.append(
            pltpu.make_async_copy(hbm.at[:, cols], w_v.at[n, mine], w_load.at[n])
        )
    down_load = pltpu.make_async_copy(wd_hbm, wd_v, w_load.at[8])
    down_load.start()
    for load in shard_loads:
        load.start()
    q_copy = pltpu.make_async_copy(wq_hbm, wq_v, q_load)
    q_copy.start()
    ups = []
    for h in range(HEADS):
        cols = pl.ds(h * HD, HD)
        ups.append(pltpu.make_async_copy(uk_hbm.at[:, cols], up_v.at[h], u_load.at[h]))
        ups.append(pltpu.make_async_copy(uv_hbm.at[:, cols], up_v.at[4 + h], u_load.at[4 + h]))
    for load in ups:
        load.start()
    x_copy = pltpu.make_async_copy(x_hbm, x_v, x_load)
    x_copy.start()
    k_copy = pltpu.make_async_copy(kc_hbm, kc_v, c_load.at[0])
    v_copy = pltpu.make_async_copy(vc_hbm, vc_v, c_load.at[1])
    k_copy.start()
    v_copy.start()

    pl.semaphore_wait(barrier, N_CTX + 2)

    def send(src, dst, send_sem, recv_sem, device):
        pltpu.make_async_remote_copy(
            src_ref=src,
            dst_ref=dst,
            send_sem=send_sem,
            recv_sem=recv_sem,
            device_id=device,
            device_id_type=MESH,
        ).start()

    for load in shard_loads:
        load.wait()

    def block_of(h):
        u = h // 2
        return jnp.where(u == 0, HEADS + s, u - 1)

    def pass_on(h, stage, shard, first, count, ctx):
        start = shard * SHARD + lax.rem(h, 2) * HALF + first
        piece = w_v.at[block_of(h), pl.ds(pl.multiple_of(start, 64), count)]
        send(piece, piece, g_send.at[h], g_recv.at[h, stage], here(ctx))

    def arrived(h, stage, shards):
        wait_bytes(w_v.at[block_of(h), pl.ds(0, shards * HALF)], g_recv.at[h, stage])

    yp, ym, zp, zm = chip(1, 0), chip(-1, 0), chip(0, 1), chip(0, -1)
    A, B, A0, A1, B0, B1, ZERO = (
        (0, 128),
        (128, 128),
        (64, 64),
        (0, 64),
        (128, 64),
        (192, 64),
        (64, 128),
    )

    def stage1(u):
        for ctx in (yp, zp, ym, zm):
            pass_on(u, 0, c, 0, HALF, ctx)

    def stage2(u):
        arrived(u, 0, 4)
        pass_on(u, 1, ym, *ZERO, yp)
        pass_on(u, 1, yp, *A1, ym)
        pass_on(u, 1, yp, *B1, ym)
        pass_on(u, 1, zm, *ZERO, zp)
        pass_on(u, 1, zp, *A1, zm)
        pass_on(u, 1, zp, *B1, zm)
        for shard in (ym, yp):
            for ctx in (zp, zm):
                pass_on(u, 1, shard, *A, ctx)
        for shard in (zm, zp):
            for ctx in (yp, ym):
                pass_on(u, 1, shard, *B, ctx)

    def stage3(u):
        arrived(u, 1, 6)
        yy, zz = chip(2, 0), chip(0, 2)
        for ctx in (zp, zm):
            pass_on(u, 2, yy, *A, ctx)
        for ctx in (yp, ym):
            pass_on(u, 2, zz, *B, ctx)
        for d in (-1, 1):
            pass_on(u, 2, chip(d, -1), *A0, zp)
            pass_on(u, 2, chip(d, 1), *A1, zm)
            pass_on(u, 2, chip(-1, d), *B0, yp)
            pass_on(u, 2, chip(1, d), *B1, ym)

    def stage4(u):
        arrived(u, 2, 4)
        pass_on(u, 3, chip(2, -1), *A0, zp)
        pass_on(u, 3, chip(2, 1), *A1, zm)
        pass_on(u, 3, chip(-1, 2), *B0, yp)
        pass_on(u, 3, chip(1, 2), *B1, ym)

    GROUPS = (
        (ym, yp, zm, zp),
        (chip(-1, -1), chip(-1, 1), chip(1, -1), chip(1, 1), chip(2, 0), chip(0, 2)),
        (chip(-1, 2), chip(1, 2), chip(2, -1), chip(2, 1)),
        (chip(2, 2),),
    )

    def across(group, half):
        for shard in GROUPS[group]:
            rows = pl.ds(pl.multiple_of(shard * SHARD + half * HALF, HALF), HALF)
            piece = w_v.at[HEADS + s, rows]
            send(piece, piece, x_send.at[0], x_recv.at[0, group], right)
            send(piece, piece, x_send.at[1], x_recv.at[1, group], left)

    def across_again(group):
        count = len(GROUPS[group])
        wait_bytes(w_v.at[HEADS + s_left, pl.ds(0, count * SHARD)], x_recv.at[0, group])
        wait_bytes(w_v.at[HEADS + s_right, pl.ds(0, count * SHARD)], x_recv.at[1, group])
        for shard in GROUPS[group]:
            rows = pl.ds(pl.multiple_of(shard * SHARD, SHARD), CUT)
            piece = w_v.at[HEADS + s_left, rows]
            send(piece, piece, f_send.at[0], f_recv.at[0, group], right)
            rows = pl.ds(pl.multiple_of(shard * SHARD + CUT, 128), SHARD - CUT)
            piece = w_v.at[HEADS + s_right, rows]
            send(piece, piece, f_send.at[1], f_recv.at[1, group], left)

    span_request = target_of[s]
    span_adapter = jnp.int32(0)
    for b in range(N_CTX):
        span_adapter = jnp.where(span_request == b, adapter_of[b], span_adapter)
    pick_row = lax.broadcasted_iota(jnp.int32, (ADAPTER_RANK, HD), 0)
    pick_col = lax.broadcasted_iota(jnp.int32, (ADAPTER_RANK, HD), 1)
    pick = jnp.where(pick_col == span_adapter * ADAPTER_RANK + pick_row, 1.0, 0.0).astype(BF16)

    def down_rows():
        down_load.wait()
        own = pl.ds(pl.multiple_of(c * SHARD, SHARD), SHARD)
        dt_v[:, own] = nt_dot(pick, wd_v[...]).astype(BF16)

        @pl.loop(1, N_CTX)
        def _(j):
            piece = dt_v.at[:, own]
            ctx = lax.rem(c + j, N_CTX)
            send(piece, piece, small_send.at[7], small_recv.at[7], here(ctx))

    def project_down():
        for load in ups:
            load.wait()
        wait_bytes(dt_v.at[:, pl.ds(0, (N_CTX - 1) * SHARD)], small_recv.at[7])
        acc[...] = jnp.zeros_like(acc)

        @pl.loop(0, 8)
        def _(i):
            part_k = pl.ds(pl.multiple_of(i * 1024, 1024), 1024)
            acc[:, 0:ADAPTER_RANK] += nt_dot(x_v[:, part_k], dt_v[:, part_k])

        down = acc[:, 0:ADAPTER_RANK].astype(BF16)
        dn[t] = jnp.dot(down, pick, preferred_element_type=F32).astype(BF16)
        send(dn.at[t], dn.at[t], small_send.at[1], small_recv.at[1], partner)

    def add_shards(n, shards, first, count):
        parts = [
            pl.ds(pl.multiple_of(shard * SHARD + first, HALF), count) for shard in shards
        ]

        @pl.loop(0, 2)
        def _(m):
            some = pl.ds(pl.multiple_of(m * 256, 256), 256)
            hidden = jnp.concatenate([x_v[some, part] for part in parts], axis=1)
            weight = jnp.concatenate([w_v[n, part] for part in parts], axis=0)
            accs[n, some] += jnp.dot(hidden, weight, preferred_element_type=F32)

    def add_across(group):
        shards = GROUPS[group] + ((c,) if group == 0 else ())
        add_shards(HEADS + s_left, shards, 0, SHARD)
        add_shards(HEADS + s_right, shards, 0, SHARD)

    def add_far(group):
        count = len(GROUPS[group])
        n = HEADS + s_far
        wait_bytes(w_v.at[n, pl.ds(0, count * CUT)], f_recv.at[0, group])
        wait_bytes(w_v.at[n, pl.ds(0, count * (SHARD - CUT))], f_recv.at[1, group])
        add_shards(n, GROUPS[group] + ((c,) if group == 0 else ()), 0, SHARD)

    def nth(p, sec):
        keys = jnp.where(p == 6, 3, p // 2)
        ahead = jnp.where(p == 2, n_sec - 1, jnp.where(p == 4, 1, jnp.where(p == 7, 2, 0)))
        is_key = (p == 1) | (p == 3) | (p == 5) | (p == 6)
        return jnp.where(is_key, keys, HEADS + lax.rem(sec + ahead, n_sec))

    def project(p):
        n = nth(p, s)

        @pl.when(p == 0)
        def _():
            wait_bytes(dn.at[0], small_recv.at[1])

        delta = jnp.dot(dn[n // HEADS], up_v[n], preferred_element_type=F32)
        row[n] = (accs[n] + ADAPTER_SCALE * delta).astype(BF16)
        send(row.at[n], raw.at[n], row_send.at[n], row_recv.at[n], right)

    def exchange(n):
        @pl.loop(1, N_CTX)
        def _(j):
            ctx = lax.rem(c + j, N_CTX)
            theirs = pl.ds(pl.multiple_of(ctx * PAIR, PAIR), PAIR)
            ours = pl.ds(pl.multiple_of(c * PAIR, PAIR), PAIR)
            send(
                sendb.at[n, theirs], pages.at[n, ours], a_send.at[n], a_recv.at[n], here(ctx)
            )

        ours = pl.ds(pl.multiple_of(c * PAIR, PAIR), PAIR)
        pages[n, ours] = sendb[n, ours]

    def place(n):
        wait_bytes(raw.at[n], row_recv.at[n])

        @pl.loop(0, 4)
        def _(i):
            some = pl.ds(pl.multiple_of(i * 256, 256), 256)
            sendb[n, some] = jnp.dot(
                place_m[some], raw[n], preferred_element_type=F32
            ).astype(BF16)

        exchange(n)

    def page_rows():
        first = lax.broadcasted_iota(jnp.int32, (16, 16), 0)
        second = lax.broadcasted_iota(jnp.int32, (16, 16), 1)
        across_ids = jnp.broadcast_to(owner_of[...].astype(F32), (16, 16))
        ids = jnp.sum(jnp.where(first == second, across_ids, 0.0), axis=1, keepdims=True)
        before = (ids == across_ids) & (second < first)
        rank = jnp.sum(jnp.where(before, 1.0, 0.0), axis=1, keepdims=True)
        slot_row = (ids * 2 + rank) * BLK
        page = lax.broadcasted_iota(jnp.int32, (16, ROWS), 0)
        lane = lax.broadcasted_iota(jnp.int32, (16, ROWS), 1)
        token = lax.rem(lane, BLK).astype(F32)
        rows = jnp.sum(
            jnp.where(lane // BLK == page, slot_row + token, 0.0), axis=0, keepdims=True
        )
        drow[...] = jnp.broadcast_to(rows, (8, ROWS)).astype(jnp.int32)
        send(drow, drow_r, small_send.at[0], small_recv.at[0], right)

    def page_flags():
        wait_bytes(drow_r, small_recv.at[0])

        @pl.loop(0, 4)
        def _(i):
            some = pl.ds(pl.multiple_of(i * 256, 256), 256)
            slot_row = lax.broadcasted_iota(jnp.int32, (256, ROWS), 0) + i * 256
            hit = slot_row == drow_r[0:1]
            place_m[some] = jnp.where(hit, 1.0, 0.0).astype(BF16)
            flag = jnp.max(jnp.where(hit, 1.0, 0.0), axis=1, keepdims=True)
            sendb[8, some] = jnp.broadcast_to(flag, (256, HD)).astype(BF16)

        exchange(8)

    def landed(n):
        wait_bytes(pages.at[n, pl.ds(0, SLOT_ROWS - PAIR)], a_recv.at[n])

    def write_out(n):
        cols = pl.ds(pl.multiple_of(lax.rem(n, HEADS) * HD, HD), HD)

        @pl.when(n < HEADS)
        def _():
            pltpu.make_async_copy(pages.at[n], pk_out.at[:, cols], out_sem.at[n]).start()

        @pl.when(n >= HEADS)
        def _():
            pltpu.make_async_copy(pages.at[n], pv_out.at[:, cols], out_sem.at[n]).start()

    def decode_project():
        q_copy.wait()

        def blocks(product, first):
            for i in range(product.shape[1] // HD):
                part[first + i] = product[:, i * HD : (i + 1) * HD]

        hid[0:4] = xd[0].astype(F32)
        hid[4:8] = xd[1].astype(F32)
        hidden = hid[...].astype(BF16)
        part[DBLOCKS - 6 :] = jnp.zeros((6, 8, HD), F32)
        for i in range(8):
            piece = wq_v[:, i * 512 : (i + 1) * 512]
            blocks(jnp.dot(hidden, piece, preferred_element_type=F32), 4 * i)
        for n in range(BLOCKS):
            blocks(jnp.dot(hidden, w_v[n, mine], preferred_element_type=F32), 32 + n)
        part[40 + t] = jnp.dot(hidden, wd_v[...], preferred_element_type=F32)
        send(part.at[40 + t], part.at[40 + t], small_send.at[2], small_recv.at[2], partner)

    def decode_spread():
        wait_bytes(part.at[0], small_recv.at[2])

        @pl.loop(1, N_CTX)
        def _(j):
            ctx = lax.rem(c + j, N_CTX)
            send(
                part.at[pl.ds(ctx * PER, PER)],
                rsr.at[c],
                small_send.at[3],
                small_recv.at[3],
                here(ctx),
            )

        rsr[c] = part[pl.ds(c * PER, PER)]

    def decode_sum():
        wait_bytes(rsr.at[pl.ds(0, N_CTX - 1)], small_recv.at[3])
        ag[pl.ds(c * PER, PER)] = jnp.sum(rsr[...], axis=0)

        @pl.loop(1, N_CTX)
        def _(j):
            ctx = lax.rem(c + j, N_CTX)
            piece = ag.at[pl.ds(c * PER, PER)]
            send(piece, piece, small_send.at[4], small_recv.at[4], here(ctx))

    def decode_rows():
        wait_bytes(ag.at[pl.ds(0, (N_CTX - 1) * PER)], small_recv.at[4])
        to = lax.broadcasted_iota(jnp.int32, (QROWS, QROWS), 0)
        at = lax.broadcasted_iota(jnp.int32, (QROWS, QROWS), 1)
        source = lax.rem(to, 8) * 8 + lax.rem(to // 8, STEPS) * RPG + to // 16
        perm = jnp.where(at == source, 1.0, 0.0).astype(BF16)
        for k in range(HEADS):
            queries = ag[8 * k : 8 * k + 8].reshape(QROWS, HD).astype(BF16)
            qp[k] = jnp.dot(perm, queries, preferred_element_type=F32).astype(BF16)
        lane = lax.broadcasted_iota(jnp.int32, (8, HD), 1) // ADAPTER_RANK
        who = lax.rem(lax.broadcasted_iota(jnp.int32, (8, HD), 0), RPG)
        adapter = jnp.zeros((8, HD), jnp.int32)
        for b in range(RPG):
            adapter = jnp.where(who == b, adapter_of[s * RPG + b], adapter)
        for kind in range(2):
            down = ag[40 + kind].astype(BF16).astype(F32)
            picked = jnp.where(lane == adapter, down, 0.0).astype(BF16)
            for k in range(HEADS):
                n = 4 * kind + k
                delta = jnp.dot(picked, up_v[n], preferred_element_type=F32)
                tkv[n] = (ag[32 + n] + ADAPTER_SCALE * delta).astype(BF16).astype(F32)
        which = lax.broadcasted_iota(jnp.int32, (QROWS, 8), 0)
        other = lax.broadcasted_iota(jnp.int32, (QROWS, 8), 1)
        tok_live = (
            (lax.rem(other, RPG) == which // 16)
            & (other // RPG <= lax.rem(which // 8, STEPS))
            & (c == 0)
        )
        for k in range(HEADS):
            tok = nt_dot(qp[k], tkv[k].astype(BF16)) * INV_ROOT
            tok_max = jnp.max(jnp.where(tok_live, tok, NEG_FLOOR), axis=1, keepdims=True)
            tok_w = jnp.where(tok_live, jnp.exp(tok - tok_max), 0.0)
            tok_out = jnp.zeros((QROWS, HD), F32)
            for i in range(8):
                tok_out = tok_out + tok_w[:, i : i + 1] * tkv[4 + k, i : i + 1]
            pst[0, k] = jnp.broadcast_to(tok_max, (QROWS, HD))
            pst[1, k] = jnp.broadcast_to(jnp.sum(tok_w, axis=1, keepdims=True), (QROWS, HD))
            pst[2, k] = tok_out

    def merge(k, rows, block_max, total, out):
        old = pst[0, k, rows]
        top = jnp.maximum(old, block_max)
        old_scale, scale = jnp.exp(old - top), jnp.exp(block_max - top)
        pst[0, k, rows] = top
        pst[1, k, rows] = old_scale * pst[1, k, rows] + scale * total
        pst[2, k, rows] = old_scale * pst[2, k, rows] + scale * out

    def cache_block(b):
        @pl.when(b == 0)
        def _():
            k_copy.wait()
            v_copy.wait()

        left_len = length_of[b] - c * CTX_DEV
        live = lax.broadcasted_iota(jnp.int32, (16, CTX_DEV), 1) < left_len
        rows = pl.ds(pl.multiple_of(b * 16, 16), 16)
        for k in range(HEADS):
            cols = slice(k * HD, (k + 1) * HD)
            scores = nt_dot(qp[k, rows], kc_v[b, :, cols]) * INV_ROOT
            block_max = jnp.max(jnp.where(live, scores, NEG_FLOOR), axis=1, keepdims=True)
            weights = jnp.where(live, jnp.exp(scores - block_max), 0.0).astype(BF16)
            total = jnp.sum(weights.astype(F32), axis=1, keepdims=True)
            out = jnp.dot(weights, vc_v[b, :, cols], preferred_element_type=F32)
            merge(k, rows, block_max, total, out)

    page_request = target_of[s_left] - s * RPG

    def page_scores(k):
        live = nt_dot(jnp.ones((16, HD), BF16), pages[8]) > 0.5
        query = jnp.zeros((16, HD), F32)
        for b in range(RPG):
            query = jnp.where(page_request == b, qp[k, b * 16 : b * 16 + 16].astype(F32), query)
        scores = nt_dot(query.astype(BF16), pages[k]) * INV_ROOT
        p_max = jnp.max(jnp.where(live, scores, NEG_FLOOR), axis=1, keepdims=True)
        weights = jnp.where(live, jnp.exp(scores - p_max), 0.0).astype(BF16)
        p_total = jnp.sum(weights.astype(F32), axis=1, keepdims=True)
        pgw[k] = weights
        pgs[0, k] = jnp.broadcast_to(p_max, (16, HD))
        pgs[1, k] = jnp.broadcast_to(p_total, (16, HD))

    def page_merge(k):
        p_out = jnp.dot(pgw[k], pages[HEADS + k], preferred_element_type=F32)
        lane = lax.broadcasted_iota(jnp.int32, (16, HD), 1)
        for b in range(RPG):
            rows = slice(b * 16, b * 16 + 16)
            wanted = page_request == b
            merge(
                k,
                rows,
                jnp.where(wanted, pgs[0, k], NEG_FLOOR),
                jnp.where(wanted, pgs[1, k], 0.0),
                jnp.where(wanted, p_out, 0.0),
            )
            mgs[k * RPG + b, 0] = pst[2, k, rows]
            mgs[k * RPG + b, 1] = jnp.where(lane < 64, pst[0, k, rows], pst[1, k, rows])
            ctx = k * RPG + b

            @pl.when(ctx != c)
            def _():
                send(mgs.at[ctx], mgr.at[c], small_send.at[5], small_recv.at[5], here(ctx))

    stage1(0)
    stage1(1)
    down_rows()
    page_rows()
    accs[...] = jnp.zeros_like(accs)

    @pl.loop(2, LAST)
    def _(i):
        @pl.when((i >= 6) & (i < HALVES + 6))
        def _():
            stage4(i - 6)

        @pl.when((i >= 4) & (i < HALVES + 4))
        def _():
            stage3(i - 4)

        @pl.when((i >= 2) & (i < HALVES + 2))
        def _():
            stage2(i - 2)

        @pl.when(i < HALVES)
        def _():
            stage1(i)

        @pl.when((i >= 8) & (i < HALVES + 8))
        def _():
            arrived(i - 8, 3, 1)

        for group in range(4):

            @pl.when((i == 2 + 2 * group) | (i == 3 + 2 * group))
            def _(group=group):
                across(group, lax.rem(i, 2))

        for group, at in enumerate(ACROSS_AT):

            @pl.when(i == at)
            def _(group=group):
                across_again(group)

        @pl.when(i == ADD_LAG[0])
        def _():
            x_copy.wait()

        for stage, lag in enumerate(ADD_LAG):

            @pl.when((i >= lag) & (i < HALVES + lag))
            def _(stage=stage, lag=lag):
                shards = GROUPS[stage] + ((c,) if stage == 0 else ())
                h = i - lag
                add_shards(block_of(h), shards, lax.rem(h, 2) * HALF, HALF)

        for group, at in enumerate(ACROSS_AT):

            @pl.when(i == at)
            def _(group=group):
                add_across(group)

        for group, at in enumerate(FAR_AT):

            @pl.when(i == at)
            def _(group=group):
                add_far(group)

        @pl.when(i == 4)
        def _():
            decode_project()

        @pl.when(i == 5)
        def _():
            decode_spread()

        @pl.when(i == 6)
        def _():
            page_flags()

        @pl.when(i == 7)
        def _():
            decode_sum()

        @pl.when(i == 8)
        def _():
            project_down()

        now, p = turn(i, PROJECT_AT)

        @pl.when(now)
        def _():
            project(p)

        @pl.when(i == 9)
        def _():
            decode_rows()

        now, q = turn(i, PLACE_AT)

        @pl.when(now)
        def _():
            place(nth(q, s_left))

        now, b = turn(i, CACHE_AT)

        @pl.when(now)
        def _():
            cache_block(b)

        @pl.when(i == LAND_AT[0])
        def _():
            landed(8)

        now, r = turn(i, LAND_AT)

        @pl.when(now)
        def _():
            n = nth(r, s_left)
            landed(n)
            write_out(n)

            @pl.when(n < HEADS)
            def _():
                page_scores(n)

    for r in (0, 2, 4):
        page_merge(nth(r, s_left) - HEADS)
    far = nth(BLOCKS - 1, s_left)
    landed(far)
    page_merge(far - HEADS)
    write_out(far)

    mgr[c] = mgs[c]
    wait_bytes(mgr.at[pl.ds(0, N_CTX - 1)], small_recv.at[5])
    stats = mgr[:, 1]
    tops, totals = stats[:, :, 0:1], stats[:, :, 64:65]
    scale = jnp.exp(tops - jnp.max(tops, axis=0, keepdims=True))
    numer = jnp.sum(scale * mgr[:, 0], axis=0)
    denom = jnp.sum(scale * totals, axis=0)
    att[c] = (numer / denom).astype(BF16)

    @pl.loop(1, N_CTX)
    def _(j):
        ctx = lax.rem(c + j, N_CTX)
        send(att.at[c], att.at[c], small_send.at[6], small_recv.at[6], here(ctx))

    wait_bytes(att.at[pl.ds(0, N_CTX - 1)], small_recv.at[6])
    att_out[...] = att[...]

    @pl.loop(0, HALVES)
    def _(h):
        wait_bytes(w_v.at[0, pl.ds(0, 15 * HALF)], g_send.at[h])

    @pl.loop(0, BLOCKS + 1)
    def _(u):
        wait_bytes(sendb.at[u, pl.ds(0, SLOT_ROWS - PAIR)], a_send.at[u])

    for d, count in ((0, CUT), (1, SHARD - CUT)):
        wait_bytes(w_v.at[0, pl.ds(0, 15 * SHARD)], x_send.at[d])
        wait_bytes(w_v.at[0, pl.ds(0, 15 * count)], f_send.at[d])

    @pl.loop(0, 2 * HEADS)
    def _(n):
        wait_bytes(row.at[n], row_send.at[n])
        wait_bytes(pages.at[n], out_sem.at[n])

    wait_bytes(drow, small_send.at[0])
    wait_bytes(dn.at[0], small_send.at[1])
    wait_bytes(part.at[0], small_send.at[2])
    wait_bytes(rsr.at[pl.ds(0, N_CTX - 1)], small_send.at[3])
    wait_bytes(ag.at[pl.ds(0, (N_CTX - 1) * PER)], small_send.at[4])
    wait_bytes(mgr.at[pl.ds(0, N_CTX - 1)], small_send.at[5])
    wait_bytes(att.at[pl.ds(0, N_CTX - 1)], small_send.at[6])
    wait_bytes(dt_v.at[:, pl.ds(0, (N_CTX - 1) * SHARD)], small_send.at[7])


def finish_kernel(pk, pv, att, pk_out, pv_out, att_out, held, rows, in_sem, out_sem):
    parts = [(j, i) for i in range(4) for j in range(2)]

    def moves(j, i):
        some = pl.ds(i * (SLOT_ROWS // 4), SLOT_ROWS // 4)
        source, result = (pk, pv)[j], (pk_out, pv_out)[j]
        return (
            pltpu.make_async_copy(source.at[some], held.at[j, some], in_sem.at[j, i]),
            pltpu.make_async_copy(held.at[j, some], result.at[some], out_sem.at[j, i]),
        )

    copies = [moves(j, i) for j, i in parts]
    for into, _ in copies:
        into.start()
    for k in range(HEADS):
        for b in range(RPG):
            block = att[k * RPG + b].astype(F32)
            for step in range(STEPS):
                for g in range(8):
                    cols = slice((k * 8 + g) * HD, (k * 8 + g + 1) * HD)
                    at = step * 8 + g
                    rows[step, b : b + 1, cols] = block[at : at + 1]
    att_out[...] = rows[...].astype(BF16)
    for into, out in copies:
        into.wait()
        out.start()
    for _, out in copies:
        out.wait()


def on_device(
    prefill_hidden_states,
    decode_hidden_states,
    query_matrix,
    key_matrix,
    value_matrix,
    adapter_down_maps,
    key_adapter_up_maps,
    value_adapter_up_maps,
    request_key_cache,
    request_value_cache,
    request_adapter_index,
    prefill_request_target,
    request_context_length,
    page_owner_index,
):
    hbm = pl.BlockSpec(memory_space=pl.ANY)
    vmem = pl.BlockSpec(memory_space=pltpu.VMEM)
    smem = pl.BlockSpec(memory_space=pltpu.SMEM)
    dma = pltpu.SemaphoreType.DMA
    page_keys, page_values, attended = pl.pallas_call(
        layer_kernel,
        out_shape=(
            jax.ShapeDtypeStruct((SLOT_ROWS, HEADS * HD), BF16),
            jax.ShapeDtypeStruct((SLOT_ROWS, HEADS * HD), BF16),
            jax.ShapeDtypeStruct((N_CTX, 16, HD), BF16),
        ),
        in_specs=[smem] * 3 + [vmem] * 2 + [hbm] * 9,
        out_specs=(hbm, hbm, vmem),
        scratch_shapes=[
            pltpu.VMEM((ROWS, 8192), BF16),
            pltpu.VMEM((BLOCKS, 8192, HD), BF16),
            pltpu.VMEM((SHARD, 4096), BF16),
            pltpu.VMEM((SHARD, HD), BF16),
            pltpu.VMEM((ADAPTER_RANK, 8192), BF16),
            pltpu.VMEM((8, SHARD), F32),
            pltpu.VMEM((8, HD, HD), BF16),
            pltpu.VMEM((RPG, CTX_DEV, HEADS * HD), BF16),
            pltpu.VMEM((RPG, CTX_DEV, HEADS * HD), BF16),
            pltpu.VMEM((ROWS, HD), F32),
            pltpu.VMEM((BLOCKS, ROWS, HD), F32),
            pltpu.VMEM((2, ROWS, HD), BF16),
            pltpu.VMEM((8, ROWS, HD), BF16),
            pltpu.VMEM((8, ROWS, HD), BF16),
            pltpu.VMEM((SLOT_ROWS, ROWS), BF16),
            pltpu.VMEM((8, ROWS), jnp.int32),
            pltpu.VMEM((8, ROWS), jnp.int32),
            pltpu.VMEM((9, SLOT_ROWS, HD), BF16),
            pltpu.VMEM((9, SLOT_ROWS, HD), BF16),
            pltpu.VMEM((DBLOCKS, 8, HD), F32),
            pltpu.VMEM((N_CTX, PER, 8, HD), F32),
            pltpu.VMEM((DBLOCKS, 8, HD), F32),
            pltpu.VMEM((HEADS, QROWS, HD), BF16),
            pltpu.VMEM((8, 8, HD), F32),
            pltpu.VMEM((3, HEADS, QROWS, HD), F32),
            pltpu.VMEM((HEADS, 16, SLOT_ROWS), BF16),
            pltpu.VMEM((2, HEADS, 16, HD), F32),
            pltpu.VMEM((N_CTX, 2, 16, HD), F32),
            pltpu.VMEM((N_CTX, 2, 16, HD), F32),
            pltpu.VMEM((N_CTX, 16, HD), BF16),
            dma((9,)),
            dma,
            dma,
            dma((2,)),
            dma((8,)),
            dma((HALVES, 4)),
            dma((HALVES,)),
            dma((2, 4)),
            dma((2,)),
            dma((2, 4)),
            dma((2,)),
            dma((8,)),
            dma((8,)),
            dma((9,)),
            dma((9,)),
            dma((8,)),
            dma((8,)),
            dma((8,)),
        ],
        compiler_params=pltpu.CompilerParams(
            collective_id=0, has_side_effects=True, vmem_limit_bytes=58 * 1024 * 1024
        ),
        cost_estimate=pl.CostEstimate(
            flops=12_000_000_000, bytes_accessed=30_000_000, transcendentals=600_000
        ),
    )(
        request_adapter_index,
        prefill_request_target,
        request_context_length,
        page_owner_index.reshape(1, 16),
        decode_hidden_states,
        prefill_hidden_states,
        query_matrix,
        key_matrix,
        value_matrix,
        adapter_down_maps,
        key_adapter_up_maps,
        value_adapter_up_maps,
        request_key_cache,
        request_value_cache,
    )
    page_shape = (SLOT_ROWS // BLK, BLK, HEADS * HD)
    page_keys, page_values, attended = pl.pallas_call(
        finish_kernel,
        out_shape=(
            jax.ShapeDtypeStruct((SLOT_ROWS, HEADS * HD), BF16),
            jax.ShapeDtypeStruct((SLOT_ROWS, HEADS * HD), BF16),
            jax.ShapeDtypeStruct((STEPS, RPG, HEADS * 8 * HD), BF16),
        ),
        in_specs=[hbm, hbm, vmem],
        out_specs=(hbm, hbm, vmem),
        scratch_shapes=[
            pltpu.VMEM((2, SLOT_ROWS, HEADS * HD), BF16),
            pltpu.VMEM((STEPS, RPG, HEADS * 8 * HD), F32),
            dma((2, 4)),
            dma((2, 4)),
        ],
        compiler_params=pltpu.CompilerParams(vmem_limit_bytes=58 * 1024 * 1024),
    )(page_keys, page_values, attended)
    return (page_keys.reshape(page_shape), page_values.reshape(page_shape), attended)


def solution(mesh):
    return jax.shard_map(
        on_device,
        mesh=mesh,
        in_specs=(
            P(("section", "ctx"), None),
            P(None, "section", "ctx"),
            P("ctx", "tp"),
            P("ctx", "tp"),
            P("ctx", "tp"),
            P("ctx", "tp"),
            P(None, "tp"),
            P(None, "tp"),
            P("section", "ctx", "tp"),
            P("section", "ctx", "tp"),
            P(),
            P(),
            P("section"),
            P(("section", "ctx"), None),
        ),
        out_specs=(
            P(("section", "ctx"), None, "tp"),
            P(("section", "ctx"), None, "tp"),
            P(None, "section", "tp"),
        ),
        check_vma=False,
    )
```

```python
import functools

import jax
import jax.numpy as jnp
from jax import lax
from jax.experimental import pallas as pl
from jax.experimental.pallas import tpu as pltpu
from jax.sharding import PartitionSpec as P

H = 64
KVH = 8
HD = 128
ADAPTER_RANK = 16
BLK = 32
STEPS = 2

ADAPTER_SCALE = 0.5
CUT = 128
NEG_FLOOR = -1e30
INV_ROOT = HD ** (-0.5)

SIDE = 4
N_CTX = 16
SHARD = 512
UNITS = 5
HALVES = 2 * UNITS
HALF = 256
BLOCKS = 8
HEADS = 4
ROWS = 512
SLOT_ROWS = 1024
PAIR = 64
RPG = 4
CTX_DEV = 1024
QROWS = 64
DBLOCKS = 48
PER = 3

STEPS_AT = ((9, 0, 1), (12, 1, 3), (13, 3, 5), (17, 5, 7))
PLACES = (13, 15, 17, 19)
LANDS = (18, 19, 20, 21)
FAR = 7
PLACE_LAG = 2
LAND_LAG = 6
CACHE_AT = (18, 19, 20, 21)
ACROSS_AT = (9, 11, 12, 12)
FAR_AT = 18
LAST = 21

MESH = pl.DeviceIdType.MESH
F32 = jnp.float32
BF16 = jnp.bfloat16


def wait_bytes(ref, sem):
    pltpu.make_async_copy(ref, ref, sem).wait()


def turn(i, slots):
    here, which = False, -1
    for at in slots:
        here = here | (i == at)
        which = which + jnp.where(i >= at, 1, 0)
    return here, which


def nt_dot(a, b):
    return lax.dot_general(a, b, (((1,), (1,)), ((), ())), preferred_element_type=F32)


def layer_kernel(
    adapter_of,
    target_of,
    length_of,
    owner_of,
    xd,
    x_hbm,
    wq_hbm,
    wk_hbm,
    wv_hbm,
    wd_hbm,
    uk_hbm,
    uv_hbm,
    kc_hbm,
    vc_hbm,
    pk_out,
    pv_out,
    att_out,
    x_v,
    w_v,
    wq_v,
    wd_v,
    dt_v,
    hid,
    up_v,
    kc_v,
    vc_v,
    acc,
    accs,
    dn,
    row,
    raw,
    place_m,
    drow,
    drow_r,
    sendb,
    pages,
    part,
    rsr,
    ag,
    qp,
    tkv,
    pst,
    pgw,
    pgs,
    mgs,
    mgr,
    att,
    w_load,
    q_load,
    x_load,
    c_load,
    u_load,
    g_recv,
    g_send,
    x_recv,
    x_send,
    f_recv,
    f_send,
    row_send,
    row_recv,
    a_send,
    a_recv,
    small_send,
    small_recv,
    out_sem,
):
    s = lax.axis_index("section")
    c = lax.axis_index("ctx")
    t = lax.axis_index("tp")
    n_sec = lax.axis_size("section")
    y = c // SIDE
    z = lax.rem(c, SIDE)

    def chip(dy, dz):
        return lax.rem(y + dy + SIDE, SIDE) * SIDE + lax.rem(z + dz + SIDE, SIDE)

    def here(ctx):
        return (s, ctx, t)

    right = (lax.rem(s + 1, n_sec), c, t)
    left = (lax.rem(s + n_sec - 1, n_sec), c, t)
    partner = (s, c, 1 - t)
    s_left = lax.rem(s + n_sec - 1, n_sec)
    s_right = lax.rem(s + 1, n_sec)
    s_far = lax.rem(s + 2, n_sec)

    barrier = pltpu.get_barrier_semaphore()

    @pl.loop(1, N_CTX)
    def _(j):
        pl.semaphore_signal(
            barrier, inc=1, device_id=here(lax.rem(c + j, N_CTX)), device_id_type=MESH
        )

    for peer in (left, right, partner):
        pl.semaphore_signal(barrier, inc=1, device_id=peer, device_id_type=MESH)

    mine = pl.ds(pl.multiple_of(c * SHARD, SHARD), SHARD)
    shard_loads = []
    for n, hbm in enumerate([wk_hbm] * HEADS + [wv_hbm] * HEADS):
        cols = pl.ds(n % HEADS * HD, HD)
        shard_loads.append(
            pltpu.make_async_copy(hbm.at[:, cols], w_v.at[n, mine], w_load.at[n])
        )
    down_load = pltpu.make_async_copy(wd_hbm, wd_v, w_load.at[8])
    down_load.start()
    for load in shard_loads:
        load.start()
    q_copy = pltpu.make_async_copy(wq_hbm, wq_v, q_load)
    q_copy.start()
    ups = []
    for h in range(HEADS):
        cols = pl.ds(h * HD, HD)
        ups.append(pltpu.make_async_copy(uk_hbm.at[:, cols], up_v.at[h], u_load.at[h]))
        ups.append(pltpu.make_async_copy(uv_hbm.at[:, cols], up_v.at[4 + h], u_load.at[4 + h]))
    for load in ups:
        load.start()
    x_copy = pltpu.make_async_copy(x_hbm, x_v, x_load)
    x_copy.start()
    k_copy = pltpu.make_async_copy(kc_hbm, kc_v, c_load.at[0])
    v_copy = pltpu.make_async_copy(vc_hbm, vc_v, c_load.at[1])
    k_copy.start()
    v_copy.start()

    pl.semaphore_wait(barrier, N_CTX + 2)

    def send(src, dst, send_sem, recv_sem, device):
        pltpu.make_async_remote_copy(
            src_ref=src,
            dst_ref=dst,
            send_sem=send_sem,
            recv_sem=recv_sem,
            device_id=device,
            device_id_type=MESH,
        ).start()

    for load in shard_loads:
        load.wait()

    def block_of(h):
        key = (h - 2) // 4 * 2 + lax.rem(h, 2)
        return jnp.where(h < 2, HEADS + s, key)

    def half_of(h):
        return jnp.where(h < 2, h, lax.rem((h - 2) // 2, 2))

    def pass_on(h, stage, shard, first, count, ctx):
        start = shard * SHARD + half_of(h) * HALF + first
        piece = w_v.at[block_of(h), pl.ds(pl.multiple_of(start, 64), count)]
        send(piece, piece, g_send.at[h], g_recv.at[h, stage], here(ctx))

    def arrived(h, stage, shards):
        wait_bytes(w_v.at[block_of(h), pl.ds(0, shards * HALF)], g_recv.at[h, stage])

    yp, ym, zp, zm = chip(1, 0), chip(-1, 0), chip(0, 1), chip(0, -1)
    A, B, A0, A1, B0, B1, ZERO = (
        (0, 128),
        (128, 128),
        (64, 64),
        (0, 64),
        (128, 64),
        (192, 64),
        (64, 128),
    )

    def stage1(u):
        for ctx in (yp, zp, ym, zm):
            pass_on(u, 0, c, 0, HALF, ctx)

    def stage2(u):
        arrived(u, 0, 4)
        pass_on(u, 1, ym, *ZERO, yp)
        pass_on(u, 1, yp, *A1, ym)
        pass_on(u, 1, yp, *B1, ym)
        pass_on(u, 1, zm, *ZERO, zp)
        pass_on(u, 1, zp, *A1, zm)
        pass_on(u, 1, zp, *B1, zm)
        for shard in (ym, yp):
            for ctx in (zp, zm):
                pass_on(u, 1, shard, *A, ctx)
        for shard in (zm, zp):
            for ctx in (yp, ym):
                pass_on(u, 1, shard, *B, ctx)

    def stage3(u):
        arrived(u, 1, 6)
        yy, zz = chip(2, 0), chip(0, 2)
        for ctx in (zp, zm):
            pass_on(u, 2, yy, *A, ctx)
        for ctx in (yp, ym):
            pass_on(u, 2, zz, *B, ctx)
        for d in (-1, 1):
            pass_on(u, 2, chip(d, -1), *A0, zp)
            pass_on(u, 2, chip(d, 1), *A1, zm)
            pass_on(u, 2, chip(-1, d), *B0, yp)
            pass_on(u, 2, chip(1, d), *B1, ym)

    def stage4(u):
        arrived(u, 2, 4)
        pass_on(u, 3, chip(2, -1), *A0, zp)
        pass_on(u, 3, chip(2, 1), *A1, zm)
        pass_on(u, 3, chip(-1, 2), *B0, yp)
        pass_on(u, 3, chip(1, 2), *B1, ym)

    GROUPS = (
        (ym, yp, zm, zp),
        (chip(-1, -1), chip(-1, 1), chip(1, -1), chip(1, 1), chip(2, 0), chip(0, 2)),
        (chip(-1, 2), chip(1, 2), chip(2, -1), chip(2, 1)),
        (chip(2, 2),),
    )

    def across(group, half):
        for shard in GROUPS[group]:
            rows = pl.ds(pl.multiple_of(shard * SHARD + half * HALF, HALF), HALF)
            piece = w_v.at[HEADS + s, rows]
            send(piece, piece, x_send.at[0], x_recv.at[0, group], right)
            send(piece, piece, x_send.at[1], x_recv.at[1, group], left)

    def across_again(group):
        count = len(GROUPS[group])
        wait_bytes(w_v.at[HEADS + s_left, pl.ds(0, count * SHARD)], x_recv.at[0, group])
        wait_bytes(w_v.at[HEADS + s_right, pl.ds(0, count * SHARD)], x_recv.at[1, group])
        for shard in GROUPS[group]:
            rows = pl.ds(pl.multiple_of(shard * SHARD, SHARD), CUT)
            piece = w_v.at[HEADS + s_left, rows]
            send(piece, piece, f_send.at[0], f_recv.at[0, group], right)
            rows = pl.ds(pl.multiple_of(shard * SHARD + CUT, 128), SHARD - CUT)
            piece = w_v.at[HEADS + s_right, rows]
            send(piece, piece, f_send.at[1], f_recv.at[1, group], left)

    span_request = target_of[s]
    span_adapter = jnp.int32(0)
    for b in range(N_CTX):
        span_adapter = jnp.where(span_request == b, adapter_of[b], span_adapter)
    pick_row = lax.broadcasted_iota(jnp.int32, (ADAPTER_RANK, HD), 0)
    pick_col = lax.broadcasted_iota(jnp.int32, (ADAPTER_RANK, HD), 1)
    pick = jnp.where(pick_col == span_adapter * ADAPTER_RANK + pick_row, 1.0, 0.0).astype(BF16)

    def down_rows():
        down_load.wait()
        own = pl.ds(pl.multiple_of(c * SHARD, SHARD), SHARD)
        dt_v[:, own] = nt_dot(pick, wd_v[...]).astype(BF16)

        @pl.loop(1, N_CTX)
        def _(j):
            piece = dt_v.at[:, own]
            ctx = lax.rem(c + j, N_CTX)
            send(piece, piece, small_send.at[7], small_recv.at[7], here(ctx))

    def project_down():
        x_copy.wait()
        for load in ups:
            load.wait()
        wait_bytes(dt_v.at[:, pl.ds(0, (N_CTX - 1) * SHARD)], small_recv.at[7])
        acc[...] = jnp.zeros_like(acc)

        @pl.loop(0, 8)
        def _(i):
            part_k = pl.ds(pl.multiple_of(i * 1024, 1024), 1024)
            acc[:, 0:ADAPTER_RANK] += nt_dot(x_v[:, part_k], dt_v[:, part_k])

        down = acc[:, 0:ADAPTER_RANK].astype(BF16)
        dn[t] = jnp.dot(down, pick, preferred_element_type=F32).astype(BF16)
        send(dn.at[t], dn.at[t], small_send.at[1], small_recv.at[1], partner)

    def add(blocks, hidden_parts, rounds):
        @pl.loop(0, rounds)
        def _(i):
            parts = hidden_parts(i)
            hidden = jnp.concatenate([x_v[:, part] for part in parts], axis=1)
            weight = jnp.concatenate(
                [jnp.concatenate([w_v[n, part] for n in blocks], axis=1) for part in parts],
                axis=0,
            )
            product = jnp.dot(hidden, weight, preferred_element_type=F32)
            for j, n in enumerate(blocks):
                accs[n] += product[:, j * HD : (j + 1) * HD]

    def whole(i):
        return [pl.ds(pl.multiple_of(i * 2048, 2048), 2048)]

    def half_rows(half):
        def parts(i):
            return [
                pl.ds(pl.multiple_of((i * 8 + j) * SHARD + half * HALF, HALF), HALF)
                for j in range(8)
            ]

        return parts

    def wait_far():
        n = HEADS + s_far
        for group in range(4):
            count = len(GROUPS[group])
            wait_bytes(w_v.at[n, pl.ds(0, count * CUT)], f_recv.at[0, group])
            wait_bytes(w_v.at[n, pl.ds(0, count * (SHARD - CUT))], f_recv.at[1, group])

    def nth(p, sec):
        ahead = jnp.where(p == 0, 0, jnp.where(p == 1, n_sec - 1, jnp.where(p == 2, 1, 2)))
        is_key = (p >= 3) & (p < 3 + HEADS)
        return jnp.where(is_key, p - 3, HEADS + lax.rem(sec + ahead, n_sec))

    def project(p):
        n = nth(p, s)

        if p == 0:
            wait_bytes(dn.at[0], small_recv.at[1])

        delta = jnp.dot(dn[n // HEADS], up_v[n], preferred_element_type=F32)
        row[p] = (accs[n] + ADAPTER_SCALE * delta).astype(BF16)

    def ship(first, end):
        some = pl.ds(first, end - first)
        send(row.at[some], raw.at[some], row_send.at[first], row_recv.at[first], right)

    def exchange(first, end):
        some = pl.ds(first, end - first)
        ours = pl.ds(pl.multiple_of(c * PAIR, PAIR), PAIR)

        @pl.loop(1, N_CTX)
        def _(j):
            ctx = lax.rem(c + j, N_CTX)
            theirs = pl.ds(pl.multiple_of(ctx * PAIR, PAIR), PAIR)
            send(
                sendb.at[some, theirs],
                pages.at[some, ours],
                a_send.at[first],
                a_recv.at[first],
                here(ctx),
            )

        for p in range(first, end):
            pages[p, ours] = sendb[p, ours]

    def place(first, end):
        wait_bytes(raw.at[pl.ds(first, end - first)], row_recv.at[first])

        @pl.loop(0, 4)
        def _(i):
            some = pl.ds(pl.multiple_of(i * 256, 256), 256)
            rows = jnp.concatenate([raw[p] for p in range(first, end)], axis=1)
            placed = jnp.dot(place_m[some], rows, preferred_element_type=F32).astype(BF16)
            for j in range(end - first):
                sendb[first + j, some] = placed[:, j * HD : (j + 1) * HD]

        exchange(first, end)

    def page_rows():
        first = lax.broadcasted_iota(jnp.int32, (16, 16), 0)
        second = lax.broadcasted_iota(jnp.int32, (16, 16), 1)
        across_ids = jnp.broadcast_to(owner_of[...].astype(F32), (16, 16))
        ids = jnp.sum(jnp.where(first == second, across_ids, 0.0), axis=1, keepdims=True)
        before = (ids == across_ids) & (second < first)
        rank = jnp.sum(jnp.where(before, 1.0, 0.0), axis=1, keepdims=True)
        slot_row = (ids * 2 + rank) * BLK
        page = lax.broadcasted_iota(jnp.int32, (16, ROWS), 0)
        lane = lax.broadcasted_iota(jnp.int32, (16, ROWS), 1)
        token = lax.rem(lane, BLK).astype(F32)
        rows = jnp.sum(
            jnp.where(lane // BLK == page, slot_row + token, 0.0), axis=0, keepdims=True
        )
        drow[...] = jnp.broadcast_to(rows, (8, ROWS)).astype(jnp.int32)
        send(drow, drow_r, small_send.at[0], small_recv.at[0], right)

    def page_flags():
        wait_bytes(drow_r, small_recv.at[0])

        @pl.loop(0, 4)
        def _(i):
            some = pl.ds(pl.multiple_of(i * 256, 256), 256)
            slot_row = lax.broadcasted_iota(jnp.int32, (256, ROWS), 0) + i * 256
            hit = slot_row == drow_r[0:1]
            place_m[some] = jnp.where(hit, 1.0, 0.0).astype(BF16)
            flag = jnp.max(jnp.where(hit, 1.0, 0.0), axis=1, keepdims=True)
            sendb[8, some] = jnp.broadcast_to(flag, (256, HD)).astype(BF16)

        exchange(8, 9)

    def landed(first, end):
        some = pl.ds(first, end - first)
        wait_bytes(pages.at[some, pl.ds(0, SLOT_ROWS - PAIR)], a_recv.at[first])

    def write_out(p):
        n = nth(p, s_left)
        cols = pl.ds(pl.multiple_of(lax.rem(n, HEADS) * HD, HD), HD)

        @pl.when(n < HEADS)
        def _():
            pltpu.make_async_copy(pages.at[p], pk_out.at[:, cols], out_sem.at[p]).start()

        @pl.when(n >= HEADS)
        def _():
            pltpu.make_async_copy(pages.at[p], pv_out.at[:, cols], out_sem.at[p]).start()

    def decode_project():
        q_copy.wait()

        def blocks(product, first):
            for i in range(product.shape[1] // HD):
                part[first + i] = product[:, i * HD : (i + 1) * HD]

        hid[0:4] = xd[0].astype(F32)
        hid[4:8] = xd[1].astype(F32)
        hidden = hid[...].astype(BF16)
        part[DBLOCKS - 6 :] = jnp.zeros((6, 8, HD), F32)
        for i in range(8):
            piece = wq_v[:, i * 512 : (i + 1) * 512]
            blocks(jnp.dot(hidden, piece, preferred_element_type=F32), 4 * i)
        for n in range(BLOCKS):
            blocks(jnp.dot(hidden, w_v[n, mine], preferred_element_type=F32), 32 + n)
        part[40 + t] = jnp.dot(hidden, wd_v[...], preferred_element_type=F32)
        send(part.at[40 + t], part.at[40 + t], small_send.at[2], small_recv.at[2], partner)

    def decode_spread():
        wait_bytes(part.at[0], small_recv.at[2])

        @pl.loop(1, N_CTX)
        def _(j):
            ctx = lax.rem(c + j, N_CTX)
            send(
                part.at[pl.ds(ctx * PER, PER)],
                rsr.at[c],
                small_send.at[3],
                small_recv.at[3],
                here(ctx),
            )

        rsr[c] = part[pl.ds(c * PER, PER)]

    def decode_sum():
        wait_bytes(rsr.at[pl.ds(0, N_CTX - 1)], small_recv.at[3])
        ag[pl.ds(c * PER, PER)] = jnp.sum(rsr[...], axis=0)

        @pl.loop(1, N_CTX)
        def _(j):
            ctx = lax.rem(c + j, N_CTX)
            piece = ag.at[pl.ds(c * PER, PER)]
            send(piece, piece, small_send.at[4], small_recv.at[4], here(ctx))

    def decode_rows():
        wait_bytes(ag.at[pl.ds(0, (N_CTX - 1) * PER)], small_recv.at[4])
        to = lax.broadcasted_iota(jnp.int32, (QROWS, QROWS), 0)
        at = lax.broadcasted_iota(jnp.int32, (QROWS, QROWS), 1)
        source = lax.rem(to, 8) * 8 + lax.rem(to // 8, STEPS) * RPG + to // 16
        perm = jnp.where(at == source, 1.0, 0.0).astype(BF16)
        for k in range(HEADS):
            queries = ag[8 * k : 8 * k + 8].reshape(QROWS, HD).astype(BF16)
            qp[k] = jnp.dot(perm, queries, preferred_element_type=F32).astype(BF16)
        lane = lax.broadcasted_iota(jnp.int32, (8, HD), 1) // ADAPTER_RANK
        who = lax.rem(lax.broadcasted_iota(jnp.int32, (8, HD), 0), RPG)
        adapter = jnp.zeros((8, HD), jnp.int32)
        for b in range(RPG):
            adapter = jnp.where(who == b, adapter_of[s * RPG + b], adapter)
        for kind in range(2):
            down = ag[40 + kind].astype(BF16).astype(F32)
            picked = jnp.where(lane == adapter, down, 0.0).astype(BF16)
            for k in range(HEADS):
                n = 4 * kind + k
                delta = jnp.dot(picked, up_v[n], preferred_element_type=F32)
                tkv[n] = (ag[32 + n] + ADAPTER_SCALE * delta).astype(BF16).astype(F32)
        which = lax.broadcasted_iota(jnp.int32, (QROWS, 8), 0)
        other = lax.broadcasted_iota(jnp.int32, (QROWS, 8), 1)
        tok_live = (
            (lax.rem(other, RPG) == which // 16)
            & (other // RPG <= lax.rem(which // 8, STEPS))
            & (c == 0)
        )
        for k in range(HEADS):
            tok = nt_dot(qp[k], tkv[k].astype(BF16)) * INV_ROOT
            tok_max = jnp.max(jnp.where(tok_live, tok, NEG_FLOOR), axis=1, keepdims=True)
            tok_w = jnp.where(tok_live, jnp.exp(tok - tok_max), 0.0)
            tok_out = jnp.zeros((QROWS, HD), F32)
            for i in range(8):
                tok_out = tok_out + tok_w[:, i : i + 1] * tkv[4 + k, i : i + 1]
            pst[0, k] = jnp.broadcast_to(tok_max, (QROWS, HD))
            pst[1, k] = jnp.broadcast_to(jnp.sum(tok_w, axis=1, keepdims=True), (QROWS, HD))
            pst[2, k] = tok_out

    def merge(k, rows, block_max, total, out):
        old = pst[0, k, rows]
        top = jnp.maximum(old, block_max)
        old_scale, scale = jnp.exp(old - top), jnp.exp(block_max - top)
        pst[0, k, rows] = top
        pst[1, k, rows] = old_scale * pst[1, k, rows] + scale * total
        pst[2, k, rows] = old_scale * pst[2, k, rows] + scale * out

    def cache_block(b):
        @pl.when(b == 0)
        def _():
            k_copy.wait()
            v_copy.wait()

        left_len = length_of[b] - c * CTX_DEV
        live = lax.broadcasted_iota(jnp.int32, (16, CTX_DEV), 1) < left_len
        rows = pl.ds(pl.multiple_of(b * 16, 16), 16)
        for k in range(HEADS):
            cols = slice(k * HD, (k + 1) * HD)
            scores = nt_dot(qp[k, rows], kc_v[b, :, cols]) * INV_ROOT
            block_max = jnp.max(jnp.where(live, scores, NEG_FLOOR), axis=1, keepdims=True)
            weights = jnp.where(live, jnp.exp(scores - block_max), 0.0).astype(BF16)
            total = jnp.sum(weights.astype(F32), axis=1, keepdims=True)
            out = jnp.dot(weights, vc_v[b, :, cols], preferred_element_type=F32)
            merge(k, rows, block_max, total, out)

    page_request = target_of[s_left] - s * RPG

    def page_scores(p):
        k = nth(p, s_left)
        live = nt_dot(jnp.ones((16, HD), BF16), pages[8]) > 0.5
        query = jnp.zeros((16, HD), F32)
        for b in range(RPG):
            query = jnp.where(page_request == b, qp[k, b * 16 : b * 16 + 16].astype(F32), query)
        scores = nt_dot(query.astype(BF16), pages[p]) * INV_ROOT
        p_max = jnp.max(jnp.where(live, scores, NEG_FLOOR), axis=1, keepdims=True)
        weights = jnp.where(live, jnp.exp(scores - p_max), 0.0).astype(BF16)
        p_total = jnp.sum(weights.astype(F32), axis=1, keepdims=True)
        pgw[k] = weights
        pgs[0, k] = jnp.broadcast_to(p_max, (16, HD))
        pgs[1, k] = jnp.broadcast_to(p_total, (16, HD))

    def page_merge(p):
        k = nth(p, s_left) - HEADS
        p_out = jnp.dot(pgw[k], pages[p], preferred_element_type=F32)
        lane = lax.broadcasted_iota(jnp.int32, (16, HD), 1)
        for b in range(RPG):
            rows = slice(b * 16, b * 16 + 16)
            wanted = page_request == b
            merge(
                k,
                rows,
                jnp.where(wanted, pgs[0, k], NEG_FLOOR),
                jnp.where(wanted, pgs[1, k], 0.0),
                jnp.where(wanted, p_out, 0.0),
            )
            mgs[k * RPG + b, 0] = pst[2, k, rows]
            mgs[k * RPG + b, 1] = jnp.where(lane < 64, pst[0, k, rows], pst[1, k, rows])
            ctx = k * RPG + b

            @pl.when(ctx != c)
            def _():
                send(mgs.at[ctx], mgr.at[c], small_send.at[5], small_recv.at[5], here(ctx))

    stage1(0)
    stage1(1)
    down_rows()
    page_rows()
    accs[...] = jnp.zeros_like(accs)

    @pl.loop(2, LAST + 1)
    def _(i):
        @pl.when((i >= 6) & (i < HALVES + 6))
        def _():
            stage4(i - 6)

        @pl.when((i >= 4) & (i < HALVES + 4))
        def _():
            stage3(i - 4)

        @pl.when((i >= 2) & (i < HALVES + 2))
        def _():
            stage2(i - 2)

        @pl.when(i < HALVES)
        def _():
            stage1(i)

        @pl.when((i >= 8) & (i < HALVES + 8))
        def _():
            arrived(i - 8, 3, 1)

        for group in range(4):

            @pl.when((i == 2 + 2 * group) | (i == 3 + 2 * group))
            def _(group=group):
                across(group, lax.rem(i, 2))

        for group, at in enumerate(ACROSS_AT):

            @pl.when(i == at)
            def _(group=group):
                across_again(group)

        @pl.when(i == 4)
        def _():
            decode_project()

        @pl.when(i == 5)
        def _():
            decode_spread()

        @pl.when(i == 6)
        def _():
            page_flags()

        @pl.when(i == 7)
        def _():
            decode_sum()

        @pl.when(i == 8)
        def _():
            project_down()

        @pl.when(i == 9)
        def _():
            add((HEADS + s,), whole, 4)

        @pl.when(i == 12)
        def _():
            add((HEADS + s_left, HEADS + s_right), whole, 4)

        for at in (11, 13, 15, 17):

            @pl.when(i == at)
            def _(at=at):
                key = (at - 11) // 4 * 2
                add((key, key + 1), half_rows((at - 11) // 2 % 2), 2)

        for at, first, end in STEPS_AT:

            @pl.when(i == at)
            def _(first=first, end=end):
                for p in range(first, end):
                    project(p)
                ship(first, end)

        @pl.when(i == 9)
        def _():
            decode_rows()

        for (_, first, end), at in zip(STEPS_AT, PLACES):

            @pl.when(i == at)
            def _(first=first, end=end):
                place(first, end)

        @pl.when(i == 18)
        def _():
            landed(8, 9)

        @pl.when(i == FAR_AT)
        def _():
            wait_far()
            add((HEADS + s_far,), whole, 4)
            project(FAR)
            ship(FAR, FAR + 1)

        now, b = turn(i, CACHE_AT)

        @pl.when(now)
        def _():
            cache_block(b)

        @pl.when(i == 20)
        def _():
            place(FAR, FAR + 1)

        for (_, first, end), at in zip(STEPS_AT, LANDS):

            @pl.when(i == at)
            def _(first=first, end=end):
                landed(first, end)
                for p in range(first, end):
                    write_out(p)
                    if 3 <= p < 7:
                        page_scores(p)

    for early in (0, 1, 2):
        page_merge(early)
    landed(FAR, FAR + 1)
    page_merge(FAR)
    write_out(FAR)

    mgr[c] = mgs[c]
    wait_bytes(mgr.at[pl.ds(0, N_CTX - 1)], small_recv.at[5])
    stats = mgr[:, 1]
    tops, totals = stats[:, :, 0:1], stats[:, :, 64:65]
    scale = jnp.exp(tops - jnp.max(tops, axis=0, keepdims=True))
    numer = jnp.sum(scale * mgr[:, 0], axis=0)
    denom = jnp.sum(scale * totals, axis=0)
    att[c] = (numer / denom).astype(BF16)

    @pl.loop(1, N_CTX)
    def _(j):
        ctx = lax.rem(c + j, N_CTX)
        send(att.at[c], att.at[c], small_send.at[6], small_recv.at[6], here(ctx))

    wait_bytes(att.at[pl.ds(0, N_CTX - 1)], small_recv.at[6])
    att_out[...] = att[...]

    @pl.loop(0, HALVES)
    def _(h):
        wait_bytes(w_v.at[0, pl.ds(0, 15 * HALF)], g_send.at[h])

    for first, end in ((0, 1), (1, 3), (3, 5), (5, 7), (7, 8), (8, 9)):
        some = pl.ds(first, end - first)
        wait_bytes(sendb.at[some, pl.ds(0, SLOT_ROWS - PAIR)], a_send.at[first])
        if end < 9:
            wait_bytes(row.at[some], row_send.at[first])

    for d, count in ((0, CUT), (1, SHARD - CUT)):
        wait_bytes(w_v.at[0, pl.ds(0, 15 * SHARD)], x_send.at[d])
        wait_bytes(w_v.at[0, pl.ds(0, 15 * count)], f_send.at[d])

    @pl.loop(0, 2 * HEADS)
    def _(n):
        wait_bytes(pages.at[n], out_sem.at[n])

    wait_bytes(drow, small_send.at[0])
    wait_bytes(dn.at[0], small_send.at[1])
    wait_bytes(part.at[0], small_send.at[2])
    wait_bytes(rsr.at[pl.ds(0, N_CTX - 1)], small_send.at[3])
    wait_bytes(ag.at[pl.ds(0, (N_CTX - 1) * PER)], small_send.at[4])
    wait_bytes(mgr.at[pl.ds(0, N_CTX - 1)], small_send.at[5])
    wait_bytes(att.at[pl.ds(0, N_CTX - 1)], small_send.at[6])
    wait_bytes(dt_v.at[:, pl.ds(0, (N_CTX - 1) * SHARD)], small_send.at[7])


def finish_kernel(pk, pv, att, pk_out, pv_out, att_out, held, rows, in_sem, out_sem):
    parts = [(j, i) for i in range(4) for j in range(2)]

    def moves(j, i):
        some = pl.ds(i * (SLOT_ROWS // 4), SLOT_ROWS // 4)
        source, result = (pk, pv)[j], (pk_out, pv_out)[j]
        return (
            pltpu.make_async_copy(source.at[some], held.at[j, some], in_sem.at[j, i]),
            pltpu.make_async_copy(held.at[j, some], result.at[some], out_sem.at[j, i]),
        )

    copies = [moves(j, i) for j, i in parts]
    for into, _ in copies:
        into.start()
    for k in range(HEADS):
        for b in range(RPG):
            block = att[k * RPG + b].astype(F32)
            for step in range(STEPS):
                for g in range(8):
                    cols = slice((k * 8 + g) * HD, (k * 8 + g + 1) * HD)
                    at = step * 8 + g
                    rows[step, b : b + 1, cols] = block[at : at + 1]
    att_out[...] = rows[...].astype(BF16)
    for into, out in copies:
        into.wait()
        out.start()
    for _, out in copies:
        out.wait()


def on_device(
    prefill_hidden_states,
    decode_hidden_states,
    query_matrix,
    key_matrix,
    value_matrix,
    adapter_down_maps,
    key_adapter_up_maps,
    value_adapter_up_maps,
    request_key_cache,
    request_value_cache,
    request_adapter_index,
    prefill_request_target,
    request_context_length,
    page_owner_index,
):
    hbm = pl.BlockSpec(memory_space=pl.ANY)
    vmem = pl.BlockSpec(memory_space=pltpu.VMEM)
    smem = pl.BlockSpec(memory_space=pltpu.SMEM)
    dma = pltpu.SemaphoreType.DMA
    page_keys, page_values, attended = pl.pallas_call(
        layer_kernel,
        out_shape=(
            jax.ShapeDtypeStruct((SLOT_ROWS, HEADS * HD), BF16),
            jax.ShapeDtypeStruct((SLOT_ROWS, HEADS * HD), BF16),
            jax.ShapeDtypeStruct((N_CTX, 16, HD), BF16),
        ),
        in_specs=[smem] * 3 + [vmem] * 2 + [hbm] * 9,
        out_specs=(hbm, hbm, vmem),
        scratch_shapes=[
            pltpu.VMEM((ROWS, 8192), BF16),
            pltpu.VMEM((BLOCKS, 8192, HD), BF16),
            pltpu.VMEM((SHARD, 4096), BF16),
            pltpu.VMEM((SHARD, HD), BF16),
            pltpu.VMEM((ADAPTER_RANK, 8192), BF16),
            pltpu.VMEM((8, SHARD), F32),
            pltpu.VMEM((8, HD, HD), BF16),
            pltpu.VMEM((RPG, CTX_DEV, HEADS * HD), BF16),
            pltpu.VMEM((RPG, CTX_DEV, HEADS * HD), BF16),
            pltpu.VMEM((ROWS, HD), F32),
            pltpu.VMEM((BLOCKS, ROWS, HD), F32),
            pltpu.VMEM((2, ROWS, HD), BF16),
            pltpu.VMEM((8, ROWS, HD), BF16),
            pltpu.VMEM((8, ROWS, HD), BF16),
            pltpu.VMEM((SLOT_ROWS, ROWS), BF16),
            pltpu.VMEM((8, ROWS), jnp.int32),
            pltpu.VMEM((8, ROWS), jnp.int32),
            pltpu.VMEM((9, SLOT_ROWS, HD), BF16),
            pltpu.VMEM((9, SLOT_ROWS, HD), BF16),
            pltpu.VMEM((DBLOCKS, 8, HD), F32),
            pltpu.VMEM((N_CTX, PER, 8, HD), F32),
            pltpu.VMEM((DBLOCKS, 8, HD), F32),
            pltpu.VMEM((HEADS, QROWS, HD), BF16),
            pltpu.VMEM((8, 8, HD), F32),
            pltpu.VMEM((3, HEADS, QROWS, HD), F32),
            pltpu.VMEM((HEADS, 16, SLOT_ROWS), BF16),
            pltpu.VMEM((2, HEADS, 16, HD), F32),
            pltpu.VMEM((N_CTX, 2, 16, HD), F32),
            pltpu.VMEM((N_CTX, 2, 16, HD), F32),
            pltpu.VMEM((N_CTX, 16, HD), BF16),
            dma((9,)),
            dma,
            dma,
            dma((2,)),
            dma((8,)),
            dma((HALVES, 4)),
            dma((HALVES,)),
            dma((2, 4)),
            dma((2,)),
            dma((2, 4)),
            dma((2,)),
            dma((8,)),
            dma((8,)),
            dma((9,)),
            dma((9,)),
            dma((8,)),
            dma((8,)),
            dma((8,)),
        ],
        compiler_params=pltpu.CompilerParams(
            collective_id=0, has_side_effects=True, vmem_limit_bytes=58 * 1024 * 1024
        ),
        cost_estimate=pl.CostEstimate(
            flops=12_000_000_000, bytes_accessed=30_000_000, transcendentals=600_000
        ),
    )(
        request_adapter_index,
        prefill_request_target,
        request_context_length,
        page_owner_index.reshape(1, 16),
        decode_hidden_states,
        prefill_hidden_states,
        query_matrix,
        key_matrix,
        value_matrix,
        adapter_down_maps,
        key_adapter_up_maps,
        value_adapter_up_maps,
        request_key_cache,
        request_value_cache,
    )
    page_shape = (SLOT_ROWS // BLK, BLK, HEADS * HD)
    page_keys, page_values, attended = pl.pallas_call(
        finish_kernel,
        out_shape=(
            jax.ShapeDtypeStruct((SLOT_ROWS, HEADS * HD), BF16),
            jax.ShapeDtypeStruct((SLOT_ROWS, HEADS * HD), BF16),
            jax.ShapeDtypeStruct((STEPS, RPG, HEADS * 8 * HD), BF16),
        ),
        in_specs=[hbm, hbm, vmem],
        out_specs=(hbm, hbm, vmem),
        scratch_shapes=[
            pltpu.VMEM((2, SLOT_ROWS, HEADS * HD), BF16),
            pltpu.VMEM((STEPS, RPG, HEADS * 8 * HD), F32),
            dma((2, 4)),
            dma((2, 4)),
        ],
        compiler_params=pltpu.CompilerParams(vmem_limit_bytes=58 * 1024 * 1024),
    )(page_keys, page_values, attended)
    return (page_keys.reshape(page_shape), page_values.reshape(page_shape), attended)


def solution(mesh):
    return jax.shard_map(
        on_device,
        mesh=mesh,
        in_specs=(
            P(("section", "ctx"), None),
            P(None, "section", "ctx"),
            P("ctx", "tp"),
            P("ctx", "tp"),
            P("ctx", "tp"),
            P("ctx", "tp"),
            P(None, "tp"),
            P(None, "tp"),
            P("section", "ctx", "tp"),
            P("section", "ctx", "tp"),
            P(),
            P(),
            P("section"),
            P(("section", "ctx"), None),
        ),
        out_specs=(
            P(("section", "ctx"), None, "tp"),
            P(("section", "ctx"), None, "tp"),
            P(None, "section", "tp"),
        ),
        check_vma=False,
    )
```

```python
import functools

import jax
import jax.numpy as jnp
from jax import lax
from jax.experimental import pallas as pl
from jax.experimental.pallas import tpu as pltpu
from jax.sharding import PartitionSpec as P

H = 64
KVH = 8
HD = 128
ADAPTER_RANK = 16
BLK = 32
STEPS = 2

ADAPTER_SCALE = 0.5
CUT = 128
NEG_FLOOR = -1e30
INV_ROOT = HD ** (-0.5)

SIDE = 4
N_CTX = 16
SHARD = 512
UNITS = 5
HALVES = 2 * UNITS
HALF = 256
BLOCKS = 8
HEADS = 4
ROWS = 512
SLOT_ROWS = 1024
FLAG_ROWS = 256
PAIR = 64
RPG = 4
CTX_DEV = 1024
QROWS = 64
DBLOCKS = 48
PER = 3

STEPS_AT = ((9, 0, 1), (12, 1, 3), (13, 3, 5), (17, 5, 7))
PLACES = (13, 15, 17, 19)
LANDS = (18, 19, 20, 21)
FAR = 7
PLACE_LAG = 2
LAND_LAG = 6
CACHE_AT = (18, 19, 20, 21)
ACROSS_AT = (9, 11, 12, 12)
FAR_AT = 18
LAST = 21

MESH = pl.DeviceIdType.MESH
F32 = jnp.float32
BF16 = jnp.bfloat16


def wait_bytes(ref, sem):
    pltpu.make_async_copy(ref, ref, sem).wait()


def turn(i, slots):
    here, which = False, -1
    for at in slots:
        here = here | (i == at)
        which = which + jnp.where(i >= at, 1, 0)
    return here, which


def nt_dot(a, b):
    return lax.dot_general(a, b, (((1,), (1,)), ((), ())), preferred_element_type=F32)


def layer_kernel(
    adapter_of,
    target_of,
    length_of,
    owner_of,
    xd,
    x_hbm,
    wq_hbm,
    wk_hbm,
    wv_hbm,
    wd_hbm,
    uk_hbm,
    uv_hbm,
    kc_hbm,
    vc_hbm,
    pk_out,
    pv_out,
    att_out,
    x_v,
    w_v,
    wq_v,
    wd_v,
    dt_v,
    hid,
    up_v,
    kc_v,
    vc_v,
    acc,
    accs,
    dn,
    row,
    raw,
    place_m,
    drow,
    drow_r,
    sendb,
    pages,
    flag_s,
    flag_r,
    live_v,
    part,
    rsr,
    ag,
    qp,
    tkv,
    pst,
    pgw,
    pgs,
    mgs,
    mgr,
    att,
    w_load,
    q_load,
    x_load,
    c_load,
    u_load,
    g_recv,
    g_send,
    x_recv,
    x_send,
    f_recv,
    f_send,
    row_send,
    row_recv,
    a_send,
    a_recv,
    small_send,
    small_recv,
    out_sem,
):
    s = lax.axis_index("section")
    c = lax.axis_index("ctx")
    t = lax.axis_index("tp")
    n_sec = lax.axis_size("section")
    y = c // SIDE
    z = lax.rem(c, SIDE)

    def chip(dy, dz):
        return lax.rem(y + dy + SIDE, SIDE) * SIDE + lax.rem(z + dz + SIDE, SIDE)

    def here(ctx):
        return (s, ctx, t)

    right = (lax.rem(s + 1, n_sec), c, t)
    left = (lax.rem(s + n_sec - 1, n_sec), c, t)
    partner = (s, c, 1 - t)
    s_left = lax.rem(s + n_sec - 1, n_sec)
    s_right = lax.rem(s + 1, n_sec)
    s_far = lax.rem(s + 2, n_sec)

    barrier = pltpu.get_barrier_semaphore()

    @pl.loop(1, N_CTX)
    def _(j):
        pl.semaphore_signal(
            barrier, inc=1, device_id=here(lax.rem(c + j, N_CTX)), device_id_type=MESH
        )

    for peer in (left, right, partner):
        pl.semaphore_signal(barrier, inc=1, device_id=peer, device_id_type=MESH)

    mine = pl.ds(pl.multiple_of(c * SHARD, SHARD), SHARD)
    shard_loads = []
    for n, hbm in enumerate([wk_hbm] * HEADS + [wv_hbm] * HEADS):
        cols = pl.ds(n % HEADS * HD, HD)
        shard_loads.append(
            pltpu.make_async_copy(hbm.at[:, cols], w_v.at[n, mine], w_load.at[n])
        )
    down_load = pltpu.make_async_copy(wd_hbm, wd_v, w_load.at[8])
    down_load.start()
    for load in shard_loads:
        load.start()
    q_copy = pltpu.make_async_copy(wq_hbm, wq_v, q_load)
    q_copy.start()
    ups = []
    for h in range(HEADS):
        cols = pl.ds(h * HD, HD)
        ups.append(pltpu.make_async_copy(uk_hbm.at[:, cols], up_v.at[h], u_load.at[h]))
        ups.append(pltpu.make_async_copy(uv_hbm.at[:, cols], up_v.at[4 + h], u_load.at[4 + h]))
    for load in ups:
        load.start()
    x_copy = pltpu.make_async_copy(x_hbm, x_v, x_load)
    x_copy.start()
    k_copy = pltpu.make_async_copy(kc_hbm, kc_v, c_load.at[0])
    v_copy = pltpu.make_async_copy(vc_hbm, vc_v, c_load.at[1])
    k_copy.start()
    v_copy.start()

    pl.semaphore_wait(barrier, N_CTX + 2)

    def send(src, dst, send_sem, recv_sem, device):
        pltpu.make_async_remote_copy(
            src_ref=src,
            dst_ref=dst,
            send_sem=send_sem,
            recv_sem=recv_sem,
            device_id=device,
            device_id_type=MESH,
        ).start()

    for load in shard_loads:
        load.wait()

    def block_of(h):
        key = (h - 2) // 4 * 2 + lax.rem(h, 2)
        return jnp.where(h < 2, HEADS + s, key)

    def half_of(h):
        return jnp.where(h < 2, h, lax.rem((h - 2) // 2, 2))

    def pass_on(h, stage, shard, first, count, ctx):
        start = shard * SHARD + half_of(h) * HALF + first
        piece = w_v.at[block_of(h), pl.ds(pl.multiple_of(start, 64), count)]
        send(piece, piece, g_send.at[h], g_recv.at[h, stage], here(ctx))

    def arrived(h, stage, shards):
        wait_bytes(w_v.at[block_of(h), pl.ds(0, shards * HALF)], g_recv.at[h, stage])

    yp, ym, zp, zm = chip(1, 0), chip(-1, 0), chip(0, 1), chip(0, -1)
    A, B, A0, A1, B0, B1, ZERO = (
        (0, 128),
        (128, 128),
        (64, 64),
        (0, 64),
        (128, 64),
        (192, 64),
        (64, 128),
    )

    def stage1(u):
        for ctx in (yp, zp, ym, zm):
            pass_on(u, 0, c, 0, HALF, ctx)

    def stage2(u):
        arrived(u, 0, 4)
        pass_on(u, 1, ym, *ZERO, yp)
        pass_on(u, 1, yp, *A1, ym)
        pass_on(u, 1, yp, *B1, ym)
        pass_on(u, 1, zm, *ZERO, zp)
        pass_on(u, 1, zp, *A1, zm)
        pass_on(u, 1, zp, *B1, zm)
        for shard in (ym, yp):
            for ctx in (zp, zm):
                pass_on(u, 1, shard, *A, ctx)
        for shard in (zm, zp):
            for ctx in (yp, ym):
                pass_on(u, 1, shard, *B, ctx)

    def stage3(u):
        arrived(u, 1, 6)
        yy, zz = chip(2, 0), chip(0, 2)
        for ctx in (zp, zm):
            pass_on(u, 2, yy, *A, ctx)
        for ctx in (yp, ym):
            pass_on(u, 2, zz, *B, ctx)
        for d in (-1, 1):
            pass_on(u, 2, chip(d, -1), *A0, zp)
            pass_on(u, 2, chip(d, 1), *A1, zm)
            pass_on(u, 2, chip(-1, d), *B0, yp)
            pass_on(u, 2, chip(1, d), *B1, ym)

    def stage4(u):
        arrived(u, 2, 4)
        pass_on(u, 3, chip(2, -1), *A0, zp)
        pass_on(u, 3, chip(2, 1), *A1, zm)
        pass_on(u, 3, chip(-1, 2), *B0, yp)
        pass_on(u, 3, chip(1, 2), *B1, ym)

    GROUPS = (
        (ym, yp, zm, zp),
        (chip(-1, -1), chip(-1, 1), chip(1, -1), chip(1, 1), chip(2, 0), chip(0, 2)),
        (chip(-1, 2), chip(1, 2), chip(2, -1), chip(2, 1)),
        (chip(2, 2),),
    )

    def across(group, half):
        for shard in GROUPS[group]:
            rows = pl.ds(pl.multiple_of(shard * SHARD + half * HALF, HALF), HALF)
            piece = w_v.at[HEADS + s, rows]
            send(piece, piece, x_send.at[0], x_recv.at[0, group], right)
            send(piece, piece, x_send.at[1], x_recv.at[1, group], left)

    def across_again(group):
        count = len(GROUPS[group])
        wait_bytes(w_v.at[HEADS + s_left, pl.ds(0, count * SHARD)], x_recv.at[0, group])
        wait_bytes(w_v.at[HEADS + s_right, pl.ds(0, count * SHARD)], x_recv.at[1, group])
        for shard in GROUPS[group]:
            rows = pl.ds(pl.multiple_of(shard * SHARD, SHARD), CUT)
            piece = w_v.at[HEADS + s_left, rows]
            send(piece, piece, f_send.at[0], f_recv.at[0, group], right)
            rows = pl.ds(pl.multiple_of(shard * SHARD + CUT, 128), SHARD - CUT)
            piece = w_v.at[HEADS + s_right, rows]
            send(piece, piece, f_send.at[1], f_recv.at[1, group], left)

    span_request = target_of[s]
    span_adapter = jnp.int32(0)
    for b in range(N_CTX):
        span_adapter = jnp.where(span_request == b, adapter_of[b], span_adapter)
    pick_row = lax.broadcasted_iota(jnp.int32, (ADAPTER_RANK, HD), 0)
    pick_col = lax.broadcasted_iota(jnp.int32, (ADAPTER_RANK, HD), 1)
    pick = jnp.where(pick_col == span_adapter * ADAPTER_RANK + pick_row, 1.0, 0.0).astype(BF16)

    def down_rows():
        down_load.wait()
        own = pl.ds(pl.multiple_of(c * SHARD, SHARD), SHARD)
        dt_v[:, own] = nt_dot(pick, wd_v[...]).astype(BF16)

        @pl.loop(1, N_CTX)
        def _(j):
            piece = dt_v.at[:, own]
            ctx = lax.rem(c + j, N_CTX)
            send(piece, piece, small_send.at[7], small_recv.at[7], here(ctx))

    def project_down():
        x_copy.wait()
        for load in ups:
            load.wait()
        wait_bytes(dt_v.at[:, pl.ds(0, (N_CTX - 1) * SHARD)], small_recv.at[7])
        acc[...] = jnp.zeros_like(acc)

        @pl.loop(0, 8)
        def _(i):
            part_k = pl.ds(pl.multiple_of(i * 1024, 1024), 1024)
            acc[:, 0:ADAPTER_RANK] += nt_dot(x_v[:, part_k], dt_v[:, part_k])

        down = acc[:, 0:ADAPTER_RANK].astype(BF16)
        dn[t] = jnp.dot(down, pick, preferred_element_type=F32).astype(BF16)
        send(dn.at[t], dn.at[t], small_send.at[1], small_recv.at[1], partner)

    def add(blocks, hidden_parts, rounds):
        @pl.loop(0, rounds)
        def _(i):
            parts = hidden_parts(i)
            hidden = jnp.concatenate([x_v[:, part] for part in parts], axis=1)
            weight = jnp.concatenate(
                [jnp.concatenate([w_v[n, part] for n in blocks], axis=1) for part in parts],
                axis=0,
            )
            product = jnp.dot(hidden, weight, preferred_element_type=F32)
            for j, n in enumerate(blocks):
                accs[n] += product[:, j * HD : (j + 1) * HD]

    def whole(i):
        return [pl.ds(pl.multiple_of(i * 2048, 2048), 2048)]

    def half_rows(half):
        def parts(i):
            return [
                pl.ds(pl.multiple_of((i * 8 + j) * SHARD + half * HALF, HALF), HALF)
                for j in range(8)
            ]

        return parts

    def wait_far():
        n = HEADS + s_far
        for group in range(4):
            count = len(GROUPS[group])
            wait_bytes(w_v.at[n, pl.ds(0, count * CUT)], f_recv.at[0, group])
            wait_bytes(w_v.at[n, pl.ds(0, count * (SHARD - CUT))], f_recv.at[1, group])

    def nth(p, sec):
        ahead = jnp.where(p == 0, 0, jnp.where(p == 1, n_sec - 1, jnp.where(p == 2, 1, 2)))
        is_key = (p >= 3) & (p < 3 + HEADS)
        return jnp.where(is_key, p - 3, HEADS + lax.rem(sec + ahead, n_sec))

    def project(p):
        n = nth(p, s)

        if p == 0:
            wait_bytes(dn.at[0], small_recv.at[1])

        delta = jnp.dot(dn[n // HEADS], up_v[n], preferred_element_type=F32)
        row[p] = (accs[n] + ADAPTER_SCALE * delta).astype(BF16)

    def ship(first, end):
        some = pl.ds(first, end - first)
        send(row.at[some], raw.at[some], row_send.at[first], row_recv.at[first], right)

    def exchange(first, end):
        some = pl.ds(first, end - first)
        ours = pl.ds(pl.multiple_of(c * PAIR, PAIR), PAIR)

        @pl.loop(1, N_CTX)
        def _(j):
            ctx = lax.rem(c + j, N_CTX)
            theirs = pl.ds(pl.multiple_of(ctx * PAIR, PAIR), PAIR)
            send(
                sendb.at[some, theirs],
                pages.at[some, ours],
                a_send.at[first],
                a_recv.at[first],
                here(ctx),
            )

        for p in range(first, end):
            pages[p, ours] = sendb[p, ours]

    def place(first, end):
        wait_bytes(raw.at[pl.ds(first, end - first)], row_recv.at[first])

        @pl.loop(0, 4)
        def _(i):
            some = pl.ds(pl.multiple_of(i * 256, 256), 256)
            rows = jnp.concatenate([raw[p] for p in range(first, end)], axis=1)
            placed = jnp.dot(place_m[some], rows, preferred_element_type=F32).astype(BF16)
            for j in range(end - first):
                sendb[first + j, some] = placed[:, j * HD : (j + 1) * HD]

        exchange(first, end)

    def page_rows():
        first = lax.broadcasted_iota(jnp.int32, (16, 16), 0)
        second = lax.broadcasted_iota(jnp.int32, (16, 16), 1)
        across_ids = jnp.broadcast_to(owner_of[...].astype(F32), (16, 16))
        ids = jnp.sum(jnp.where(first == second, across_ids, 0.0), axis=1, keepdims=True)
        before = (ids == across_ids) & (second < first)
        rank = jnp.sum(jnp.where(before, 1.0, 0.0), axis=1, keepdims=True)
        slot_row = (ids * 2 + rank) * BLK
        page = lax.broadcasted_iota(jnp.int32, (16, ROWS), 0)
        lane = lax.broadcasted_iota(jnp.int32, (16, ROWS), 1)
        token = lax.rem(lane, BLK).astype(F32)
        rows = jnp.sum(
            jnp.where(lane // BLK == page, slot_row + token, 0.0), axis=0, keepdims=True
        )
        drow[...] = jnp.broadcast_to(rows, (8, ROWS)).astype(jnp.int32)
        send(drow, drow_r, small_send.at[0], small_recv.at[0], right)

    def page_flags():
        wait_bytes(drow_r, small_recv.at[0])

        @pl.loop(0, 4)
        def _(i):
            some = pl.ds(pl.multiple_of(i * 256, 256), 256)
            slot_row = lax.broadcasted_iota(jnp.int32, (256, ROWS), 0) + i * 256
            hit = slot_row == drow_r[0:1]
            place_m[some] = jnp.where(hit, 1.0, 0.0).astype(BF16)

        slot = lax.broadcasted_iota(jnp.int32, (FLAG_ROWS, ROWS), 0) // 8
        taken = jnp.where(drow_r[0:1] == slot * BLK, 1.0, 0.0)
        flag = jnp.max(taken, axis=1, keepdims=True)
        flag_s[...] = jnp.broadcast_to(flag, (FLAG_ROWS, HD)).astype(BF16)
        ours = pl.ds(pl.multiple_of(c * 16, 16), 16)

        @pl.loop(1, N_CTX)
        def _(j):
            ctx = lax.rem(c + j, N_CTX)
            theirs = pl.ds(pl.multiple_of(ctx * 16, 16), 16)
            send(flag_s.at[theirs], flag_r.at[ours], a_send.at[8], a_recv.at[8], here(ctx))

        flag_r[ours] = flag_s[ours]

    def page_live():
        wait_bytes(flag_r.at[pl.ds(0, FLAG_ROWS - 16)], a_recv.at[8])
        flags = nt_dot(jnp.ones((16, HD), BF16), flag_r[...]).astype(BF16)
        at = lax.broadcasted_iota(jnp.int32, (FLAG_ROWS, SLOT_ROWS), 0)
        to = lax.broadcasted_iota(jnp.int32, (FLAG_ROWS, SLOT_ROWS), 1)
        spread = jnp.where((lax.rem(at, 8) == 0) & (at // 8 == to // BLK), 1.0, 0.0)
        live_v[...] = jnp.dot(flags, spread.astype(BF16), preferred_element_type=F32)

    def landed(first, end):
        some = pl.ds(first, end - first)
        wait_bytes(pages.at[some, pl.ds(0, SLOT_ROWS - PAIR)], a_recv.at[first])

    def write_out(p):
        n = nth(p, s_left)
        cols = pl.ds(pl.multiple_of(lax.rem(n, HEADS) * HD, HD), HD)

        @pl.when(n < HEADS)
        def _():
            pltpu.make_async_copy(pages.at[p], pk_out.at[:, cols], out_sem.at[p]).start()

        @pl.when(n >= HEADS)
        def _():
            pltpu.make_async_copy(pages.at[p], pv_out.at[:, cols], out_sem.at[p]).start()

    def decode_project():
        q_copy.wait()

        def blocks(product, first):
            for i in range(product.shape[1] // HD):
                part[first + i] = product[:, i * HD : (i + 1) * HD]

        hid[0:4] = xd[0].astype(F32)
        hid[4:8] = xd[1].astype(F32)
        hidden = hid[...].astype(BF16)
        part[DBLOCKS - 6 :] = jnp.zeros((6, 8, HD), F32)
        for i in range(8):
            piece = wq_v[:, i * 512 : (i + 1) * 512]
            blocks(jnp.dot(hidden, piece, preferred_element_type=F32), 4 * i)
        for n in range(BLOCKS):
            blocks(jnp.dot(hidden, w_v[n, mine], preferred_element_type=F32), 32 + n)
        part[40 + t] = jnp.dot(hidden, wd_v[...], preferred_element_type=F32)
        send(part.at[40 + t], part.at[40 + t], small_send.at[2], small_recv.at[2], partner)

    def decode_spread():
        wait_bytes(part.at[0], small_recv.at[2])

        @pl.loop(1, N_CTX)
        def _(j):
            ctx = lax.rem(c + j, N_CTX)
            send(
                part.at[pl.ds(ctx * PER, PER)],
                rsr.at[c],
                small_send.at[3],
                small_recv.at[3],
                here(ctx),
            )

        rsr[c] = part[pl.ds(c * PER, PER)]

    def decode_sum():
        wait_bytes(rsr.at[pl.ds(0, N_CTX - 1)], small_recv.at[3])
        ag[pl.ds(c * PER, PER)] = jnp.sum(rsr[...], axis=0)

        @pl.loop(1, N_CTX)
        def _(j):
            ctx = lax.rem(c + j, N_CTX)
            piece = ag.at[pl.ds(c * PER, PER)]
            send(piece, piece, small_send.at[4], small_recv.at[4], here(ctx))

    def decode_rows():
        wait_bytes(ag.at[pl.ds(0, (N_CTX - 1) * PER)], small_recv.at[4])
        to = lax.broadcasted_iota(jnp.int32, (QROWS, QROWS), 0)
        at = lax.broadcasted_iota(jnp.int32, (QROWS, QROWS), 1)
        source = lax.rem(to, 8) * 8 + lax.rem(to // 8, STEPS) * RPG + to // 16
        perm = jnp.where(at == source, 1.0, 0.0).astype(BF16)
        for k in range(HEADS):
            queries = ag[8 * k : 8 * k + 8].reshape(QROWS, HD).astype(BF16)
            qp[k] = jnp.dot(perm, queries, preferred_element_type=F32).astype(BF16)
        lane = lax.broadcasted_iota(jnp.int32, (8, HD), 1) // ADAPTER_RANK
        who = lax.rem(lax.broadcasted_iota(jnp.int32, (8, HD), 0), RPG)
        adapter = jnp.zeros((8, HD), jnp.int32)
        for b in range(RPG):
            adapter = jnp.where(who == b, adapter_of[s * RPG + b], adapter)
        for kind in range(2):
            down = ag[40 + kind].astype(BF16).astype(F32)
            picked = jnp.where(lane == adapter, down, 0.0).astype(BF16)
            for k in range(HEADS):
                n = 4 * kind + k
                delta = jnp.dot(picked, up_v[n], preferred_element_type=F32)
                tkv[n] = (ag[32 + n] + ADAPTER_SCALE * delta).astype(BF16).astype(F32)
        which = lax.broadcasted_iota(jnp.int32, (QROWS, 8), 0)
        other = lax.broadcasted_iota(jnp.int32, (QROWS, 8), 1)
        tok_live = (
            (lax.rem(other, RPG) == which // 16)
            & (other // RPG <= lax.rem(which // 8, STEPS))
            & (c == 0)
        )
        for k in range(HEADS):
            tok = nt_dot(qp[k], tkv[k].astype(BF16)) * INV_ROOT
            tok_max = jnp.max(jnp.where(tok_live, tok, NEG_FLOOR), axis=1, keepdims=True)
            tok_w = jnp.where(tok_live, jnp.exp(tok - tok_max), 0.0)
            tok_out = jnp.zeros((QROWS, HD), F32)
            for i in range(8):
                tok_out = tok_out + tok_w[:, i : i + 1] * tkv[4 + k, i : i + 1]
            pst[0, k] = jnp.broadcast_to(tok_max, (QROWS, HD))
            pst[1, k] = jnp.broadcast_to(jnp.sum(tok_w, axis=1, keepdims=True), (QROWS, HD))
            pst[2, k] = tok_out

    def merge(k, rows, block_max, total, out):
        old = pst[0, k, rows]
        top = jnp.maximum(old, block_max)
        old_scale, scale = jnp.exp(old - top), jnp.exp(block_max - top)
        pst[0, k, rows] = top
        pst[1, k, rows] = old_scale * pst[1, k, rows] + scale * total
        pst[2, k, rows] = old_scale * pst[2, k, rows] + scale * out

    def cache_block(b):
        @pl.when(b == 0)
        def _():
            k_copy.wait()
            v_copy.wait()

        left_len = length_of[b] - c * CTX_DEV
        live = lax.broadcasted_iota(jnp.int32, (16, CTX_DEV), 1) < left_len
        rows = pl.ds(pl.multiple_of(b * 16, 16), 16)
        for k in range(HEADS):
            cols = slice(k * HD, (k + 1) * HD)
            scores = nt_dot(qp[k, rows], kc_v[b, :, cols]) * INV_ROOT
            block_max = jnp.max(jnp.where(live, scores, NEG_FLOOR), axis=1, keepdims=True)
            weights = jnp.where(live, jnp.exp(scores - block_max), 0.0).astype(BF16)
            total = jnp.sum(weights.astype(F32), axis=1, keepdims=True)
            out = jnp.dot(weights, vc_v[b, :, cols], preferred_element_type=F32)
            merge(k, rows, block_max, total, out)

    page_request = target_of[s_left] - s * RPG

    def page_scores(p):
        k = nth(p, s_left)
        live = live_v[...] > 0.5
        query = jnp.zeros((16, HD), F32)
        for b in range(RPG):
            query = jnp.where(page_request == b, qp[k, b * 16 : b * 16 + 16].astype(F32), query)
        scores = nt_dot(query.astype(BF16), pages[p]) * INV_ROOT
        p_max = jnp.max(jnp.where(live, scores, NEG_FLOOR), axis=1, keepdims=True)
        weights = jnp.where(live, jnp.exp(scores - p_max), 0.0).astype(BF16)
        p_total = jnp.sum(weights.astype(F32), axis=1, keepdims=True)
        pgw[k] = weights
        pgs[0, k] = jnp.broadcast_to(p_max, (16, HD))
        pgs[1, k] = jnp.broadcast_to(p_total, (16, HD))

    def page_merge(p):
        k = nth(p, s_left) - HEADS
        p_out = jnp.dot(pgw[k], pages[p], preferred_element_type=F32)
        lane = lax.broadcasted_iota(jnp.int32, (16, HD), 1)
        for b in range(RPG):
            rows = slice(b * 16, b * 16 + 16)
            wanted = page_request == b
            merge(
                k,
                rows,
                jnp.where(wanted, pgs[0, k], NEG_FLOOR),
                jnp.where(wanted, pgs[1, k], 0.0),
                jnp.where(wanted, p_out, 0.0),
            )
            mgs[k * RPG + b, 0] = pst[2, k, rows]
            mgs[k * RPG + b, 1] = jnp.where(lane < 64, pst[0, k, rows], pst[1, k, rows])
            ctx = k * RPG + b

            @pl.when(ctx != c)
            def _():
                send(mgs.at[ctx], mgr.at[c], small_send.at[5], small_recv.at[5], here(ctx))

    stage1(0)
    stage1(1)
    down_rows()
    page_rows()
    accs[...] = jnp.zeros_like(accs)

    @pl.loop(2, LAST + 1)
    def _(i):
        @pl.when((i >= 6) & (i < HALVES + 6))
        def _():
            stage4(i - 6)

        @pl.when((i >= 4) & (i < HALVES + 4))
        def _():
            stage3(i - 4)

        @pl.when((i >= 2) & (i < HALVES + 2))
        def _():
            stage2(i - 2)

        @pl.when(i < HALVES)
        def _():
            stage1(i)

        @pl.when((i >= 8) & (i < HALVES + 8))
        def _():
            arrived(i - 8, 3, 1)

        for group in range(4):

            @pl.when((i == 2 + 2 * group) | (i == 3 + 2 * group))
            def _(group=group):
                across(group, lax.rem(i, 2))

        for group, at in enumerate(ACROSS_AT):

            @pl.when(i == at)
            def _(group=group):
                across_again(group)

        @pl.when(i == 4)
        def _():
            decode_project()

        @pl.when(i == 5)
        def _():
            decode_spread()

        @pl.when(i == 6)
        def _():
            page_flags()

        @pl.when(i == 7)
        def _():
            decode_sum()

        @pl.when(i == 8)
        def _():
            project_down()

        @pl.when(i == 9)
        def _():
            add((HEADS + s,), whole, 4)

        @pl.when(i == 12)
        def _():
            add((HEADS + s_left, HEADS + s_right), whole, 4)

        for at in (11, 13, 15, 17):

            @pl.when(i == at)
            def _(at=at):
                key = (at - 11) // 4 * 2
                add((key, key + 1), half_rows((at - 11) // 2 % 2), 2)

        for at, first, end in STEPS_AT:

            @pl.when(i == at)
            def _(first=first, end=end):
                for p in range(first, end):
                    project(p)
                ship(first, end)

        @pl.when(i == 9)
        def _():
            decode_rows()

        for (_, first, end), at in zip(STEPS_AT, PLACES):

            @pl.when(i == at)
            def _(first=first, end=end):
                place(first, end)

        @pl.when(i == 18)
        def _():
            page_live()

        @pl.when(i == FAR_AT)
        def _():
            wait_far()
            add((HEADS + s_far,), whole, 4)
            project(FAR)
            ship(FAR, FAR + 1)

        now, b = turn(i, CACHE_AT)

        @pl.when(now)
        def _():
            cache_block(b)

        @pl.when(i == 20)
        def _():
            place(FAR, FAR + 1)

        for (_, first, end), at in zip(STEPS_AT, LANDS):

            @pl.when(i == at)
            def _(first=first, end=end):
                landed(first, end)
                for p in range(first, end):
                    write_out(p)
                    if 3 <= p < 7:
                        page_scores(p)

    for early in (0, 1, 2):
        page_merge(early)
    landed(FAR, FAR + 1)
    page_merge(FAR)
    write_out(FAR)

    mgr[c] = mgs[c]
    wait_bytes(mgr.at[pl.ds(0, N_CTX - 1)], small_recv.at[5])
    stats = mgr[:, 1]
    tops, totals = stats[:, :, 0:1], stats[:, :, 64:65]
    scale = jnp.exp(tops - jnp.max(tops, axis=0, keepdims=True))
    numer = jnp.sum(scale * mgr[:, 0], axis=0)
    denom = jnp.sum(scale * totals, axis=0)
    att[c] = (numer / denom).astype(BF16)

    @pl.loop(1, N_CTX)
    def _(j):
        ctx = lax.rem(c + j, N_CTX)
        send(att.at[c], att.at[c], small_send.at[6], small_recv.at[6], here(ctx))

    wait_bytes(att.at[pl.ds(0, N_CTX - 1)], small_recv.at[6])
    att_out[...] = att[...]

    @pl.loop(0, HALVES)
    def _(h):
        wait_bytes(w_v.at[0, pl.ds(0, 15 * HALF)], g_send.at[h])

    for first, end in ((0, 1), (1, 3), (3, 5), (5, 7), (7, 8)):
        some = pl.ds(first, end - first)
        wait_bytes(sendb.at[some, pl.ds(0, SLOT_ROWS - PAIR)], a_send.at[first])
        wait_bytes(row.at[some], row_send.at[first])

    wait_bytes(flag_s.at[pl.ds(0, FLAG_ROWS - 16)], a_send.at[8])

    for d, count in ((0, CUT), (1, SHARD - CUT)):
        wait_bytes(w_v.at[0, pl.ds(0, 15 * SHARD)], x_send.at[d])
        wait_bytes(w_v.at[0, pl.ds(0, 15 * count)], f_send.at[d])

    @pl.loop(0, 2 * HEADS)
    def _(n):
        wait_bytes(pages.at[n], out_sem.at[n])

    wait_bytes(drow, small_send.at[0])
    wait_bytes(dn.at[0], small_send.at[1])
    wait_bytes(part.at[0], small_send.at[2])
    wait_bytes(rsr.at[pl.ds(0, N_CTX - 1)], small_send.at[3])
    wait_bytes(ag.at[pl.ds(0, (N_CTX - 1) * PER)], small_send.at[4])
    wait_bytes(mgr.at[pl.ds(0, N_CTX - 1)], small_send.at[5])
    wait_bytes(att.at[pl.ds(0, N_CTX - 1)], small_send.at[6])
    wait_bytes(dt_v.at[:, pl.ds(0, (N_CTX - 1) * SHARD)], small_send.at[7])


def finish_kernel(pk, pv, att, pk_out, pv_out, att_out, held, rows, in_sem, out_sem):
    parts = [(j, i) for i in range(4) for j in range(2)]

    def moves(j, i):
        some = pl.ds(i * (SLOT_ROWS // 4), SLOT_ROWS // 4)
        source, result = (pk, pv)[j], (pk_out, pv_out)[j]
        return (
            pltpu.make_async_copy(source.at[some], held.at[j, some], in_sem.at[j, i]),
            pltpu.make_async_copy(held.at[j, some], result.at[some], out_sem.at[j, i]),
        )

    copies = [moves(j, i) for j, i in parts]
    for into, _ in copies:
        into.start()
    for k in range(HEADS):
        for b in range(RPG):
            block = att[k * RPG + b].astype(F32)
            for step in range(STEPS):
                for g in range(8):
                    cols = slice((k * 8 + g) * HD, (k * 8 + g + 1) * HD)
                    at = step * 8 + g
                    rows[step, b : b + 1, cols] = block[at : at + 1]
    att_out[...] = rows[...].astype(BF16)
    for into, out in copies:
        into.wait()
        out.start()
    for _, out in copies:
        out.wait()


def on_device(
    prefill_hidden_states,
    decode_hidden_states,
    query_matrix,
    key_matrix,
    value_matrix,
    adapter_down_maps,
    key_adapter_up_maps,
    value_adapter_up_maps,
    request_key_cache,
    request_value_cache,
    request_adapter_index,
    prefill_request_target,
    request_context_length,
    page_owner_index,
):
    hbm = pl.BlockSpec(memory_space=pl.ANY)
    vmem = pl.BlockSpec(memory_space=pltpu.VMEM)
    smem = pl.BlockSpec(memory_space=pltpu.SMEM)
    dma = pltpu.SemaphoreType.DMA
    page_keys, page_values, attended = pl.pallas_call(
        layer_kernel,
        out_shape=(
            jax.ShapeDtypeStruct((SLOT_ROWS, HEADS * HD), BF16),
            jax.ShapeDtypeStruct((SLOT_ROWS, HEADS * HD), BF16),
            jax.ShapeDtypeStruct((N_CTX, 16, HD), BF16),
        ),
        in_specs=[smem] * 3 + [vmem] * 2 + [hbm] * 9,
        out_specs=(hbm, hbm, vmem),
        scratch_shapes=[
            pltpu.VMEM((ROWS, 8192), BF16),
            pltpu.VMEM((BLOCKS, 8192, HD), BF16),
            pltpu.VMEM((SHARD, 4096), BF16),
            pltpu.VMEM((SHARD, HD), BF16),
            pltpu.VMEM((ADAPTER_RANK, 8192), BF16),
            pltpu.VMEM((8, SHARD), F32),
            pltpu.VMEM((8, HD, HD), BF16),
            pltpu.VMEM((RPG, CTX_DEV, HEADS * HD), BF16),
            pltpu.VMEM((RPG, CTX_DEV, HEADS * HD), BF16),
            pltpu.VMEM((ROWS, HD), F32),
            pltpu.VMEM((BLOCKS, ROWS, HD), F32),
            pltpu.VMEM((2, ROWS, HD), BF16),
            pltpu.VMEM((8, ROWS, HD), BF16),
            pltpu.VMEM((8, ROWS, HD), BF16),
            pltpu.VMEM((SLOT_ROWS, ROWS), BF16),
            pltpu.VMEM((8, ROWS), jnp.int32),
            pltpu.VMEM((8, ROWS), jnp.int32),
            pltpu.VMEM((BLOCKS, SLOT_ROWS, HD), BF16),
            pltpu.VMEM((BLOCKS, SLOT_ROWS, HD), BF16),
            pltpu.VMEM((FLAG_ROWS, HD), BF16),
            pltpu.VMEM((FLAG_ROWS, HD), BF16),
            pltpu.VMEM((16, SLOT_ROWS), F32),
            pltpu.VMEM((DBLOCKS, 8, HD), F32),
            pltpu.VMEM((N_CTX, PER, 8, HD), F32),
            pltpu.VMEM((DBLOCKS, 8, HD), F32),
            pltpu.VMEM((HEADS, QROWS, HD), BF16),
            pltpu.VMEM((8, 8, HD), F32),
            pltpu.VMEM((3, HEADS, QROWS, HD), F32),
            pltpu.VMEM((HEADS, 16, SLOT_ROWS), BF16),
            pltpu.VMEM((2, HEADS, 16, HD), F32),
            pltpu.VMEM((N_CTX, 2, 16, HD), F32),
            pltpu.VMEM((N_CTX, 2, 16, HD), F32),
            pltpu.VMEM((N_CTX, 16, HD), BF16),
            dma((9,)),
            dma,
            dma,
            dma((2,)),
            dma((8,)),
            dma((HALVES, 4)),
            dma((HALVES,)),
            dma((2, 4)),
            dma((2,)),
            dma((2, 4)),
            dma((2,)),
            dma((8,)),
            dma((8,)),
            dma((9,)),
            dma((9,)),
            dma((8,)),
            dma((8,)),
            dma((8,)),
        ],
        compiler_params=pltpu.CompilerParams(
            collective_id=0, has_side_effects=True, vmem_limit_bytes=58 * 1024 * 1024
        ),
        cost_estimate=pl.CostEstimate(
            flops=12_000_000_000, bytes_accessed=30_000_000, transcendentals=600_000
        ),
    )(
        request_adapter_index,
        prefill_request_target,
        request_context_length,
        page_owner_index.reshape(1, 16),
        decode_hidden_states,
        prefill_hidden_states,
        query_matrix,
        key_matrix,
        value_matrix,
        adapter_down_maps,
        key_adapter_up_maps,
        value_adapter_up_maps,
        request_key_cache,
        request_value_cache,
    )
    page_shape = (SLOT_ROWS // BLK, BLK, HEADS * HD)
    page_keys, page_values, attended = pl.pallas_call(
        finish_kernel,
        out_shape=(
            jax.ShapeDtypeStruct((SLOT_ROWS, HEADS * HD), BF16),
            jax.ShapeDtypeStruct((SLOT_ROWS, HEADS * HD), BF16),
            jax.ShapeDtypeStruct((STEPS, RPG, HEADS * 8 * HD), BF16),
        ),
        in_specs=[hbm, hbm, vmem],
        out_specs=(hbm, hbm, vmem),
        scratch_shapes=[
            pltpu.VMEM((2, SLOT_ROWS, HEADS * HD), BF16),
            pltpu.VMEM((STEPS, RPG, HEADS * 8 * HD), F32),
            dma((2, 4)),
            dma((2, 4)),
        ],
        compiler_params=pltpu.CompilerParams(vmem_limit_bytes=58 * 1024 * 1024),
    )(page_keys, page_values, attended)
    return (page_keys.reshape(page_shape), page_values.reshape(page_shape), attended)


def solution(mesh):
    return jax.shard_map(
        on_device,
        mesh=mesh,
        in_specs=(
            P(("section", "ctx"), None),
            P(None, "section", "ctx"),
            P("ctx", "tp"),
            P("ctx", "tp"),
            P("ctx", "tp"),
            P("ctx", "tp"),
            P(None, "tp"),
            P(None, "tp"),
            P("section", "ctx", "tp"),
            P("section", "ctx", "tp"),
            P(),
            P(),
            P("section"),
            P(("section", "ctx"), None),
        ),
        out_specs=(
            P(("section", "ctx"), None, "tp"),
            P(("section", "ctx"), None, "tp"),
            P(None, "section", "tp"),
        ),
        check_vma=False,
    )
```

```python
import functools

import jax
import jax.numpy as jnp
from jax import lax
from jax.experimental import pallas as pl
from jax.experimental.pallas import tpu as pltpu
from jax.sharding import PartitionSpec as P

H = 64
KVH = 8
HD = 128
ADAPTER_RANK = 16
BLK = 32
STEPS = 2

ADAPTER_SCALE = 0.5
CUT = 128
NEG_FLOOR = -1e30
INV_ROOT = HD ** (-0.5)

SIDE = 4
N_CTX = 16
SHARD = 512
UNITS = 5
HALVES = 2 * UNITS
HALF = 256
BLOCKS = 8
HEADS = 4
ROWS = 512
SLOT_ROWS = 1024
FLAG_ROWS = 256
PAIR = 64
RPG = 4
CTX_DEV = 1024
QROWS = 64
DBLOCKS = 48
PER = 3

STEPS_AT = ((9, 0, 1), (12, 1, 3), (13, 3, 5), (17, 5, 7))
PLACES = (13, 15, 17, 19)
LANDS = (18, 19, 20, 21)
FAR = 7
PLACE_LAG = 2
LAND_LAG = 6
CACHE_AT = (15, 16, 18, 19)
ACROSS_AT = (9, 11, 12, 12)
FAR_AT = 18
LAST = 21

MESH = pl.DeviceIdType.MESH
F32 = jnp.float32
BF16 = jnp.bfloat16


def wait_bytes(ref, sem):
    pltpu.make_async_copy(ref, ref, sem).wait()


def turn(i, slots):
    here, which = False, -1
    for at in slots:
        here = here | (i == at)
        which = which + jnp.where(i >= at, 1, 0)
    return here, which


def nt_dot(a, b):
    return lax.dot_general(a, b, (((1,), (1,)), ((), ())), preferred_element_type=F32)


def layer_kernel(
    adapter_of,
    target_of,
    length_of,
    owner_of,
    xd,
    x_hbm,
    wq_hbm,
    wk_hbm,
    wv_hbm,
    wd_hbm,
    uk_hbm,
    uv_hbm,
    kc_hbm,
    vc_hbm,
    pk_out,
    pv_out,
    att_out,
    x_v,
    w_v,
    wq_v,
    wd_v,
    dt_v,
    hid,
    up_v,
    kc_v,
    vc_v,
    acc,
    accs,
    dn,
    row,
    raw,
    place_m,
    drow,
    drow_r,
    sendb,
    pages,
    flag_s,
    flag_r,
    live_v,
    part,
    rsr,
    ag,
    qp,
    tkv,
    pst,
    pgw,
    pgs,
    mgs,
    mgr,
    att,
    w_load,
    q_load,
    x_load,
    c_load,
    u_load,
    g_recv,
    g_send,
    x_recv,
    x_send,
    f_recv,
    f_send,
    row_send,
    row_recv,
    a_send,
    a_recv,
    small_send,
    small_recv,
    out_sem,
):
    s = lax.axis_index("section")
    c = lax.axis_index("ctx")
    t = lax.axis_index("tp")
    n_sec = lax.axis_size("section")
    y = c // SIDE
    z = lax.rem(c, SIDE)

    def chip(dy, dz):
        return lax.rem(y + dy + SIDE, SIDE) * SIDE + lax.rem(z + dz + SIDE, SIDE)

    def here(ctx):
        return (s, ctx, t)

    right = (lax.rem(s + 1, n_sec), c, t)
    left = (lax.rem(s + n_sec - 1, n_sec), c, t)
    partner = (s, c, 1 - t)
    s_left = lax.rem(s + n_sec - 1, n_sec)
    s_right = lax.rem(s + 1, n_sec)
    s_far = lax.rem(s + 2, n_sec)

    barrier = pltpu.get_barrier_semaphore()

    @pl.loop(1, N_CTX)
    def _(j):
        pl.semaphore_signal(
            barrier, inc=1, device_id=here(lax.rem(c + j, N_CTX)), device_id_type=MESH
        )

    for peer in (left, right, partner):
        pl.semaphore_signal(barrier, inc=1, device_id=peer, device_id_type=MESH)

    mine = pl.ds(pl.multiple_of(c * SHARD, SHARD), SHARD)
    shard_loads = []
    for n, hbm in enumerate([wk_hbm] * HEADS + [wv_hbm] * HEADS):
        cols = pl.ds(n % HEADS * HD, HD)
        shard_loads.append(
            pltpu.make_async_copy(hbm.at[:, cols], w_v.at[n, mine], w_load.at[n])
        )
    down_load = pltpu.make_async_copy(wd_hbm, wd_v, w_load.at[8])
    down_load.start()
    for load in shard_loads:
        load.start()
    q_copy = pltpu.make_async_copy(wq_hbm, wq_v, q_load)
    q_copy.start()
    ups = []
    for h in range(HEADS):
        cols = pl.ds(h * HD, HD)
        ups.append(pltpu.make_async_copy(uk_hbm.at[:, cols], up_v.at[h], u_load.at[h]))
        ups.append(pltpu.make_async_copy(uv_hbm.at[:, cols], up_v.at[4 + h], u_load.at[4 + h]))
    for load in ups:
        load.start()
    x_copy = pltpu.make_async_copy(x_hbm, x_v, x_load)
    x_copy.start()
    k_copy = pltpu.make_async_copy(kc_hbm, kc_v, c_load.at[0])
    v_copy = pltpu.make_async_copy(vc_hbm, vc_v, c_load.at[1])
    k_copy.start()
    v_copy.start()

    pl.semaphore_wait(barrier, N_CTX + 2)

    def send(src, dst, send_sem, recv_sem, device):
        pltpu.make_async_remote_copy(
            src_ref=src,
            dst_ref=dst,
            send_sem=send_sem,
            recv_sem=recv_sem,
            device_id=device,
            device_id_type=MESH,
        ).start()

    for load in shard_loads:
        load.wait()

    def block_of(h):
        key = (h - 2) // 4 * 2 + lax.rem(h, 2)
        return jnp.where(h < 2, HEADS + s, key)

    def half_of(h):
        return jnp.where(h < 2, h, lax.rem((h - 2) // 2, 2))

    def pass_on(h, stage, shard, first, count, ctx):
        start = shard * SHARD + half_of(h) * HALF + first
        piece = w_v.at[block_of(h), pl.ds(pl.multiple_of(start, 64), count)]
        send(piece, piece, g_send.at[h], g_recv.at[h, stage], here(ctx))

    def arrived(h, stage, shards):
        wait_bytes(w_v.at[block_of(h), pl.ds(0, shards * HALF)], g_recv.at[h, stage])

    yp, ym, zp, zm = chip(1, 0), chip(-1, 0), chip(0, 1), chip(0, -1)
    A, B, A0, A1, B0, B1, ZERO = (
        (0, 128),
        (128, 128),
        (64, 64),
        (0, 64),
        (128, 64),
        (192, 64),
        (64, 128),
    )

    def stage1(u):
        for ctx in (yp, zp, ym, zm):
            pass_on(u, 0, c, 0, HALF, ctx)

    def stage2(u):
        arrived(u, 0, 4)
        pass_on(u, 1, ym, *ZERO, yp)
        pass_on(u, 1, yp, *A1, ym)
        pass_on(u, 1, yp, *B1, ym)
        pass_on(u, 1, zm, *ZERO, zp)
        pass_on(u, 1, zp, *A1, zm)
        pass_on(u, 1, zp, *B1, zm)
        for shard in (ym, yp):
            for ctx in (zp, zm):
                pass_on(u, 1, shard, *A, ctx)
        for shard in (zm, zp):
            for ctx in (yp, ym):
                pass_on(u, 1, shard, *B, ctx)

    def stage3(u):
        arrived(u, 1, 6)
        yy, zz = chip(2, 0), chip(0, 2)
        for ctx in (zp, zm):
            pass_on(u, 2, yy, *A, ctx)
        for ctx in (yp, ym):
            pass_on(u, 2, zz, *B, ctx)
        for d in (-1, 1):
            pass_on(u, 2, chip(d, -1), *A0, zp)
            pass_on(u, 2, chip(d, 1), *A1, zm)
            pass_on(u, 2, chip(-1, d), *B0, yp)
            pass_on(u, 2, chip(1, d), *B1, ym)

    def stage4(u):
        arrived(u, 2, 4)
        pass_on(u, 3, chip(2, -1), *A0, zp)
        pass_on(u, 3, chip(2, 1), *A1, zm)
        pass_on(u, 3, chip(-1, 2), *B0, yp)
        pass_on(u, 3, chip(1, 2), *B1, ym)

    GROUPS = (
        (ym, yp, zm, zp),
        (chip(-1, -1), chip(-1, 1), chip(1, -1), chip(1, 1), chip(2, 0), chip(0, 2)),
        (chip(-1, 2), chip(1, 2), chip(2, -1), chip(2, 1)),
        (chip(2, 2),),
    )

    def across(group, half):
        for shard in GROUPS[group]:
            rows = pl.ds(pl.multiple_of(shard * SHARD + half * HALF, HALF), HALF)
            piece = w_v.at[HEADS + s, rows]
            send(piece, piece, x_send.at[0], x_recv.at[0, group], right)
            send(piece, piece, x_send.at[1], x_recv.at[1, group], left)

    def across_again(group):
        count = len(GROUPS[group])
        wait_bytes(w_v.at[HEADS + s_left, pl.ds(0, count * SHARD)], x_recv.at[0, group])
        wait_bytes(w_v.at[HEADS + s_right, pl.ds(0, count * SHARD)], x_recv.at[1, group])
        for shard in GROUPS[group]:
            rows = pl.ds(pl.multiple_of(shard * SHARD, SHARD), CUT)
            piece = w_v.at[HEADS + s_left, rows]
            send(piece, piece, f_send.at[0], f_recv.at[0, group], right)
            rows = pl.ds(pl.multiple_of(shard * SHARD + CUT, 128), SHARD - CUT)
            piece = w_v.at[HEADS + s_right, rows]
            send(piece, piece, f_send.at[1], f_recv.at[1, group], left)

    span_request = target_of[s]
    span_adapter = jnp.int32(0)
    for b in range(N_CTX):
        span_adapter = jnp.where(span_request == b, adapter_of[b], span_adapter)
    pick_row = lax.broadcasted_iota(jnp.int32, (ADAPTER_RANK, HD), 0)
    pick_col = lax.broadcasted_iota(jnp.int32, (ADAPTER_RANK, HD), 1)
    pick = jnp.where(pick_col == span_adapter * ADAPTER_RANK + pick_row, 1.0, 0.0).astype(BF16)

    def down_rows():
        down_load.wait()
        own = pl.ds(pl.multiple_of(c * SHARD, SHARD), SHARD)
        dt_v[:, own] = nt_dot(pick, wd_v[...]).astype(BF16)

        @pl.loop(1, N_CTX)
        def _(j):
            piece = dt_v.at[:, own]
            ctx = lax.rem(c + j, N_CTX)
            send(piece, piece, small_send.at[7], small_recv.at[7], here(ctx))

    def project_down():
        x_copy.wait()
        for load in ups:
            load.wait()
        wait_bytes(dt_v.at[:, pl.ds(0, (N_CTX - 1) * SHARD)], small_recv.at[7])
        acc[...] = jnp.zeros_like(acc)

        @pl.loop(0, 8)
        def _(i):
            part_k = pl.ds(pl.multiple_of(i * 1024, 1024), 1024)
            acc[:, 0:ADAPTER_RANK] += nt_dot(x_v[:, part_k], dt_v[:, part_k])

        down = acc[:, 0:ADAPTER_RANK].astype(BF16)
        dn[t] = jnp.dot(down, pick, preferred_element_type=F32).astype(BF16)
        send(dn.at[t], dn.at[t], small_send.at[1], small_recv.at[1], partner)

    def add(blocks, hidden_parts, rounds):
        @pl.loop(0, rounds)
        def _(i):
            parts = hidden_parts(i)
            hidden = jnp.concatenate([x_v[:, part] for part in parts], axis=1)
            weight = jnp.concatenate(
                [jnp.concatenate([w_v[n, part] for n in blocks], axis=1) for part in parts],
                axis=0,
            )
            product = jnp.dot(hidden, weight, preferred_element_type=F32)
            for j, n in enumerate(blocks):
                accs[n] += product[:, j * HD : (j + 1) * HD]

    def whole(i):
        return [pl.ds(pl.multiple_of(i * 2048, 2048), 2048)]

    def half_rows(half):
        def parts(i):
            return [
                pl.ds(pl.multiple_of((i * 8 + j) * SHARD + half * HALF, HALF), HALF)
                for j in range(8)
            ]

        return parts

    def wait_far():
        n = HEADS + s_far
        for group in range(4):
            count = len(GROUPS[group])
            wait_bytes(w_v.at[n, pl.ds(0, count * CUT)], f_recv.at[0, group])
            wait_bytes(w_v.at[n, pl.ds(0, count * (SHARD - CUT))], f_recv.at[1, group])

    def nth(p, sec):
        ahead = jnp.where(p == 0, 0, jnp.where(p == 1, n_sec - 1, jnp.where(p == 2, 1, 2)))
        is_key = (p >= 3) & (p < 3 + HEADS)
        return jnp.where(is_key, p - 3, HEADS + lax.rem(sec + ahead, n_sec))

    def project(p):
        n = nth(p, s)

        if p == 0:
            wait_bytes(dn.at[0], small_recv.at[1])

        delta = jnp.dot(dn[n // HEADS], up_v[n], preferred_element_type=F32)
        row[p] = (accs[n] + ADAPTER_SCALE * delta).astype(BF16)

    def ship(first, end):
        some = pl.ds(first, end - first)
        send(row.at[some], raw.at[some], row_send.at[first], row_recv.at[first], right)

    def exchange(first, end):
        some = pl.ds(first, end - first)
        ours = pl.ds(pl.multiple_of(c * PAIR, PAIR), PAIR)

        @pl.loop(1, N_CTX)
        def _(j):
            ctx = lax.rem(c + j, N_CTX)
            theirs = pl.ds(pl.multiple_of(ctx * PAIR, PAIR), PAIR)
            send(
                sendb.at[some, theirs],
                pages.at[some, ours],
                a_send.at[first],
                a_recv.at[first],
                here(ctx),
            )

        for p in range(first, end):
            pages[p, ours] = sendb[p, ours]

    def place(first, end):
        wait_bytes(raw.at[pl.ds(first, end - first)], row_recv.at[first])

        @pl.loop(0, 4)
        def _(i):
            some = pl.ds(pl.multiple_of(i * 256, 256), 256)
            rows = jnp.concatenate([raw[p] for p in range(first, end)], axis=1)
            placed = jnp.dot(place_m[some], rows, preferred_element_type=F32).astype(BF16)
            for j in range(end - first):
                sendb[first + j, some] = placed[:, j * HD : (j + 1) * HD]

        exchange(first, end)

    def page_rows():
        first = lax.broadcasted_iota(jnp.int32, (16, 16), 0)
        second = lax.broadcasted_iota(jnp.int32, (16, 16), 1)
        across_ids = jnp.broadcast_to(owner_of[...].astype(F32), (16, 16))
        ids = jnp.sum(jnp.where(first == second, across_ids, 0.0), axis=1, keepdims=True)
        before = (ids == across_ids) & (second < first)
        rank = jnp.sum(jnp.where(before, 1.0, 0.0), axis=1, keepdims=True)
        slot_row = (ids * 2 + rank) * BLK
        page = lax.broadcasted_iota(jnp.int32, (16, ROWS), 0)
        lane = lax.broadcasted_iota(jnp.int32, (16, ROWS), 1)
        token = lax.rem(lane, BLK).astype(F32)
        rows = jnp.sum(
            jnp.where(lane // BLK == page, slot_row + token, 0.0), axis=0, keepdims=True
        )
        drow[...] = jnp.broadcast_to(rows, (8, ROWS)).astype(jnp.int32)
        send(drow, drow_r, small_send.at[0], small_recv.at[0], right)

    def page_flags():
        wait_bytes(drow_r, small_recv.at[0])

        @pl.loop(0, 4)
        def _(i):
            some = pl.ds(pl.multiple_of(i * 256, 256), 256)
            slot_row = lax.broadcasted_iota(jnp.int32, (256, ROWS), 0) + i * 256
            hit = slot_row == drow_r[0:1]
            place_m[some] = jnp.where(hit, 1.0, 0.0).astype(BF16)

        slot = lax.broadcasted_iota(jnp.int32, (FLAG_ROWS, ROWS), 0) // 8
        taken = jnp.where(drow_r[0:1] == slot * BLK, 1.0, 0.0)
        flag = jnp.max(taken, axis=1, keepdims=True)
        flag_s[...] = jnp.broadcast_to(flag, (FLAG_ROWS, HD)).astype(BF16)
        ours = pl.ds(pl.multiple_of(c * 16, 16), 16)

        @pl.loop(1, N_CTX)
        def _(j):
            ctx = lax.rem(c + j, N_CTX)
            theirs = pl.ds(pl.multiple_of(ctx * 16, 16), 16)
            send(flag_s.at[theirs], flag_r.at[ours], a_send.at[8], a_recv.at[8], here(ctx))

        flag_r[ours] = flag_s[ours]

    def page_live():
        wait_bytes(flag_r.at[pl.ds(0, FLAG_ROWS - 16)], a_recv.at[8])
        flags = nt_dot(jnp.ones((16, HD), BF16), flag_r[...]).astype(BF16)
        at = lax.broadcasted_iota(jnp.int32, (FLAG_ROWS, SLOT_ROWS), 0)
        to = lax.broadcasted_iota(jnp.int32, (FLAG_ROWS, SLOT_ROWS), 1)
        spread = jnp.where((lax.rem(at, 8) == 0) & (at // 8 == to // BLK), 1.0, 0.0)
        live_v[...] = jnp.dot(flags, spread.astype(BF16), preferred_element_type=F32)

    def landed(first, end):
        some = pl.ds(first, end - first)
        wait_bytes(pages.at[some, pl.ds(0, SLOT_ROWS - PAIR)], a_recv.at[first])

    def write_out(p):
        n = nth(p, s_left)
        cols = pl.ds(pl.multiple_of(lax.rem(n, HEADS) * HD, HD), HD)

        @pl.when(n < HEADS)
        def _():
            pltpu.make_async_copy(pages.at[p], pk_out.at[:, cols], out_sem.at[p]).start()

        @pl.when(n >= HEADS)
        def _():
            pltpu.make_async_copy(pages.at[p], pv_out.at[:, cols], out_sem.at[p]).start()

    def decode_project():
        q_copy.wait()

        def blocks(product, first):
            for i in range(product.shape[1] // HD):
                part[first + i] = product[:, i * HD : (i + 1) * HD]

        hid[0:4] = xd[0].astype(F32)
        hid[4:8] = xd[1].astype(F32)
        hidden = hid[...].astype(BF16)
        part[DBLOCKS - 6 :] = jnp.zeros((6, 8, HD), F32)
        for i in range(8):
            piece = wq_v[:, i * 512 : (i + 1) * 512]
            blocks(jnp.dot(hidden, piece, preferred_element_type=F32), 4 * i)
        for n in range(BLOCKS):
            blocks(jnp.dot(hidden, w_v[n, mine], preferred_element_type=F32), 32 + n)
        part[40 + t] = jnp.dot(hidden, wd_v[...], preferred_element_type=F32)
        send(part.at[40 + t], part.at[40 + t], small_send.at[2], small_recv.at[2], partner)

    def decode_spread():
        wait_bytes(part.at[0], small_recv.at[2])

        @pl.loop(1, N_CTX)
        def _(j):
            ctx = lax.rem(c + j, N_CTX)
            send(
                part.at[pl.ds(ctx * PER, PER)],
                rsr.at[c],
                small_send.at[3],
                small_recv.at[3],
                here(ctx),
            )

        rsr[c] = part[pl.ds(c * PER, PER)]

    def decode_sum():
        wait_bytes(rsr.at[pl.ds(0, N_CTX - 1)], small_recv.at[3])
        ag[pl.ds(c * PER, PER)] = jnp.sum(rsr[...], axis=0)

        @pl.loop(1, N_CTX)
        def _(j):
            ctx = lax.rem(c + j, N_CTX)
            piece = ag.at[pl.ds(c * PER, PER)]
            send(piece, piece, small_send.at[4], small_recv.at[4], here(ctx))

    def decode_rows():
        wait_bytes(ag.at[pl.ds(0, (N_CTX - 1) * PER)], small_recv.at[4])
        to = lax.broadcasted_iota(jnp.int32, (QROWS, QROWS), 0)
        at = lax.broadcasted_iota(jnp.int32, (QROWS, QROWS), 1)
        source = lax.rem(to, 8) * 8 + lax.rem(to // 8, STEPS) * RPG + to // 16
        perm = jnp.where(at == source, 1.0, 0.0).astype(BF16)
        for k in range(HEADS):
            queries = ag[8 * k : 8 * k + 8].reshape(QROWS, HD).astype(BF16)
            qp[k] = jnp.dot(perm, queries, preferred_element_type=F32).astype(BF16)
        lane = lax.broadcasted_iota(jnp.int32, (8, HD), 1) // ADAPTER_RANK
        who = lax.rem(lax.broadcasted_iota(jnp.int32, (8, HD), 0), RPG)
        adapter = jnp.zeros((8, HD), jnp.int32)
        for b in range(RPG):
            adapter = jnp.where(who == b, adapter_of[s * RPG + b], adapter)
        for kind in range(2):
            down = ag[40 + kind].astype(BF16).astype(F32)
            picked = jnp.where(lane == adapter, down, 0.0).astype(BF16)
            for k in range(HEADS):
                n = 4 * kind + k
                delta = jnp.dot(picked, up_v[n], preferred_element_type=F32)
                tkv[n] = (ag[32 + n] + ADAPTER_SCALE * delta).astype(BF16).astype(F32)
        which = lax.broadcasted_iota(jnp.int32, (QROWS, 8), 0)
        other = lax.broadcasted_iota(jnp.int32, (QROWS, 8), 1)
        tok_live = (
            (lax.rem(other, RPG) == which // 16)
            & (other // RPG <= lax.rem(which // 8, STEPS))
            & (c == 0)
        )
        for k in range(HEADS):
            tok = nt_dot(qp[k], tkv[k].astype(BF16)) * INV_ROOT
            tok_max = jnp.max(jnp.where(tok_live, tok, NEG_FLOOR), axis=1, keepdims=True)
            tok_w = jnp.where(tok_live, jnp.exp(tok - tok_max), 0.0)
            tok_out = jnp.zeros((QROWS, HD), F32)
            for i in range(8):
                tok_out = tok_out + tok_w[:, i : i + 1] * tkv[4 + k, i : i + 1]
            pst[0, k] = jnp.broadcast_to(tok_max, (QROWS, HD))
            pst[1, k] = jnp.broadcast_to(jnp.sum(tok_w, axis=1, keepdims=True), (QROWS, HD))
            pst[2, k] = tok_out

    def merge(k, rows, block_max, total, out):
        old = pst[0, k, rows]
        top = jnp.maximum(old, block_max)
        old_scale, scale = jnp.exp(old - top), jnp.exp(block_max - top)
        pst[0, k, rows] = top
        pst[1, k, rows] = old_scale * pst[1, k, rows] + scale * total
        pst[2, k, rows] = old_scale * pst[2, k, rows] + scale * out

    def cache_block(b):
        @pl.when(b == 0)
        def _():
            k_copy.wait()
            v_copy.wait()

        left_len = length_of[b] - c * CTX_DEV
        live = lax.broadcasted_iota(jnp.int32, (16, CTX_DEV), 1) < left_len
        rows = pl.ds(pl.multiple_of(b * 16, 16), 16)
        for k in range(HEADS):
            cols = slice(k * HD, (k + 1) * HD)
            scores = nt_dot(qp[k, rows], kc_v[b, :, cols]) * INV_ROOT
            block_max = jnp.max(jnp.where(live, scores, NEG_FLOOR), axis=1, keepdims=True)
            weights = jnp.where(live, jnp.exp(scores - block_max), 0.0).astype(BF16)
            total = jnp.sum(weights.astype(F32), axis=1, keepdims=True)
            out = jnp.dot(weights, vc_v[b, :, cols], preferred_element_type=F32)
            merge(k, rows, block_max, total, out)

    page_request = target_of[s_left] - s * RPG

    def page_scores(p):
        k = nth(p, s_left)
        live = live_v[...] > 0.5
        query = jnp.zeros((16, HD), F32)
        for b in range(RPG):
            query = jnp.where(page_request == b, qp[k, b * 16 : b * 16 + 16].astype(F32), query)
        scores = nt_dot(query.astype(BF16), pages[p]) * INV_ROOT
        p_max = jnp.max(jnp.where(live, scores, NEG_FLOOR), axis=1, keepdims=True)
        weights = jnp.where(live, jnp.exp(scores - p_max), 0.0).astype(BF16)
        p_total = jnp.sum(weights.astype(F32), axis=1, keepdims=True)
        pgw[k] = weights
        pgs[0, k] = jnp.broadcast_to(p_max, (16, HD))
        pgs[1, k] = jnp.broadcast_to(p_total, (16, HD))

    def page_merge(p):
        k = nth(p, s_left) - HEADS
        p_out = jnp.dot(pgw[k], pages[p], preferred_element_type=F32)
        lane = lax.broadcasted_iota(jnp.int32, (16, HD), 1)
        for b in range(RPG):
            rows = slice(b * 16, b * 16 + 16)
            wanted = page_request == b
            merge(
                k,
                rows,
                jnp.where(wanted, pgs[0, k], NEG_FLOOR),
                jnp.where(wanted, pgs[1, k], 0.0),
                jnp.where(wanted, p_out, 0.0),
            )
            mgs[k * RPG + b, 0] = pst[2, k, rows]
            mgs[k * RPG + b, 1] = jnp.where(lane < 64, pst[0, k, rows], pst[1, k, rows])
            ctx = k * RPG + b

            @pl.when(ctx != c)
            def _():
                send(mgs.at[ctx], mgr.at[c], small_send.at[5], small_recv.at[5], here(ctx))

    stage1(0)
    stage1(1)
    down_rows()
    page_rows()
    accs[...] = jnp.zeros_like(accs)

    @pl.loop(2, LAST + 1)
    def _(i):
        @pl.when((i >= 6) & (i < HALVES + 6))
        def _():
            stage4(i - 6)

        @pl.when((i >= 4) & (i < HALVES + 4))
        def _():
            stage3(i - 4)

        @pl.when((i >= 2) & (i < HALVES + 2))
        def _():
            stage2(i - 2)

        @pl.when(i < HALVES)
        def _():
            stage1(i)

        @pl.when((i >= 8) & (i < HALVES + 8))
        def _():
            arrived(i - 8, 3, 1)

        for group in range(4):

            @pl.when((i == 2 + 2 * group) | (i == 3 + 2 * group))
            def _(group=group):
                across(group, lax.rem(i, 2))

        for group, at in enumerate(ACROSS_AT):

            @pl.when(i == at)
            def _(group=group):
                across_again(group)

        @pl.when(i == 4)
        def _():
            decode_project()

        @pl.when(i == 5)
        def _():
            decode_spread()

        @pl.when(i == 6)
        def _():
            page_flags()

        @pl.when(i == 7)
        def _():
            decode_sum()

        @pl.when(i == 8)
        def _():
            project_down()

        @pl.when(i == 9)
        def _():
            add((HEADS + s,), whole, 4)

        @pl.when(i == 12)
        def _():
            add((HEADS + s_left, HEADS + s_right), whole, 4)

        for at in (11, 13, 15, 17):

            @pl.when(i == at)
            def _(at=at):
                key = (at - 11) // 4 * 2
                add((key, key + 1), half_rows((at - 11) // 2 % 2), 2)

        for at, first, end in STEPS_AT:

            @pl.when(i == at)
            def _(first=first, end=end):
                for p in range(first, end):
                    project(p)
                ship(first, end)

        @pl.when(i == 9)
        def _():
            decode_rows()

        for (_, first, end), at in zip(STEPS_AT, PLACES):

            @pl.when(i == at)
            def _(first=first, end=end):
                place(first, end)

        @pl.when(i == 18)
        def _():
            page_live()

        @pl.when(i == FAR_AT)
        def _():
            wait_far()
            add((HEADS + s_far,), whole, 4)
            project(FAR)
            ship(FAR, FAR + 1)

        now, b = turn(i, CACHE_AT)

        @pl.when(now)
        def _():
            cache_block(b)

        @pl.when(i == 20)
        def _():
            place(FAR, FAR + 1)

        for (_, first, end), at in zip(STEPS_AT, LANDS):

            @pl.when(i == at)
            def _(first=first, end=end):
                landed(first, end)
                for p in range(first, end):
                    write_out(p)
                    if 3 <= p < 7:
                        page_scores(p)

    for early in (0, 1, 2):
        page_merge(early)
    landed(FAR, FAR + 1)
    page_merge(FAR)
    write_out(FAR)

    mgr[c] = mgs[c]
    wait_bytes(mgr.at[pl.ds(0, N_CTX - 1)], small_recv.at[5])
    stats = mgr[:, 1]
    tops, totals = stats[:, :, 0:1], stats[:, :, 64:65]
    scale = jnp.exp(tops - jnp.max(tops, axis=0, keepdims=True))
    numer = jnp.sum(scale * mgr[:, 0], axis=0)
    denom = jnp.sum(scale * totals, axis=0)
    att[c] = (numer / denom).astype(BF16)

    @pl.loop(1, N_CTX)
    def _(j):
        ctx = lax.rem(c + j, N_CTX)
        send(att.at[c], att.at[c], small_send.at[6], small_recv.at[6], here(ctx))

    wait_bytes(att.at[pl.ds(0, N_CTX - 1)], small_recv.at[6])
    att_out[...] = att[...]

    @pl.loop(0, HALVES)
    def _(h):
        wait_bytes(w_v.at[0, pl.ds(0, 15 * HALF)], g_send.at[h])

    for first, end in ((0, 1), (1, 3), (3, 5), (5, 7), (7, 8)):
        some = pl.ds(first, end - first)
        wait_bytes(sendb.at[some, pl.ds(0, SLOT_ROWS - PAIR)], a_send.at[first])
        wait_bytes(row.at[some], row_send.at[first])

    wait_bytes(flag_s.at[pl.ds(0, FLAG_ROWS - 16)], a_send.at[8])

    for d, count in ((0, CUT), (1, SHARD - CUT)):
        wait_bytes(w_v.at[0, pl.ds(0, 15 * SHARD)], x_send.at[d])
        wait_bytes(w_v.at[0, pl.ds(0, 15 * count)], f_send.at[d])

    @pl.loop(0, 2 * HEADS)
    def _(n):
        wait_bytes(pages.at[n], out_sem.at[n])

    wait_bytes(drow, small_send.at[0])
    wait_bytes(dn.at[0], small_send.at[1])
    wait_bytes(part.at[0], small_send.at[2])
    wait_bytes(rsr.at[pl.ds(0, N_CTX - 1)], small_send.at[3])
    wait_bytes(ag.at[pl.ds(0, (N_CTX - 1) * PER)], small_send.at[4])
    wait_bytes(mgr.at[pl.ds(0, N_CTX - 1)], small_send.at[5])
    wait_bytes(att.at[pl.ds(0, N_CTX - 1)], small_send.at[6])
    wait_bytes(dt_v.at[:, pl.ds(0, (N_CTX - 1) * SHARD)], small_send.at[7])


def finish_kernel(pk, pv, att, pk_out, pv_out, att_out, held, rows, in_sem, out_sem):
    parts = [(j, i) for i in range(4) for j in range(2)]

    def moves(j, i):
        some = pl.ds(i * (SLOT_ROWS // 4), SLOT_ROWS // 4)
        source, result = (pk, pv)[j], (pk_out, pv_out)[j]
        return (
            pltpu.make_async_copy(source.at[some], held.at[j, some], in_sem.at[j, i]),
            pltpu.make_async_copy(held.at[j, some], result.at[some], out_sem.at[j, i]),
        )

    copies = [moves(j, i) for j, i in parts]
    for into, _ in copies:
        into.start()
    for k in range(HEADS):
        for b in range(RPG):
            block = att[k * RPG + b].astype(F32)
            for step in range(STEPS):
                for g in range(8):
                    cols = slice((k * 8 + g) * HD, (k * 8 + g + 1) * HD)
                    at = step * 8 + g
                    rows[step, b : b + 1, cols] = block[at : at + 1]
    att_out[...] = rows[...].astype(BF16)
    for into, out in copies:
        into.wait()
        out.start()
    for _, out in copies:
        out.wait()


def on_device(
    prefill_hidden_states,
    decode_hidden_states,
    query_matrix,
    key_matrix,
    value_matrix,
    adapter_down_maps,
    key_adapter_up_maps,
    value_adapter_up_maps,
    request_key_cache,
    request_value_cache,
    request_adapter_index,
    prefill_request_target,
    request_context_length,
    page_owner_index,
):
    hbm = pl.BlockSpec(memory_space=pl.ANY)
    vmem = pl.BlockSpec(memory_space=pltpu.VMEM)
    smem = pl.BlockSpec(memory_space=pltpu.SMEM)
    dma = pltpu.SemaphoreType.DMA
    page_keys, page_values, attended = pl.pallas_call(
        layer_kernel,
        out_shape=(
            jax.ShapeDtypeStruct((SLOT_ROWS, HEADS * HD), BF16),
            jax.ShapeDtypeStruct((SLOT_ROWS, HEADS * HD), BF16),
            jax.ShapeDtypeStruct((N_CTX, 16, HD), BF16),
        ),
        in_specs=[smem] * 3 + [vmem] * 2 + [hbm] * 9,
        out_specs=(hbm, hbm, vmem),
        scratch_shapes=[
            pltpu.VMEM((ROWS, 8192), BF16),
            pltpu.VMEM((BLOCKS, 8192, HD), BF16),
            pltpu.VMEM((SHARD, 4096), BF16),
            pltpu.VMEM((SHARD, HD), BF16),
            pltpu.VMEM((ADAPTER_RANK, 8192), BF16),
            pltpu.VMEM((8, SHARD), F32),
            pltpu.VMEM((8, HD, HD), BF16),
            pltpu.VMEM((RPG, CTX_DEV, HEADS * HD), BF16),
            pltpu.VMEM((RPG, CTX_DEV, HEADS * HD), BF16),
            pltpu.VMEM((ROWS, HD), F32),
            pltpu.VMEM((BLOCKS, ROWS, HD), F32),
            pltpu.VMEM((2, ROWS, HD), BF16),
            pltpu.VMEM((8, ROWS, HD), BF16),
            pltpu.VMEM((8, ROWS, HD), BF16),
            pltpu.VMEM((SLOT_ROWS, ROWS), BF16),
            pltpu.VMEM((8, ROWS), jnp.int32),
            pltpu.VMEM((8, ROWS), jnp.int32),
            pltpu.VMEM((BLOCKS, SLOT_ROWS, HD), BF16),
            pltpu.VMEM((BLOCKS, SLOT_ROWS, HD), BF16),
            pltpu.VMEM((FLAG_ROWS, HD), BF16),
            pltpu.VMEM((FLAG_ROWS, HD), BF16),
            pltpu.VMEM((16, SLOT_ROWS), F32),
            pltpu.VMEM((DBLOCKS, 8, HD), F32),
            pltpu.VMEM((N_CTX, PER, 8, HD), F32),
            pltpu.VMEM((DBLOCKS, 8, HD), F32),
            pltpu.VMEM((HEADS, QROWS, HD), BF16),
            pltpu.VMEM((8, 8, HD), F32),
            pltpu.VMEM((3, HEADS, QROWS, HD), F32),
            pltpu.VMEM((HEADS, 16, SLOT_ROWS), BF16),
            pltpu.VMEM((2, HEADS, 16, HD), F32),
            pltpu.VMEM((N_CTX, 2, 16, HD), F32),
            pltpu.VMEM((N_CTX, 2, 16, HD), F32),
            pltpu.VMEM((N_CTX, 16, HD), BF16),
            dma((9,)),
            dma,
            dma,
            dma((2,)),
            dma((8,)),
            dma((HALVES, 4)),
            dma((HALVES,)),
            dma((2, 4)),
            dma((2,)),
            dma((2, 4)),
            dma((2,)),
            dma((8,)),
            dma((8,)),
            dma((9,)),
            dma((9,)),
            dma((8,)),
            dma((8,)),
            dma((8,)),
        ],
        compiler_params=pltpu.CompilerParams(
            collective_id=0, has_side_effects=True, vmem_limit_bytes=58 * 1024 * 1024
        ),
        cost_estimate=pl.CostEstimate(
            flops=12_000_000_000, bytes_accessed=30_000_000, transcendentals=600_000
        ),
    )(
        request_adapter_index,
        prefill_request_target,
        request_context_length,
        page_owner_index.reshape(1, 16),
        decode_hidden_states,
        prefill_hidden_states,
        query_matrix,
        key_matrix,
        value_matrix,
        adapter_down_maps,
        key_adapter_up_maps,
        value_adapter_up_maps,
        request_key_cache,
        request_value_cache,
    )
    page_shape = (SLOT_ROWS // BLK, BLK, HEADS * HD)
    page_keys, page_values, attended = pl.pallas_call(
        finish_kernel,
        out_shape=(
            jax.ShapeDtypeStruct((SLOT_ROWS, HEADS * HD), BF16),
            jax.ShapeDtypeStruct((SLOT_ROWS, HEADS * HD), BF16),
            jax.ShapeDtypeStruct((STEPS, RPG, HEADS * 8 * HD), BF16),
        ),
        in_specs=[hbm, hbm, vmem],
        out_specs=(hbm, hbm, vmem),
        scratch_shapes=[
            pltpu.VMEM((2, SLOT_ROWS, HEADS * HD), BF16),
            pltpu.VMEM((STEPS, RPG, HEADS * 8 * HD), F32),
            dma((2, 4)),
            dma((2, 4)),
        ],
        compiler_params=pltpu.CompilerParams(vmem_limit_bytes=58 * 1024 * 1024),
    )(page_keys, page_values, attended)
    return (page_keys.reshape(page_shape), page_values.reshape(page_shape), attended)


def solution(mesh):
    return jax.shard_map(
        on_device,
        mesh=mesh,
        in_specs=(
            P(("section", "ctx"), None),
            P(None, "section", "ctx"),
            P("ctx", "tp"),
            P("ctx", "tp"),
            P("ctx", "tp"),
            P("ctx", "tp"),
            P(None, "tp"),
            P(None, "tp"),
            P("section", "ctx", "tp"),
            P("section", "ctx", "tp"),
            P(),
            P(),
            P("section"),
            P(("section", "ctx"), None),
        ),
        out_specs=(
            P(("section", "ctx"), None, "tp"),
            P(("section", "ctx"), None, "tp"),
            P(None, "section", "tp"),
        ),
        check_vma=False,
    )
```
